128 devices in a mesh: ctx: 8 (over z_hi, x), fsdp: 16 (over y, z_lo, core).
Axes of the slice: x: 4, y: 4, z: 4 (z_hi: 2, z_lo: 2; z = z_hi * 2 + z_lo), core: 2. Of those that a mesh axis runs over, the one named last changes fastest.
Arguments:
- layer_input: bfloat16 [16, 1024, 2048], P('fsdp', 'ctx'), may hold values from -6 to 6
- cotangent: bfloat16 [16, 1024, 2048], P('fsdp', 'ctx'), may hold values from -6 to 6
- query_weight: bfloat16 [2048, 2048], P('fsdp'), may hold values from -0.125 to 0.125
- key_weight: bfloat16 [2048, 2048], P('fsdp'), may hold values from -0.125 to 0.125
- value_weight: bfloat16 [2048, 2048], P('fsdp'), may hold values from -0.125 to 0.125
- out_weight: bfloat16 [2048, 2048], P('fsdp'), may hold values from -0.125 to 0.125
- gate_weight: bfloat16 [2048, 5632], P('fsdp'), may hold values from -0.125 to 0.125
- up_weight: bfloat16 [2048, 5632], P('fsdp'), may hold values from -0.125 to 0.125
- down_weight: bfloat16 [5632, 2048], P('fsdp'), may hold values from -0.078125 to 0.078125
- query_gain: bfloat16 [2048], P('fsdp'), may hold values from 0.5 to 1.5
- key_gain: bfloat16 [2048], P('fsdp'), may hold values from 0.5 to 1.5
- attention_gain: bfloat16 [2048], P('fsdp'), may hold values from 0.5 to 1.5
- feed_gain: bfloat16 [2048], P('fsdp'), may hold values from 0.5 to 1.5
- pair_table: int32 [8, 2], replicated, may hold values from 0 to 15, as said below
Outputs:
- result: bfloat16 [16, 1024, 2048], P('fsdp', 'ctx')
- input_grad: float32 [16, 1024, 2048], P('fsdp', 'ctx')
- query_weight_grad: float32 [2048, 2048], P('fsdp')
- key_weight_grad: float32 [2048, 2048], P('fsdp')
- value_weight_grad: float32 [2048, 2048], P('fsdp')
- out_weight_grad: float32 [2048, 2048], P('fsdp')
- gate_weight_grad: float32 [2048, 5632], P('fsdp')
- up_weight_grad: float32 [2048, 5632], P('fsdp')
- down_weight_grad: float32 [5632, 2048], P('fsdp')
- query_gain_grad: float32 [2048], P('fsdp')
- key_gain_grad: float32 [2048], P('fsdp')
- attention_gain_grad: float32 [2048], P('fsdp')
- feed_gain_grad: float32 [2048], P('fsdp')
The draws below stay inside these ranges and needn't reach their ends.
Inputs may be any that keep to these rules, and one draw needn't show every extreme that they name: `pair_table`: row r holds a block p and then block 2 n - 1 - p, n the rows of the table; the values p of the rows are a permutation of 0 to n - 1.
All inputs are finite; a program needn't handle non-finite values.
Results may differ from the reference program's by a relative error of at most 0.028.
Values may be sent and summed in bfloat16 or wider, within the bound.
A program may use at most 896 MiB of HBM per device.

```python
import math
import jax
import jax.numpy as jnp
from jax import lax

D = 2048
H = 32
HD = 64
FF = 5632
SEQ_LEN = 1024
SEQS = 16
N_CTX = 8


def draw_pair_table(key, part):
    key = jax.random.fold_in(key, 7)
    order = jax.random.permutation(key, N_CTX).astype(jnp.int32)
    return jnp.stack([order, 2 * N_CTX - 1 - order], axis=1)


def shard_levels(key, shape, shards, low, top_value):
    def one(dim, shards_of):
        draws = jax.random.uniform(jax.random.fold_in(jax.random.fold_in(key, 6), dim), (shards_of,), jnp.float32, low / len(shards), top_value / len(shards))
        return jnp.repeat(jnp.exp(draws), shape[dim] // shards_of).reshape((-1,) + (1,) * (len(shape) - dim - 1))

    loudness = one(*shards[0])
    for cut in shards[1:]:
        loudness = loudness * one(*cut)
    return loudness


def centred(stream_key, shape, scale, limit, shards=(), kind=jnp.bfloat16):
    drawn = jax.random.normal(stream_key, shape, jnp.float32) * scale
    if len(shards) > 0:
        drawn = shard_levels(stream_key, shape, shards, -0.22, 0.18) * drawn
    return jnp.clip(drawn, min=-limit, max=limit).astype(kind)


def setup_inputs(seed: int = 0) -> dict:
    splits = jax.random.split(jax.random.key(seed), 15)
    layer_input = centred(splits[0], (SEQS, SEQ_LEN, D), 1.0, 6.0, ((0, 16), (1, 8)))
    cotangent = centred(splits[1], (SEQS, SEQ_LEN, D), 1.0, 6.0, ((0, 16), (1, 8)))
    query_weight = centred(splits[2], (D, D), D ** -0.5, 0.125, ((0, 16),))
    key_weight = centred(splits[3], (D, D), D ** -0.5, 0.125, ((0, 16),))
    value_weight = centred(splits[4], (D, D), D ** -0.5, 0.125, ((0, 16),))
    out_weight = centred(splits[5], (D, D), D ** -0.5, 0.125, ((0, 16),))
    gate_weight = centred(splits[6], (D, FF), D ** -0.5, 0.125, ((0, 16),))
    up_weight = centred(splits[7], (D, FF), D ** -0.5, 0.125, ((0, 16),))
    down_weight = centred(splits[8], (FF, D), FF ** -0.5, 0.078125, ((0, 16),))
    query_gain = jnp.clip(0.5 + 1.0 * jax.random.uniform(splits[9], (D,), jnp.float32) ** shard_levels(splits[9], (D,), ((0, 16),), -0.2, 0.2), 0.5, 1.5).astype(jnp.bfloat16)
    key_gain = jnp.clip(0.5 + 1.0 * jax.random.uniform(splits[10], (D,), jnp.float32) ** shard_levels(splits[10], (D,), ((0, 16),), -0.2, 0.2), 0.5, 1.5).astype(jnp.bfloat16)
    attention_gain = jnp.clip(0.5 + 1.0 * jax.random.uniform(splits[11], (D,), jnp.float32) ** shard_levels(splits[11], (D,), ((0, 16),), -0.2, 0.2), 0.5, 1.5).astype(jnp.bfloat16)
    feed_gain = jnp.clip(0.5 + 1.0 * jax.random.uniform(splits[12], (D,), jnp.float32) ** shard_levels(splits[12], (D,), ((0, 16),), -0.2, 0.2), 0.5, 1.5).astype(jnp.bfloat16)
    pair_table = draw_pair_table(jax.random.fold_in(splits[14], 71), 0)
    return {"layer_input": layer_input, "cotangent": cotangent, "query_weight": query_weight, "key_weight": key_weight, "value_weight": value_weight, "out_weight": out_weight, "gate_weight": gate_weight, "up_weight": up_weight, "down_weight": down_weight, "query_gain": query_gain, "key_gain": key_gain, "attention_gain": attention_gain, "feed_gain": feed_gain, "pair_table": pair_table}


@jax.custom_vjp
def low(v):
    return lax.optimization_barrier(v.astype(jnp.bfloat16)).astype(jnp.float32)

@jax.custom_vjp
def low_back(v):
    return v

def low_keep(v):
    return (low(v), None)

def low_pass(kept, grad):
    return (grad,)

def back_keep(v):
    return (v, None)

def back_low(kept, grad):
    return (low(grad),)
low.defvjp(low_keep, low_pass)
low_back.defvjp(back_keep, back_low)
EPSILON = 1e-06
THETA = 500000.0

def rms_scale(values, gain):
    return values * lax.rsqrt(lax.optimization_barrier(jnp.mean(values * values, axis=-1, keepdims=True)) + EPSILON) * gain

def rotate(values, positions):
    freqs = THETA ** (-jnp.arange(0, HD, 2, dtype=jnp.float32) / HD)
    phase = positions.astype(jnp.float32)[:, None] * freqs[None, :]
    cosine = jnp.concatenate([jnp.cos(phase), jnp.cos(phase)], axis=-1)
    sine = jnp.concatenate([jnp.sin(phase), jnp.sin(phase)], axis=-1)
    shaped = values.reshape(values.shape[0], H, HD)
    middle = HD // 2
    turned = jnp.concatenate([-shaped[..., middle:], shaped[..., :middle]], axis=-1)
    return (shaped * cosine[:, None, :] + turned * sine[:, None, :]).reshape(values.shape)

def matmul(left, right):
    return jnp.dot(left, right, precision=lax.Precision.HIGHEST)

def layer(inputs, positions, query_weight, key_weight, value_weight, out_weight, gate_weight, up_weight, down_weight, query_gain, key_gain, attention_gain, feed_gain):
    length = inputs.shape[0]
    query_proj = low_back(matmul(inputs, query_weight))
    key_proj = low_back(matmul(inputs, key_weight))
    values = low(low_back(matmul(inputs, value_weight)))
    queries = low(rotate(rms_scale(query_proj, query_gain), positions))
    keys = low(rotate(rms_scale(key_proj, key_gain), positions))
    scores = jnp.einsum('qhd,khd->hqk', queries.reshape(length, H, HD), keys.reshape(length, H, HD), precision=lax.Precision.HIGHEST)
    scores = low_back(scores * HD ** (-0.5))
    allowed = positions[:, None] >= positions[None, :]
    scores = jnp.where(allowed[None], scores, -1e+30)
    probs = low(jax.nn.softmax(scores, axis=-1))
    mixed = jnp.einsum('hqk,khd->qhd', probs, values.reshape(length, H, HD), precision=lax.Precision.HIGHEST).reshape(length, -1)
    mixed = low(low_back(mixed))
    attn_raw = low_back(matmul(mixed, out_weight))
    hidden = inputs + rms_scale(attn_raw, attention_gain)
    hidden_low = low(hidden)
    gate_pre = low_back(matmul(hidden_low, gate_weight))
    up_pre = low_back(matmul(hidden_low, up_weight))
    product = low(jax.nn.silu(gate_pre) * up_pre)
    down_pre = low_back(matmul(product, down_weight))
    return hidden + rms_scale(down_pre, feed_gain)

def reference(layer_input, cotangent, query_weight, key_weight, value_weight, out_weight, gate_weight, up_weight, down_weight, query_gain, key_gain, attention_gain, feed_gain, pair_table):
    block_len = SEQ_LEN // (2 * N_CTX)
    blocks = pair_table.reshape(-1).astype(jnp.int32)
    positions = (blocks[:, None] * block_len + jnp.arange(block_len, dtype=jnp.int32)[None, :]).reshape(-1)
    params = tuple((weight.astype(jnp.float32) for weight in (query_weight, key_weight, value_weight, out_weight, gate_weight, up_weight, down_weight, query_gain, key_gain, attention_gain, feed_gain)))
    group = math.gcd(SEQS, 4)
    inputs = layer_input.astype(jnp.float32).reshape(SEQS // group, group, SEQ_LEN, D)
    upstream = cotangent.astype(jnp.float32).reshape(SEQS // group, group, SEQ_LEN, D)

    def forward(batch, *weights):
        return jax.vmap(lambda single: layer(single, positions, *weights))(batch)

    def step(totals, batch):
        batch_in, batch_cot = batch
        output, pull = jax.vjp(forward, batch_in, *params)
        grads = pull(batch_cot)
        return (tuple((total + grad for total, grad in zip(totals, grads[1:]))), (output, grads[0]))
    zeros = tuple((jnp.zeros_like(weight) for weight in params))
    totals, (outputs, input_grads) = lax.scan(step, zeros, (inputs, upstream))
    return (outputs.reshape(SEQS, SEQ_LEN, D).astype(jnp.bfloat16), input_grads.reshape(SEQS, SEQ_LEN, D), totals[0], totals[1], totals[2], totals[3], totals[4], totals[5], totals[6], totals[7], totals[8], totals[9], totals[10])
```

```python
import jax
import jax.numpy as jnp
from jax import lax
from jax.sharding import PartitionSpec as P

H = 32
HD = 64
EPSILON = 1e-06
THETA = 500000.0


def rms_scale(values, gain):
    return values * lax.rsqrt(jnp.mean(values * values, axis=-1, keepdims=True) + EPSILON) * gain


def angles(positions):
    freqs = THETA ** (-jnp.arange(0, HD, 2, dtype=jnp.float32) / HD)
    phase = positions.astype(jnp.float32)[:, None] * freqs[None, :]
    cosine = jnp.concatenate([jnp.cos(phase), jnp.cos(phase)], axis=-1)
    sine = jnp.concatenate([jnp.sin(phase), jnp.sin(phase)], axis=-1)
    return (cosine, sine)


def rotate(values, cosine, sine):
    shaped = values.reshape(values.shape[0], -1, HD)
    middle = HD // 2
    turned = jnp.concatenate([-shaped[..., middle:], shaped[..., :middle]], axis=-1)
    return (shaped * cosine[:, None, :] + turned * sine[:, None, :]).reshape(values.shape)


def rotate_back(values, cosine, sine):
    shaped = values.reshape(values.shape[0], -1, HD)
    middle = HD // 2
    spun = shaped * sine[:, None, :]
    turned = jnp.concatenate([spun[..., middle:], -spun[..., :middle]], axis=-1)
    return (shaped * cosine[:, None, :] + turned).reshape(values.shape)


def masked_scores(query_heads, key_heads, positions):
    raw = jnp.einsum(
        "qhd,khd->hqk", query_heads, key_heads, preferred_element_type=jnp.float32
    ) * HD ** (-0.5)
    allowed = positions[:, None] >= positions[None, :]
    return jnp.where(allowed[None], raw, -1e30)


def dot(left, right):
    return jnp.dot(left, right, preferred_element_type=jnp.float32)


def outer_sum(left, right):
    return lax.dot_general(
        left, right, (((0,), (0,)), ((), ())), preferred_element_type=jnp.float32
    )


def back_dot(grad, weight):
    return lax.dot_general(
        grad, weight, (((1,), (1,)), ((), ())), preferred_element_type=jnp.float32
    )


def low(values):
    return values.astype(jnp.bfloat16)


def over_ctx(block):
    return lax.all_gather(block, "ctx", axis=0, tiled=True)


def sum_ctx(partial):
    return lax.psum_scatter(low(partial), "ctx", scatter_dimension=0, tiled=True).astype(jnp.float32)


def body(
    layer_input,
    cotangent,
    query_weight,
    key_weight,
    value_weight,
    out_weight,
    gate_weight,
    up_weight,
    down_weight,
    query_gain,
    key_gain,
    attention_gain,
    feed_gain,
    pair_table,
):
    row_count = layer_input.shape[1]
    block_len = row_count // 2
    rank = lax.axis_index("ctx")
    owner = lax.axis_index("fsdp")
    ranks = lax.axis_size("ctx")
    width = query_weight.shape[1]
    share = width // ranks
    units = gate_weight.shape[1] // ranks
    blocks = pair_table.reshape(-1)
    positions = (
        blocks[:, None] * block_len + jnp.arange(block_len, dtype=jnp.int32)[None, :]
    ).reshape(-1)
    cosine, sine = angles(positions)

    def cut(weight, size):
        return lax.dynamic_slice_in_dim(weight, rank * size, size, axis=1)

    def rows_of(weight):
        here = (2 * rank + jnp.arange(2)) == owner
        placed = jnp.where(here[:, None, None], weight[None], jnp.zeros((), weight.dtype))
        return lax.psum(placed.reshape(-1, weight.shape[1]), "fsdp")

    inputs = layer_input[0]
    qkv = lax.all_gather(
        jnp.concatenate([cut(w, share) for w in (query_weight, key_weight, value_weight)], axis=1),
        "fsdp",
        axis=0,
        tiled=True,
    )
    gains = lax.all_gather(
        jnp.stack([query_gain, key_gain, attention_gain, feed_gain]), "fsdp", axis=1, tiled=True
    ).astype(jnp.float32)
    query_scale = lax.dynamic_slice_in_dim(gains[0], rank * share, share)
    key_scale = lax.dynamic_slice_in_dim(gains[1], rank * share, share)
    attn_scale, feed_scale = gains[2], gains[3]
    seq_inputs = over_ctx(inputs)
    gate_up = lax.all_gather(
        jnp.concatenate([cut(gate_weight, units), cut(up_weight, units)], axis=1),
        "fsdp",
        axis=0,
        tiled=True,
    )
    out_rows = rows_of(out_weight)
    down_rows = rows_of(down_weight)

    proj = dot(seq_inputs, qkv)
    query_proj, key_proj, value_proj = (
        proj[:, :share],
        proj[:, share : 2 * share],
        proj[:, 2 * share :],
    )
    squares = jnp.stack(
        [jnp.sum(query_proj * query_proj, axis=-1), jnp.sum(key_proj * key_proj, axis=-1)]
    )
    inverse = lax.rsqrt(lax.psum(squares, "ctx") / width + EPSILON)
    query_inv, key_inv = inverse[0][:, None], inverse[1][:, None]
    queries = low(rotate(query_proj * query_inv * query_scale, cosine, sine))
    keys = low(rotate(key_proj * key_inv * key_scale, cosine, sine))
    values = low(value_proj)
    length = queries.shape[0]
    query_heads = queries.reshape(length, -1, HD)
    key_heads = keys.reshape(length, -1, HD)
    value_heads = values.reshape(length, -1, HD)
    scores = masked_scores(query_heads, key_heads, positions)
    row_top = jnp.max(scores, axis=-1, keepdims=True)
    expo = jnp.exp(scores - row_top)
    totals = jnp.sum(expo, axis=-1, keepdims=True)
    log_total = row_top + jnp.log(totals)
    probs_low = low(expo / totals)
    mixed = low(
        jnp.einsum(
            "hqk,khd->qhd", probs_low, value_heads, preferred_element_type=jnp.float32
        ).reshape(length, -1)
    )
    attn_raw = sum_ctx(dot(mixed, out_rows))
    hidden = inputs.astype(jnp.float32) + rms_scale(attn_raw, attn_scale)
    seq_hidden = over_ctx(low(hidden))
    pre = dot(seq_hidden, gate_up)
    gate_pre, up_pre = pre[:, :units], pre[:, units:]
    sigmoid = jax.nn.sigmoid(gate_pre)
    product = low(gate_pre * sigmoid * up_pre)
    down_pre = sum_ctx(dot(product, down_rows))
    result = hidden + rms_scale(down_pre, feed_scale)
    upstream = cotangent[0].astype(jnp.float32)
    _, pull_feed = jax.vjp(rms_scale, down_pre, feed_scale)
    down_grad, feed_term = pull_feed(upstream)
    seq_down = over_ctx(low(down_grad))
    product_grad = back_dot(seq_down, down_rows)
    gate_low = low(product_grad * up_pre * sigmoid * (1.0 + gate_pre * (1.0 - sigmoid)))
    up_low = low(product_grad * gate_pre * sigmoid)
    both_low = jnp.concatenate([gate_low, up_low], axis=1)
    hidden_grad = upstream + sum_ctx(back_dot(both_low, gate_up))
    gate_up_grad = outer_sum(seq_hidden, both_low)
    down_rows_grad = outer_sum(product, seq_down)
    gate_up_share = lax.psum_scatter(low(gate_up_grad), "fsdp", scatter_dimension=0, tiled=True)
    down_share = lax.psum_scatter(low(down_rows_grad), "fsdp", scatter_dimension=1, tiled=True)
    _, pull_attn = jax.vjp(rms_scale, attn_raw, attn_scale)
    attn_grad, attn_term = pull_attn(hidden_grad)
    seq_attn = over_ctx(low(attn_grad))
    out_rows_grad = outer_sum(mixed, seq_attn)
    out_share = lax.psum_scatter(low(out_rows_grad), "fsdp", scatter_dimension=1, tiled=True)
    mixed_grad = low(back_dot(seq_attn, out_rows)).reshape(length, -1, HD)
    probs_back = jnp.exp(masked_scores(query_heads, key_heads, positions) - log_total)
    prob_grad = jnp.einsum(
        "qhd,khd->hqk", mixed_grad, value_heads, preferred_element_type=jnp.float32
    )
    delta = jnp.sum(probs_back * prob_grad, axis=-1, keepdims=True)
    score_low = low(probs_back * (prob_grad - delta))
    query_rot_grad = jnp.einsum(
        "hqk,khd->qhd", score_low, key_heads, preferred_element_type=jnp.float32
    ).reshape(length, -1) * HD ** (-0.5)
    key_rot_grad = jnp.einsum(
        "hqk,qhd->khd", score_low, query_heads, preferred_element_type=jnp.float32
    ).reshape(length, -1) * HD ** (-0.5)
    value_low = low(
        jnp.einsum(
            "hqk,qhd->khd", low(probs_back), mixed_grad, preferred_element_type=jnp.float32
        ).reshape(length, -1)
    )
    query_turn = rotate_back(query_rot_grad, cosine, sine)
    key_turn = rotate_back(key_rot_grad, cosine, sine)
    query_unit, key_unit = query_proj * query_inv, key_proj * key_inv
    query_term = jnp.sum(query_turn * query_unit, axis=0)
    key_term = jnp.sum(key_turn * key_unit, axis=0)
    query_pull, key_pull = query_turn * query_scale, key_turn * key_scale
    dots = jnp.stack(
        [jnp.sum(query_pull * query_unit, axis=-1), jnp.sum(key_pull * key_unit, axis=-1)]
    )
    means = lax.psum(dots, "ctx") / width
    query_low = low(query_inv * (query_pull - query_unit * means[0][:, None]))
    key_low = low(key_inv * (key_pull - key_unit * means[1][:, None]))
    qkv_low = jnp.concatenate([query_low, key_low, value_low], axis=1)
    input_grad = hidden_grad + sum_ctx(back_dot(qkv_low, qkv))
    qkv_grad = outer_sum(seq_inputs, qkv_low)
    qkv_share = lax.psum_scatter(low(qkv_grad), "fsdp", scatter_dimension=0, tiled=True)

    def columns(part, count):
        all_parts = lax.all_gather(part, "ctx", axis=0)
        size = part.shape[1] // count
        return tuple(
            all_parts[:, :, i * size : (i + 1) * size]
            .transpose(1, 0, 2)
            .reshape(part.shape[0], -1)
            .astype(jnp.float32)
            for i in range(count)
        )

    def rows(part):
        all_parts = lax.all_gather(part, "ctx", axis=0, tiled=True)
        return lax.all_to_all(
            all_parts, "fsdp", split_axis=0, concat_axis=1, tiled=True
        ).astype(jnp.float32)

    gate_share, up_share = columns(gate_up_share, 2)
    query_share, key_share, value_share = columns(qkv_share, 3)
    down_share = rows(down_share)
    out_share = rows(out_share)

    def placed(term):
        return lax.dynamic_update_slice_in_dim(
            jnp.zeros((width,), jnp.float32), term, rank * share, axis=0
        )

    gain_terms = lax.psum(
        jnp.stack([placed(query_term), placed(key_term), attn_term, feed_term]), ("ctx", "fsdp")
    )
    mine = lax.dynamic_slice_in_dim(
        gain_terms, owner * query_gain.shape[0], query_gain.shape[0], axis=1
    )
    return (
        result.astype(jnp.bfloat16)[None],
        input_grad[None],
        query_share,
        key_share,
        value_share,
        out_share,
        gate_share,
        up_share,
        down_share,
        mine[0],
        mine[1],
        mine[2],
        mine[3],
    )


def solution(mesh):
    weights = (P("fsdp", None),) * 7
    gains = (P("fsdp"),) * 4
    tokens = P("fsdp", "ctx", None)
    in_specs = (tokens, tokens, *weights, *gains, P())
    out_specs = (tokens, tokens, *weights, *gains)
    return jax.shard_map(body, mesh=mesh, in_specs=in_specs, out_specs=out_specs, check_vma=False)
```

```python
import functools

import jax
import jax.numpy as jnp
from jax import lax
from jax.experimental import pallas as pl
from jax.experimental.pallas import tpu as pltpu
from jax.sharding import PartitionSpec as P

HD = 64
EPSILON = 1e-06
THETA = 500000.0
MESH = pl.DeviceIdType.MESH
F32 = jnp.float32
BF16 = jnp.bfloat16
ROOM = 56 * 2**20
NEG = -1e30


def angles(positions):
    freqs = THETA ** (-jnp.arange(0, HD, 2, dtype=F32) / HD)
    phase = positions.astype(F32)[:, None] * freqs[None, :]
    cosine, sine = jnp.cos(phase), jnp.sin(phase)
    return jnp.tile(cosine, (1, 4)), jnp.tile(sine, (1, 4))


def rms_scale(values, gain):
    return values * lax.rsqrt(jnp.mean(values * values, axis=-1, keepdims=True) + EPSILON) * gain


def dot(left, right):
    return jnp.dot(left, right, preferred_element_type=F32)


def outer_sum(left, right):
    return lax.dot_general(left, right, (((0,), (0,)), ((), ())), preferred_element_type=F32)


def back_dot(grad, weight):
    return lax.dot_general(grad, weight, (((1,), (1,)), ((), ())), preferred_element_type=F32)


def low(values):
    return values.astype(BF16)


def places():
    rank = lax.axis_index("ctx")
    ring = lax.axis_size("ctx") // 2
    z, x = rank // ring, lax.rem(rank, ring)

    def at(other, step):
        row = 1 - z if other else z
        return row * ring + lax.rem(x + step, ring)

    return rank, at


def meet(peers):
    barrier = pltpu.get_barrier_semaphore()
    for peer in peers:
        pl.semaphore_signal(barrier, inc=1, device_id={"ctx": peer}, device_id_type=MESH)
    pl.semaphore_wait(barrier, len(peers))


def send(src, dst, sems, index, peer):
    out, into = sems
    return pltpu.make_async_remote_copy(
        src_ref=src,
        dst_ref=dst,
        send_sem=out.at[index],
        recv_sem=into.at[index],
        device_id={"ctx": peer},
        device_id_type=MESH,
    )


def rows_at(index, size):
    return pl.ds(pl.multiple_of(index * size, size), size)


def gather_kernel(tile, transposed, *refs):
    if tile:
        block, weight_far, whole, product, landed, weight, sent, came, local = refs
    else:
        block, whole, landed, sent, came, local = refs
    rank, at = places()
    size = block.shape[0]
    half = size // 2
    left, right, partner = at(False, 3), at(False, 1), at(True, 0)
    if tile:
        fetch = pltpu.make_async_copy(weight_far, weight, local.at[8])
        fetch.start()
    meet((left, right, partner))
    sems = (sent, came)

    def move(src, index, part, number, peer):
        view = landed.at[index] if part is None else landed.at[index, pl.ds(part * half, half)]
        copy = send(view if src is None else src, view, sems, number, peer)
        copy.start()
        return copy

    copies = [
        move(block, rank, None, 0, right),
        move(block, rank, None, 1, left),
        move(block, rank, None, 2, partner),
    ]
    stores = []

    def use(src, index, number):
        store = pltpu.make_async_copy(src, whole.at[index], local.at[number])
        store.start()
        stores.append(store)
        if not tile:
            return
        rows = rows_at(index, size)
        value = src[...]

        def step(i, carry):
            span = rows_at(i, tile)
            if transposed:
                product[rows, span] = back_dot(value, weight[span, :])
            else:
                product[rows, span] = dot(value, weight[:, span])
            return carry

        lax.fori_loop(0, product.shape[1] // tile, step, 0)

    if tile:
        fetch.wait()
    use(block, rank, 0)
    copies[0].wait_recv()
    copies.append(move(None, left, 0, 5, right))
    copies[1].wait_recv()
    copies.append(move(None, right, 1, 6, left))
    copies[2].wait_recv()
    copies.append(move(None, partner, None, 3, right))
    copies.append(move(None, partner, None, 4, left))
    use(landed.at[left], left, 1)
    use(landed.at[right], right, 2)
    use(landed.at[partner], partner, 3)
    copies[5].wait_recv()
    copies.append(move(None, at(True, 3), 0, 7, right))
    copies[6].wait_recv()
    copies.append(move(None, at(True, 1), 1, 8, left))
    use(landed.at[at(True, 3)], at(True, 3), 4)
    use(landed.at[at(True, 1)], at(True, 1), 5)
    copies[3].wait_recv()
    copies[4].wait_recv()
    use(landed.at[at(False, 2)], at(False, 2), 6)
    copies[7].wait_recv()
    copies[8].wait_recv()
    use(landed.at[at(True, 2)], at(True, 2), 7)
    for copy in copies:
        copy.wait_send()
    for store in stores:
        store.wait()


def gather_dot(block, weight, number, tile=0, transposed=False):
    ranks = lax.axis_size("ctx")
    size, depth = block.shape
    anywhere = pl.BlockSpec(memory_space=pl.ANY)
    near = pl.BlockSpec(memory_space=pltpu.VMEM)
    out_shape = [jax.ShapeDtypeStruct((ranks, size, depth), block.dtype)]
    out_specs, in_specs, args = [anywhere], [near], [block]
    scratch = [pltpu.VMEM((ranks, size, depth), block.dtype)]
    moved = ranks * size * depth * 2
    flops = 0
    if tile:
        columns = weight.shape[0] if transposed else weight.shape[1]
        out_shape.append(jax.ShapeDtypeStruct((ranks * size, columns), F32))
        out_specs.append(near)
        in_specs.append(anywhere)
        args.append(weight)
        scratch.append(pltpu.VMEM(weight.shape, weight.dtype))
        flops = 2 * ranks * size * depth * columns
    outs = pl.pallas_call(
        functools.partial(gather_kernel, tile, transposed),
        out_shape=out_shape,
        in_specs=in_specs,
        out_specs=out_specs,
        scratch_shapes=scratch
        + [
            pltpu.SemaphoreType.DMA((9,)),
            pltpu.SemaphoreType.DMA((9,)),
            pltpu.SemaphoreType.DMA((9,)),
        ],
        cost_estimate=pl.CostEstimate(flops=flops, bytes_accessed=30 * moved, transcendentals=0),
        compiler_params=pltpu.CompilerParams(
            collective_id=number, has_side_effects=True, vmem_limit_bytes=ROOM
        ),
    )(*args)
    whole = outs[0].reshape(ranks * size, depth)
    return (whole, outs[1]) if tile else whole


def scatter_kernel(
    tile,
    transposed,
    act_far,
    weight_far,
    total,
    act,
    weight,
    part,
    from_far,
    from_side,
    from_partner,
    sent,
    came,
    local,
):
    rank, at = places()
    size, width = total.shape
    half = width // 2
    left, right, partner = at(False, 3), at(False, 1), at(True, 0)
    fetch_act = pltpu.make_async_copy(act_far, act, local.at[0])
    fetch_act.start()
    fetch = pltpu.make_async_copy(weight_far, weight, local.at[1])
    fetch.start()
    meet((left, right, partner))
    sems = (sent, came)
    first, second = pl.ds(0, half), pl.ds(half, half)

    def work(index, keep):
        value = act[rows_at(index, size), :]

        def step(i, carry):
            span = rows_at(i, tile)
            if transposed:
                piece = back_dot(value, weight[span, :])
            else:
                piece = dot(value, weight[:, span])
            if keep:
                total[:, span] = piece
            else:
                part[index, :, span] = low(piece)
            return carry

        lax.fori_loop(0, width // tile, step, 0)

    fetch_act.wait()
    fetch.wait()
    copies = []
    far = []
    for i, other in enumerate((True, False)):
        index = at(other, 2)
        work(index, False)
        far.append(
            (
                send(part.at[index, :, first], from_far.at[0, i], sems, 4 * i, right),
                send(part.at[index, :, second], from_far.at[1, i], sems, 4 * i + 1, left),
            )
        )
        for copy in far[-1]:
            copy.start()
            copies.append(copy)
    side = []
    for i, other in enumerate((True, False)):
        after, before = at(other, 1), at(other, 3)
        work(after, False)
        work(before, False)
        far[i][0].wait_recv()
        part[after, :, first] = low(
            part[after, :, first].astype(F32) + from_far[0, i].astype(F32)
        )
        to_right = send(part.at[after], from_side.at[0, i], sems, 4 * i + 2, right)
        to_right.start()
        far[i][1].wait_recv()
        part[before, :, second] = low(
            part[before, :, second].astype(F32) + from_far[1, i].astype(F32)
        )
        to_left = send(part.at[before], from_side.at[1, i], sems, 4 * i + 3, left)
        to_left.start()
        side.append((to_right, to_left))
        copies += [to_right, to_left]
    work(partner, False)
    work(rank, True)
    side[0][0].wait_recv()
    side[0][1].wait_recv()
    part[partner] = low(
        part[partner].astype(F32) + from_side[0, 0].astype(F32) + from_side[1, 0].astype(F32)
    )
    across = send(part.at[partner], from_partner, sems, 8, partner)
    across.start()
    side[1][0].wait_recv()
    side[1][1].wait_recv()
    total[...] += from_side[0, 1].astype(F32) + from_side[1, 1].astype(F32)
    across.wait_recv()
    total[...] += from_partner[...].astype(F32)
    for copy in copies:
        copy.wait_send()
    across.wait_send()


def dot_scatter(act, weight, number, tile=512, transposed=False):
    ranks = lax.axis_size("ctx")
    size = act.shape[0] // ranks
    width = weight.shape[0] if transposed else weight.shape[1]
    anywhere = pl.BlockSpec(memory_space=pl.ANY)
    return pl.pallas_call(
        functools.partial(scatter_kernel, tile, transposed),
        out_shape=jax.ShapeDtypeStruct((size, width), F32),
        in_specs=[anywhere, anywhere],
        out_specs=pl.BlockSpec(memory_space=pltpu.VMEM),
        scratch_shapes=[
            pltpu.VMEM(act.shape, act.dtype),
            pltpu.VMEM(weight.shape, weight.dtype),
            pltpu.VMEM((ranks, size, width), BF16),
            pltpu.VMEM((2, 2, size, width // 2), BF16),
            pltpu.VMEM((2, 2, size, width), BF16),
            pltpu.VMEM((size, width), BF16),
            pltpu.SemaphoreType.DMA((9,)),
            pltpu.SemaphoreType.DMA((9,)),
            pltpu.SemaphoreType.DMA((2,)),
        ],
        cost_estimate=pl.CostEstimate(
            flops=2 * act.shape[0] * act.shape[1] * width,
            bytes_accessed=30 * ranks * size * width * 2,
            transcendentals=0,
        ),
        compiler_params=pltpu.CompilerParams(
            collective_id=number, has_side_effects=True, vmem_limit_bytes=ROOM
        ),
    )(act, weight)


def total_kernel(mine, total, landed, sent, came):
    rank = lax.axis_index("ctx")
    ranks = lax.axis_size("ctx")
    peers = [lax.rem(rank + step, ranks) for step in range(1, ranks)]
    meet(peers)
    copies = [
        send(mine, landed.at[i], (sent, came), i, peer) for i, peer in enumerate(peers)
    ]
    for copy in copies:
        copy.start()
    for copy in copies:
        copy.wait()
    total[...] = mine[...] + jnp.sum(landed[...], axis=0)


def total_over_ctx(pair, number):
    peers = lax.axis_size("ctx") - 1
    mine = jnp.concatenate([pair] * 4, axis=0)
    near = pl.BlockSpec(memory_space=pltpu.VMEM)
    return pl.pallas_call(
        total_kernel,
        out_shape=jax.ShapeDtypeStruct(mine.shape, F32),
        in_specs=[near],
        out_specs=near,
        scratch_shapes=[
            pltpu.VMEM((peers, *mine.shape), F32),
            pltpu.SemaphoreType.DMA((peers,)),
            pltpu.SemaphoreType.DMA((peers,)),
        ],
        compiler_params=pltpu.CompilerParams(
            collective_id=number, has_side_effects=True, vmem_limit_bytes=ROOM
        ),
    )(mine)[:2]


def head_lanes(shape):
    return lax.broadcasted_iota(jnp.int32, shape, 1) < HD


def turn_lanes(shape):
    return lax.rem(lax.broadcasted_iota(jnp.int32, shape, 1), HD) < HD // 2


def turned(values):
    lanes = values.shape[1]
    ahead = pltpu.roll(values, lanes - HD // 2, 1)
    behind = pltpu.roll(values, HD // 2, 1)
    return jnp.where(turn_lanes(values.shape), -ahead, behind)


def turned_back(values):
    lanes = values.shape[1]
    ahead = pltpu.roll(values, lanes - HD // 2, 1)
    behind = pltpu.roll(values, HD // 2, 1)
    return jnp.where(turn_lanes(values.shape), ahead, -behind)


def soft(keys, query, key_pos, query_pos):
    scores = back_dot(keys, query) * HD ** (-0.5)
    scores = jnp.where(query_pos >= key_pos, scores, NEG)
    expo = jnp.exp(scores - jnp.max(scores, axis=0, keepdims=True))
    return expo / jnp.sum(expo, axis=0, keepdims=True)


def mix_kernel(
    chunk,
    query_unit,
    key_unit,
    value_proj,
    query_gain,
    key_gain,
    cosine,
    sine,
    key_pos,
    query_pos,
    queries,
    keys,
    values,
    mixed,
):
    def front(unit, gain):
        scaled = unit[...] * gain[...]
        return low(scaled * cosine[...] + turned(scaled) * sine[...])

    queries[...] = front(query_unit, query_gain)
    keys[...] = front(key_unit, key_gain)
    values[...] = low(value_proj[...])
    value_turned = values[...].astype(F32).T.astype(BF16)

    def step(i, carry):
        rows = rows_at(i, chunk)
        query = queries[rows, :]
        first = head_lanes(query.shape)
        nothing = jnp.zeros_like(query)
        outs = []
        for mask in (first, jnp.logical_not(first)):
            probs = soft(
                keys[...], jnp.where(mask, query, nothing), key_pos[...], query_pos[:, rows]
            )
            outs.append(dot(value_turned, low(probs)))
        both = jnp.concatenate([outs[0][:HD], outs[1][HD:]], axis=0)
        mixed[rows, :] = low(both.T)
        return carry

    lax.fori_loop(0, queries.shape[0] // chunk, step, 0)


def mix(query_unit, key_unit, value_proj, query_gain, key_gain, cosine, sine, positions, chunk=256):
    length, share = query_unit.shape
    lanes = 2 * HD
    columns = pl.BlockSpec((length, lanes), lambda i: (0, i))
    fixed = lambda shape: pl.BlockSpec(shape, lambda i: (0, 0))
    gain = pl.BlockSpec((1, lanes), lambda i: (0, i))
    return pl.pallas_call(
        functools.partial(mix_kernel, chunk),
        grid=(share // lanes,),
        out_shape=[jax.ShapeDtypeStruct((length, share), BF16)] * 4,
        in_specs=[columns] * 3
        + [gain] * 2
        + [fixed((length, lanes))] * 2
        + [fixed((length, 1)), fixed((1, length))],
        out_specs=[columns] * 4,
        compiler_params=pltpu.CompilerParams(vmem_limit_bytes=ROOM),
    )(
        query_unit,
        key_unit,
        value_proj,
        query_gain[None],
        key_gain[None],
        cosine,
        sine,
        positions[:, None],
        positions[None, :],
    )


def mix_back_kernel(
    chunk,
    queries,
    keys,
    values,
    mixed_grad,
    cosine,
    sine,
    key_pos,
    query_pos,
    query_turn,
    key_turn,
    value_low,
    key_sum,
    value_sum,
):
    key_turned = keys[...].astype(F32).T.astype(BF16)
    key_sum[...] = jnp.zeros_like(key_sum)
    value_sum[...] = jnp.zeros_like(value_sum)

    def step(i, carry):
        rows = rows_at(i, chunk)
        query, grad = queries[rows, :], mixed_grad[rows, :]
        first = head_lanes(query.shape)
        nothing = jnp.zeros_like(query)
        outs = []
        for mask in (first, jnp.logical_not(first)):
            query_head, grad_head = jnp.where(mask, query, nothing), jnp.where(mask, grad, nothing)
            probs = soft(keys[...], query_head, key_pos[...], query_pos[:, rows])
            prob_grad = back_dot(values[...], grad_head)
            delta = jnp.sum(probs * prob_grad, axis=0, keepdims=True)
            score_low = low(probs * (prob_grad - delta))
            value_sum[...] += dot(low(probs), grad_head)
            key_sum[...] += dot(score_low, query_head)
            outs.append(dot(key_turned, score_low))
        both = jnp.concatenate([outs[0][:HD], outs[1][HD:]], axis=0) * HD ** (-0.5)
        query_rot = both.T
        query_turn[rows, :] = query_rot * cosine[rows, :] + turned_back(query_rot * sine[rows, :])
        return carry

    lax.fori_loop(0, queries.shape[0] // chunk, step, 0)
    key_rot = key_sum[...] * HD ** (-0.5)
    key_turn[...] = key_rot * cosine[...] + turned_back(key_rot * sine[...])
    value_low[...] = low(value_sum[...])


def mix_back(queries, keys, values, mixed_grad, cosine, sine, positions, chunk=256):
    length, share = queries.shape
    lanes = 2 * HD
    columns = pl.BlockSpec((length, lanes), lambda i: (0, i))
    fixed = lambda shape: pl.BlockSpec(shape, lambda i: (0, 0))
    return pl.pallas_call(
        functools.partial(mix_back_kernel, chunk),
        grid=(share // lanes,),
        out_shape=[
            jax.ShapeDtypeStruct((length, share), F32),
            jax.ShapeDtypeStruct((length, share), F32),
            jax.ShapeDtypeStruct((length, share), BF16),
        ],
        in_specs=[columns] * 4
        + [fixed((length, lanes))] * 2
        + [fixed((length, 1)), fixed((1, length))],
        out_specs=[columns] * 3,
        scratch_shapes=[pltpu.VMEM((length, lanes), F32), pltpu.VMEM((length, lanes), F32)],
        compiler_params=pltpu.CompilerParams(vmem_limit_bytes=ROOM),
    )(queries, keys, values, mixed_grad, cosine, sine, positions[:, None], positions[None, :])


def body(
    layer_input,
    cotangent,
    query_weight,
    key_weight,
    value_weight,
    out_weight,
    gate_weight,
    up_weight,
    down_weight,
    query_gain,
    key_gain,
    attention_gain,
    feed_gain,
    pair_table,
):
    row_count = layer_input.shape[1]
    block_len = row_count // 2
    rank = lax.axis_index("ctx")
    owner = lax.axis_index("fsdp")
    ranks = lax.axis_size("ctx")
    owners = lax.axis_size("fsdp")
    width = query_weight.shape[1]
    share = width // ranks
    strip = width // owners
    units = gate_weight.shape[1] // ranks
    room = -(-units // 256) * 256
    blocks = pair_table.reshape(-1)
    positions = (
        blocks[:, None] * block_len + jnp.arange(block_len, dtype=jnp.int32)[None, :]
    ).reshape(-1)
    cosine, sine = angles(positions)

    def cut(weight, size):
        return lax.dynamic_slice_in_dim(weight, rank * size, size, axis=1)

    def wide(weight):
        return jnp.pad(cut(weight, units), ((0, 0), (0, room - units)))

    flat = lambda c, f: c * owners + f
    odd = lax.rem(owner, 2)
    routes = [
        [
            (flat(c, 2 * d + j), flat(d, 2 * c + (j ^ k)))
            for c in range(ranks)
            for d in range(ranks)
            for j in range(2)
        ]
        for k in range(2)
    ]
    axes = ("ctx", "fsdp")
    tall = jnp.concatenate([out_weight, down_weight], axis=0)
    pieces = []
    for k, route in enumerate(routes):
        target = 2 * rank + (odd ^ k)
        strips = lax.dynamic_slice_in_dim(tall, target * strip, strip, axis=1)
        pieces.append(lax.ppermute(strips, axes, route))

    def in_order(pair):
        return jnp.where(odd == 0, pair[0], pair[1]), jnp.where(odd == 0, pair[1], pair[0])

    low_piece, high_piece = in_order(pieces)
    out_size = out_weight.shape[0]
    strips = jnp.concatenate(
        [
            low_piece[:out_size],
            high_piece[:out_size],
            low_piece[out_size:],
            high_piece[out_size:],
            jnp.zeros((room - units, strip), BF16),
        ],
        axis=0,
    )

    inputs = layer_input[0]
    qkv = lax.all_gather(
        jnp.concatenate([cut(w, share) for w in (query_weight, key_weight, value_weight)], axis=1),
        "fsdp",
        axis=0,
        tiled=True,
    )
    gains = lax.all_gather(
        jnp.stack([query_gain, key_gain, attention_gain, feed_gain]), "fsdp", axis=1, tiled=True
    ).astype(F32)
    query_scale = lax.dynamic_slice_in_dim(gains[0], rank * share, share)
    key_scale = lax.dynamic_slice_in_dim(gains[1], rank * share, share)
    attn_scale, feed_scale = gains[2], gains[3]
    seq_inputs = gather_dot(inputs, None, 1)
    out_down = lax.all_gather(strips, "fsdp", axis=1, tiled=True)
    out_rows, down_rows = out_down[:share], out_down[share:]
    gate_up = lax.all_gather(
        jnp.concatenate([wide(gate_weight), wide(up_weight)], axis=1), "fsdp", axis=0, tiled=True
    )

    proj = dot(seq_inputs, qkv)
    query_proj, key_proj, value_proj = (
        proj[:, :share],
        proj[:, share : 2 * share],
        proj[:, 2 * share :],
    )
    squares = jnp.stack(
        [jnp.sum(query_proj * query_proj, axis=-1), jnp.sum(key_proj * key_proj, axis=-1)]
    )
    inverse = lax.rsqrt(total_over_ctx(squares, 2) / width + EPSILON)
    query_inv, key_inv = inverse[0][:, None], inverse[1][:, None]
    query_unit, key_unit = query_proj * query_inv, key_proj * key_inv
    queries, keys, values, mixed = mix(
        query_unit, key_unit, value_proj, query_scale, key_scale, cosine, sine, positions
    )
    attn_raw = dot_scatter(mixed, out_rows, 3)
    hidden = inputs.astype(F32) + rms_scale(attn_raw, attn_scale)
    seq_hidden, pre = gather_dot(low(hidden), gate_up, 4, tile=512)
    gate_pre, up_pre = pre[:, :room], pre[:, room:]
    sigmoid = jax.nn.sigmoid(gate_pre)
    product = low(gate_pre * sigmoid * up_pre)
    down_pre = dot_scatter(product, down_rows, 5)
    result = hidden + rms_scale(down_pre, feed_scale)
    upstream = cotangent[0].astype(F32)
    _, pull_feed = jax.vjp(rms_scale, down_pre, feed_scale)
    down_grad, feed_term = pull_feed(upstream)
    seq_down, product_grad = gather_dot(low(down_grad), down_rows, 6, tile=256, transposed=True)
    gate_low = low(product_grad * up_pre * sigmoid * (1.0 + gate_pre * (1.0 - sigmoid)))
    up_low = low(product_grad * gate_pre * sigmoid)
    both_low = jnp.concatenate([gate_low, up_low], axis=1)
    hidden_grad = upstream + dot_scatter(both_low, gate_up, 7, transposed=True)
    gate_up_grad = outer_sum(seq_hidden, both_low)
    down_rows_grad = outer_sum(product, seq_down)
    gate_up_share = lax.psum_scatter(low(gate_up_grad), "fsdp", scatter_dimension=0, tiled=True)
    _, pull_attn = jax.vjp(rms_scale, attn_raw, attn_scale)
    attn_grad, attn_term = pull_attn(hidden_grad)
    seq_attn, mixed_grad = gather_dot(low(attn_grad), out_rows, 8, tile=256, transposed=True)
    out_rows_grad = outer_sum(mixed, seq_attn)
    out_down_share = lax.psum_scatter(
        low(jnp.concatenate([out_rows_grad, down_rows_grad], axis=0)),
        "fsdp",
        scatter_dimension=1,
        tiled=True,
    )
    query_turn, key_turn, value_low = mix_back(
        queries, keys, values, low(mixed_grad), cosine, sine, positions
    )
    query_term = jnp.sum(query_turn * query_unit, axis=0)
    key_term = jnp.sum(key_turn * key_unit, axis=0)
    query_pull, key_pull = query_turn * query_scale, key_turn * key_scale
    dots = jnp.stack(
        [jnp.sum(query_pull * query_unit, axis=-1), jnp.sum(key_pull * key_unit, axis=-1)]
    )
    means = total_over_ctx(dots, 9) / width
    query_low = low(query_inv * (query_pull - query_unit * means[0][:, None]))
    key_low = low(key_inv * (key_pull - key_unit * means[1][:, None]))
    qkv_low = jnp.concatenate([query_low, key_low, value_low], axis=1)
    qkv_grad = outer_sum(seq_inputs, qkv_low)
    qkv_share = lax.psum_scatter(low(qkv_grad), "fsdp", scatter_dimension=0, tiled=True)
    input_grad = hidden_grad + dot_scatter(qkv_low, qkv, 10, transposed=True)

    down_at = 2 * out_size
    down_size = down_weight.shape[0]
    by_owner = [
        jnp.concatenate(
            [
                out_down_share[j * out_size : (j + 1) * out_size],
                out_down_share[down_at + j * down_size : down_at + (j + 1) * down_size],
            ],
            axis=0,
        )
        for j in range(2)
    ]
    by_route = in_order(by_owner)
    returned = [
        lax.ppermute(piece, axes, [(b, a) for a, b in route])
        for piece, route in zip(by_route, routes)
    ]
    tall_share = jnp.concatenate(in_order(returned), axis=1)

    def spread(part, sizes):
        all_parts = lax.all_gather(part, "ctx", axis=0)
        outs, at = [], 0
        for size, step in sizes:
            columns = all_parts[:, :, at : at + size]
            outs.append(columns.transpose(1, 0, 2).reshape(part.shape[0], -1).astype(F32))
            at += step
        return outs

    gate_share, up_share = spread(gate_up_share, ((units, room),) * 2)
    (tall_whole,) = spread(tall_share, ((share, share),))
    query_share, key_share, value_share = spread(qkv_share, ((share, share),) * 3)
    out_share, down_share = tall_whole[:out_size], tall_whole[out_size:]

    def placed(term):
        return lax.dynamic_update_slice_in_dim(
            jnp.zeros((width,), F32), term, rank * share, axis=0
        )

    gain_terms = lax.psum(
        jnp.stack([placed(query_term), placed(key_term), attn_term, feed_term]), axes
    )
    mine = lax.dynamic_slice_in_dim(
        gain_terms, owner * query_gain.shape[0], query_gain.shape[0], axis=1
    )
    return (
        low(result)[None],
        input_grad[None],
        query_share,
        key_share,
        value_share,
        out_share,
        gate_share,
        up_share,
        down_share,
        mine[0],
        mine[1],
        mine[2],
        mine[3],
    )


def solution(mesh):
    weights = (P("fsdp", None),) * 7
    gains = (P("fsdp"),) * 4
    tokens = P("fsdp", "ctx", None)
    in_specs = (tokens, tokens, *weights, *gains, P())
    out_specs = (tokens, tokens, *weights, *gains)
    return jax.shard_map(body, mesh=mesh, in_specs=in_specs, out_specs=out_specs, check_vma=False)
```

```python
import functools

import jax
import jax.numpy as jnp
from jax import lax
from jax.experimental import pallas as pl
from jax.experimental.pallas import tpu as pltpu
from jax.sharding import PartitionSpec as P

HD = 64
EPSILON = 1e-06
THETA = 500000.0
MESH = pl.DeviceIdType.MESH
F32 = jnp.float32
BF16 = jnp.bfloat16
ROOM = 56 * 2**20
NEG = -1e30


def angles(positions):
    freqs = THETA ** (-jnp.arange(0, HD, 2, dtype=F32) / HD)
    phase = positions.astype(F32)[:, None] * jnp.tile(freqs, 4)[None, :]
    return jnp.cos(phase), jnp.sin(phase)


def rms_scale(values, gain):
    return values * lax.rsqrt(jnp.mean(values * values, axis=-1, keepdims=True) + EPSILON) * gain


def dot(left, right):
    return jnp.dot(left, right, preferred_element_type=F32)


def outer_sum(left, right):
    return lax.dot_general(left, right, (((0,), (0,)), ((), ())), preferred_element_type=F32)


def back_dot(grad, weight):
    return lax.dot_general(grad, weight, (((1,), (1,)), ((), ())), preferred_element_type=F32)


def low(values):
    return values.astype(BF16)


class Group:
    def __init__(self, axis):
        me = lax.axis_index(axis)
        self.axis = axis
        self.size = lax.axis_size(axis)
        self.me = me
        if axis == "ctx":
            self.core, self.pair, self.place = 0, me // 4, lax.rem(me, 4)
        else:
            self.core, self.pair, self.place = lax.rem(me, 2), lax.rem(me, 4) // 2, me // 4
        self.sibling = me + 1 - 2 * self.core if axis == "fsdp" else None
        self.right, self.left, self.partner = self.at(False, 1), self.at(False, 3), self.at(True, 0)

    def at(self, other, step):
        pair = 1 - self.pair if other else self.pair
        place = lax.rem(self.place + step, 4)
        if self.axis == "ctx":
            return pair * 4 + place
        return place * 4 + pair * 2 + self.core

    def peers(self):
        near = [self.right, self.left, self.partner]
        if self.sibling is not None:
            near.append(self.sibling)
        return [{self.axis: peer} for peer in near]


def meet(peers):
    barrier = pltpu.get_barrier_semaphore()
    for peer in peers:
        pl.semaphore_signal(barrier, inc=1, device_id=peer, device_id_type=MESH)
    pl.semaphore_wait(barrier, len(peers))


class Copies:
    def __init__(self, sent, came):
        self.sent, self.came, self.count, self.all = sent, came, 0, []

    def start(self, src, dst, peer):
        copy = pltpu.make_async_remote_copy(
            src_ref=src,
            dst_ref=dst,
            send_sem=self.sent.at[self.count],
            recv_sem=self.came.at[self.count],
            device_id=peer,
            device_id_type=MESH,
        )
        self.count += 1
        self.all.append(copy)
        copy.start()
        return copy

    def drain(self):
        for copy in self.all:
            copy.wait_send()


class Stores:
    def __init__(self, sems):
        self.sems, self.count, self.all = sems, 0, []

    def start(self, src, dst):
        copy = pltpu.make_async_copy(src, dst, self.sems.at[self.count])
        self.count += 1
        copy.start()
        self.all.append(copy)
        return copy

    def drain(self, done=()):
        for copy in self.all:
            if not any(copy is other for other in done):
                copy.wait()


def rows_at(index, size):
    return pl.ds(pl.multiple_of(index * size, size), size)


def block_of(ref, blocks, index, part=None):
    size = ref.shape[0] // blocks
    if part is None:
        return ref.at[rows_at(index, size)]
    half = size // 2
    return ref.at[pl.ds(pl.multiple_of(index * size + part * half, half), half)]


def arrived(copies):
    for copy in copies:
        copy.wait_recv()


def ring_gather(group, copies, items):
    blocks, at = group.size, group.at
    right, left, partner = ({group.axis: peer} for peer in (group.right, group.left, group.partner))

    def move(index, part, peer, own=False):
        started = []
        for mine, whole in items:
            view = block_of(whole, blocks, index, part)
            started.append(copies.start(mine if own else view, view, peer))
        return started

    near_left = move(group.me, None, right, True)
    near_right = move(group.me, None, left, True)
    across = move(group.me, None, partner, True)
    yield [group.me]
    arrived(near_left)
    far_left = move(group.left, 0, right)
    arrived(near_right)
    far_right = move(group.right, 1, left)
    arrived(across)
    other_left = move(group.partner, None, right)
    other_right = move(group.partner, None, left)
    yield [group.left, group.right, group.partner]
    arrived(other_left)
    last_left = move(at(True, 3), 0, right)
    arrived(other_right)
    last_right = move(at(True, 1), 1, left)
    yield [at(True, 3), at(True, 1)]
    arrived(far_left)
    arrived(far_right)
    yield [at(False, 2)]
    arrived(last_left)
    arrived(last_right)
    yield [at(True, 2)]


def ring_scatter(group, copies, items, prepare):
    blocks, at = group.size, group.at
    right, left, partner = ({group.axis: peer} for peer in (group.right, group.left, group.partner))

    def add(ref, others):
        value = ref[...].astype(F32)
        for other in others:
            value += other[...].astype(F32)
        ref[...] = low(value)

    far = []
    for i, other in enumerate((True, False)):
        index = at(other, 2)
        prepare(other, 2)
        pair = ([], [])
        for part, from_far, _, _ in items:
            for side, peer in enumerate((right, left)):
                pair[side].append(
                    copies.start(block_of(part, blocks, index, side), from_far.at[side, i], peer)
                )
        far.append(pair)
        yield
    near = []
    for i, other in enumerate((True, False)):
        pair = ([], [])
        for side, (step, peer) in enumerate(((1, right), (3, left))):
            index = at(other, step)
            prepare(other, step)
            arrived(far[i][side])
            for part, from_far, from_side, _ in items:
                add(block_of(part, blocks, index, side), [from_far.at[side, i]])
                pair[side].append(
                    copies.start(block_of(part, blocks, index), from_side.at[side, i], peer)
                )
        near.append(pair)
        yield
    prepare(True, 0)
    yield
    arrived(near[0][0])
    arrived(near[0][1])
    across = []
    for part, _, from_side, from_partner in items:
        view = block_of(part, blocks, group.partner)
        add(view, [from_side.at[0, 0], from_side.at[1, 0]])
        across.append(copies.start(view, from_partner, partner))
    yield
    prepare(False, 0)
    yield
    arrived(near[1][0])
    arrived(near[1][1])
    arrived(across)
    yield


def landing(rows, columns):
    return [
        pltpu.VMEM((2, 2, rows // 2, columns), BF16),
        pltpu.VMEM((2, 2, rows, columns), BF16),
        pltpu.VMEM((rows, columns), BF16),
    ]


def item_total(group, item):
    part, _, from_side, from_partner = item
    own = block_of(part, group.size, group.me)[...].astype(F32)
    sides = from_side[0, 1].astype(F32) + from_side[1, 1].astype(F32)
    return own + sides + from_partner[...].astype(F32)


def sem_scratch(remote, local):
    dma = pltpu.SemaphoreType.DMA
    return [dma((remote,)), dma((remote,)), dma((local,))]


def run(kernel, number, args, in_specs, out_shape, out_specs, scratch, seconds, flops=0):
    return pl.pallas_call(
        kernel,
        out_shape=out_shape,
        in_specs=in_specs,
        out_specs=out_specs,
        scratch_shapes=scratch,
        cost_estimate=pl.CostEstimate(
            flops=flops, bytes_accessed=int(seconds * 3.6e12), transcendentals=0
        ),
        compiler_params=pltpu.CompilerParams(
            collective_id=number, has_side_effects=True, vmem_limit_bytes=ROOM
        ),
    )(*args)


FAR = pl.BlockSpec(memory_space=pl.ANY)
NEAR = pl.BlockSpec(memory_space=pltpu.VMEM)


def shape(dims, kind=BF16):
    return jax.ShapeDtypeStruct(dims, kind)


def owner_parts(group, copies, sources, blocks_ref, from_sibling, local):
    order = [group.at(other, step) for step in (2, 1, 3, 0) for other in (True, False)]
    sibling = {"fsdp": group.sibling}
    turn = 1 - 2 * group.core
    waits = {}
    for number, index in enumerate(order):
        pairs = []
        for source, part, landed in zip(sources, blocks_ref, from_sibling):
            fetch = local.start(source(index), block_of(part, group.size, index))
            give = copies.start(source(index + turn), landed.at[number], sibling)
            pairs.append((fetch, give))
        waits[number] = pairs
    numbers = {(other, step): i for i, (step, other) in enumerate(
        (step, other) for step in (2, 1, 3, 0) for other in (True, False)
    )}

    def prepare(other, step):
        number = numbers[other, step]
        index = order[number]
        for (fetch, give), part, landed in zip(waits[number], blocks_ref, from_sibling):
            fetch.wait()
            give.wait_recv()
            view = block_of(part, group.size, index)
            view[...] = low(view[...].astype(F32) + landed[number].astype(F32))

    return prepare, [fetch for pairs in waits.values() for fetch, _ in pairs]


def tiles(product, rows, value, weight, tile, transposed):
    def step(i, carry):
        span = rows_at(i, tile)
        if transposed:
            piece = back_dot(value, weight[span, :])
        else:
            piece = dot(value, weight[:, span])
        product[rows, span] = piece.astype(product.dtype)
        return carry

    lax.fori_loop(0, product.shape[1] // tile, step, 0)


class Gathered:
    def __init__(self, group, copies, stores, block, landed, whole, use):
        self.group, self.stores, self.use = group, stores, use
        self.block, self.landed, self.whole = block, landed, whole
        self.stream = ring_gather(group, copies, [(block, landed)])
        self.ready, self.fresh = [], True

    def consume(self):
        for own, index in self.ready:
            src = self.block if own else block_of(self.landed, self.group.size, index)
            if self.whole is not None:
                self.stores.start(src, block_of(self.whole, self.group.size, index))
            self.use(src, index)
        self.ready = []

    def step(self):
        self.ready += [(self.fresh, index) for index in next(self.stream)]
        self.fresh = False

    def rest(self):
        self.consume()
        for indexes in self.stream:
            self.ready += [(False, i) for i in indexes]
            self.consume()


def gather_kernel(
    tile, transposed, block, weight_far, whole, product, landed, weight, sent, came, local
):
    group, copies, stores = Group("ctx"), Copies(sent, came), Stores(local)
    size = block.shape[0]
    fetch = stores.start(weight_far, weight)
    meet(group.peers())

    def use(src, index):
        tiles(product, rows_at(index, size), src[...], weight, tile, transposed)

    gathered = Gathered(group, copies, stores, block, landed, whole, use)
    gathered.step()
    fetch.wait()
    gathered.rest()
    copies.drain()
    stores.drain([fetch])


def gather_dot(block, weight, number, tile, transposed=False):
    ranks = lax.axis_size("ctx")
    size, depth = block.shape
    columns = weight.shape[0] if transposed else weight.shape[1]
    return run(
        functools.partial(gather_kernel, tile, transposed),
        number,
        [block, weight],
        [NEAR, FAR],
        [shape((ranks * size, depth)), shape((ranks * size, columns), F32)],
        [FAR, NEAR],
        [pltpu.VMEM((ranks * size, depth), BF16), pltpu.VMEM(weight.shape, BF16)]
        + sem_scratch(9, 9),
        40e-6,
        2 * ranks * size * depth * columns,
    )


def front_kernel(
    block,
    qkv_mine,
    gains_mine,
    whole,
    qkv_far,
    gains_out,
    proj,
    totals,
    landed,
    qkv,
    gains,
    sums,
    sums_landed,
    sent,
    came,
    local,
):
    group, owner = Group("ctx"), Group("fsdp")
    copies, stores = Copies(sent, came), Stores(local)
    ranks, owners, size = group.size, owner.size, block.shape[0]
    others = [{"ctx": lax.rem(group.me + step, ranks)} for step in range(1, ranks)]
    meet(others + owner.peers())
    normed = 2 * (proj.shape[1] // 3)
    lanes = lax.broadcasted_iota(jnp.int32, (8, normed), 1) < normed // 2
    firsts = lax.broadcasted_iota(jnp.int32, (8, normed), 0) < 4
    select = jnp.where(lanes == firsts, 1.0, 0.0)

    def use(src, index):
        rows = rows_at(index, size)
        tiles(proj, rows, src[...], qkv, 256, False)
        value = proj[rows, pl.ds(0, normed)]
        sums[:, rows] = lax.dot_general(
            select,
            value * value,
            (((1,), (1,)), ((), ())),
            precision=lax.Precision.HIGHEST,
            preferred_element_type=F32,
        )

    gathered = Gathered(group, copies, stores, block, landed, whole, use)
    items = [(qkv_mine, qkv), (gains_mine, gains)]
    weights = ring_gather(owner, copies, items)
    sibling = {"fsdp": owner.sibling}
    passed = []

    def pass_on(own=False):
        for index in next(weights):
            for mine, all_of_it in items:
                view = block_of(all_of_it, owners, index)
                passed.append(copies.start(mine if own else view, view, sibling))

    pass_on(True)
    gathered.step()
    for mine, all_of_it in items:
        block_of(all_of_it, owners, owner.me)[...] = mine[...]
    pass_on()
    pass_on()
    gathered.step()
    pass_on()
    pass_on()
    arrived(passed)
    stores.start(qkv, qkv_far)
    gains_out[...] = gains[...]
    gathered.rest()
    received = [copies.start(sums, sums_landed.at[i], peer) for i, peer in enumerate(others)]
    arrived(received)
    totals[...] = sums[...] + jnp.sum(sums_landed[...], axis=0)
    copies.drain()
    stores.drain()


def front(block, qkv_mine, gains_mine, number):
    ranks, owners = lax.axis_size("ctx"), lax.axis_size("fsdp")
    (size, depth), columns = block.shape, qkv_mine.shape[1]
    length = ranks * size
    gains_shape = (owners * gains_mine.shape[0], gains_mine.shape[1])
    return run(
        front_kernel,
        number,
        [block, qkv_mine, gains_mine],
        [NEAR] * 3,
        [
            shape((length, depth)),
            shape((depth, columns)),
            shape(gains_shape),
            shape((length, columns), F32),
            shape((8, length), F32),
        ],
        [FAR, FAR, NEAR, NEAR, NEAR],
        [
            pltpu.VMEM((length, depth), BF16),
            pltpu.VMEM((depth, columns), BF16),
            pltpu.VMEM(gains_shape, BF16),
            pltpu.VMEM((8, length), F32),
            pltpu.VMEM((ranks - 1, 8, length), F32),
        ]
        + sem_scratch(9 + 18 + 16 + ranks - 1, 9),
        45e-6,
        2 * length * depth * columns,
    )


class Summed:
    def __init__(self, group, copies, act, weight, parts, tile, transposed):
        size = act.shape[0] // group.size
        self.group, self.parts = group, parts

        def prepare(other, step):
            index = group.at(other, step)
            value = act[rows_at(index, size), :]
            part = parts[0]

            def one(i, carry):
                span = rows_at(i, tile)
                if transposed:
                    piece = back_dot(value, weight[span, :])
                else:
                    piece = dot(value, weight[:, span])
                part[rows_at(index, size), span] = low(piece)
                return carry

            lax.fori_loop(0, part.shape[1] // tile, one, 0)

        self.stream = ring_scatter(group, copies, [parts], prepare)

    def result(self):
        return item_total(self.group, self.parts)


def scatter_kernel(
    tile,
    transposed,
    act_far,
    weight_far,
    total,
    act,
    weight,
    part,
    from_far,
    from_side,
    from_partner,
    sent,
    came,
    local,
):
    group, copies, stores = Group("ctx"), Copies(sent, came), Stores(local)
    stores.start(act_far, act)
    stores.start(weight_far, weight)
    meet(group.peers())
    parts = (part, from_far, from_side, from_partner)
    summed = Summed(group, copies, act, weight, parts, tile, transposed)
    stores.drain()
    for _ in summed.stream:
        pass
    total[...] = summed.result()
    copies.drain()


def dot_scatter(act, weight, number, tile=512, transposed=False):
    ranks = lax.axis_size("ctx")
    size = act.shape[0] // ranks
    width = weight.shape[0] if transposed else weight.shape[1]
    return run(
        functools.partial(scatter_kernel, tile, transposed),
        number,
        [act, weight],
        [FAR, FAR],
        shape((size, width), F32),
        NEAR,
        [
            pltpu.VMEM(act.shape, BF16),
            pltpu.VMEM(weight.shape, BF16),
            pltpu.VMEM((ranks * size, width), BF16),
        ]
        + landing(size, width)
        + sem_scratch(9, 2),
        40e-6,
        2 * act.shape[0] * act.shape[1] * width,
    )


def strip_of(grad, width):
    def source(index):
        return grad.at[:, rows_at(index, width)]

    return source


def gather_sum_kernel(
    tile,
    block,
    weight_far,
    grad,
    whole,
    product,
    strip,
    landed,
    weight,
    part,
    from_sibling,
    from_far,
    from_side,
    from_partner,
    sent,
    came,
    local,
):
    group, owner = Group("ctx"), Group("fsdp")
    copies, stores = Copies(sent, came), Stores(local)
    size = block.shape[0]
    fetch = stores.start(weight_far, weight)
    meet(group.peers() + owner.peers())

    def use(src, index):
        tiles(product, rows_at(index, size), src[...], weight, tile, True)

    gathered = Gathered(group, copies, stores, block, landed, whole, use)
    gathered.step()
    prepare, fetched = owner_parts(
        owner, copies, [strip_of(grad, strip.shape[1])], [part], [from_sibling], stores
    )
    parts = (part, from_far, from_side, from_partner)
    summed = ring_scatter(owner, copies, [parts], prepare)
    next(summed)
    next(summed)
    fetch.wait()
    gathered.consume()
    gathered.step()
    next(summed)
    next(summed)
    gathered.consume()
    gathered.step()
    next(summed)
    next(summed)
    gathered.consume()
    for _ in summed:
        pass
    strip[...] = low(item_total(owner, parts))
    gathered.rest()
    copies.drain()
    stores.drain([fetch] + fetched)


def gather_dot_sum(block, weight, grad, number, tile):
    ranks, owners = lax.axis_size("ctx"), lax.axis_size("fsdp")
    size, depth = block.shape
    columns = weight.shape[0]
    tall, strip = grad.shape[0], grad.shape[1] // owners
    return run(
        functools.partial(gather_sum_kernel, tile),
        number,
        [block, weight, grad],
        [NEAR, FAR, FAR],
        [
            shape((ranks * size, depth)),
            shape((ranks * size, columns)),
            shape((tall, strip)),
        ],
        [FAR, NEAR, NEAR],
        [
            pltpu.VMEM((ranks * size, depth), BF16),
            pltpu.VMEM(weight.shape, BF16),
            pltpu.VMEM((owners * tall, strip), BF16),
            pltpu.VMEM((8, tall, strip), BF16),
        ]
        + landing(tall, strip)
        + sem_scratch(9 + 8 + 9, 9 + 8),
        45e-6,
        2 * ranks * size * depth * columns,
    )


def scatter_sum_kernel(tile, counts, *refs):
    refs = list(refs)

    def take(count):
        taken = refs[:count]
        del refs[:count]
        return taken

    number = sum(counts)
    act_far, weight_far = take(2)
    grads = take(number)
    (total,) = take(1)
    outs = take(number)
    act, weight, part = take(3)
    parts = (part, *take(3))
    owned = []
    for _ in range(number):
        owned.append(take(5))
    sent, came, local = refs
    group, owner = Group("ctx"), Group("fsdp")
    copies, stores = Copies(sent, came), Stores(local)
    fetches = [stores.start(act_far, act), stores.start(weight_far, weight)]
    meet(group.peers() + owner.peers())
    summed = Summed(group, copies, act, weight, parts, tile, True)
    sources = [
        rows_of(grad, out.shape[0]) if i < counts[0] else strip_of(grad, out.shape[1])
        for i, (grad, out) in enumerate(zip(grads, outs))
    ]
    prepare, fetched = owner_parts(
        owner, copies, sources, [own[0] for own in owned], [own[1] for own in owned], stores
    )
    items = [(own[0], own[2], own[3], own[4]) for own in owned]
    stream = ring_scatter(owner, copies, items, prepare)
    for fetch in fetches:
        fetch.wait()
    for _ in range(2):
        next(summed.stream)
        next(stream)
    for _ in range(6):
        next(stream)
        next(summed.stream)
    for out, item in zip(outs, items):
        out[...] = low(item_total(owner, item))
    total[...] = summed.result()
    copies.drain()
    stores.drain(fetches + fetched)


def rows_of(grad, height):
    def source(index):
        return grad.at[rows_at(index, height)]

    return source


def dot_scatter_sum(act, weight, by_rows, by_strips, number, tile=512):
    ranks, owners = lax.axis_size("ctx"), lax.axis_size("fsdp")
    size = act.shape[0] // ranks
    width = weight.shape[0]
    outs = [(grad.shape[0] // owners, grad.shape[1]) for grad in by_rows]
    outs += [(grad.shape[0], grad.shape[1] // owners) for grad in by_strips]
    scratch = [
        pltpu.VMEM(act.shape, BF16),
        pltpu.VMEM(weight.shape, BF16),
        pltpu.VMEM((ranks * size, width), BF16),
        *landing(size, width),
    ]
    for rows, columns in outs:
        scratch += [
            pltpu.VMEM((owners * rows, columns), BF16),
            pltpu.VMEM((owners // 2, rows, columns), BF16),
            *landing(rows, columns),
        ]
    count = len(outs)
    return run(
        functools.partial(scatter_sum_kernel, tile, (len(by_rows), len(by_strips))),
        number,
        [act, weight, *by_rows, *by_strips],
        [FAR] * (2 + count),
        [shape((size, width), F32)] + [shape(out) for out in outs],
        [NEAR] * (1 + count),
        scratch + sem_scratch(9 + 17 * count, 2 + 8 * count),
        48e-6,
        2 * act.shape[0] * act.shape[1] * width,
    )


def spread_kernel(count, *refs):
    mine, fars, wholes = refs[:count], refs[count : 2 * count], refs[2 * count : 3 * count]
    sent, came, local = refs[3 * count :]
    group, copies, stores = Group("ctx"), Copies(sent, came), Stores(local)
    meet(group.peers())
    own = True
    for indexes in ring_gather(group, copies, list(zip(mine, wholes))):
        for index in indexes:
            for block, whole, far in zip(mine, wholes, fars):
                src = block if own else block_of(whole, group.size, index)
                stores.start(src, block_of(far, group.size, index))
            own = False
    copies.drain()
    stores.drain()


def spread(parts, number):
    ranks, count = lax.axis_size("ctx"), len(parts)
    wholes = [(ranks * part.shape[0], part.shape[1]) for part in parts]
    return run(
        functools.partial(spread_kernel, count),
        number,
        parts,
        [NEAR] * count,
        [shape(dims) for dims in wholes],
        [FAR] * count,
        [pltpu.VMEM(dims, BF16) for dims in wholes] + sem_scratch(9 * count, 8 * count),
        35e-6,
    )


def head_lanes(shape):
    return lax.broadcasted_iota(jnp.int32, shape, 1) < HD


def turn_lanes(shape):
    return lax.rem(lax.broadcasted_iota(jnp.int32, shape, 1), HD) < HD // 2


def turned(values):
    lanes = values.shape[1]
    ahead = pltpu.roll(values, lanes - HD // 2, 1)
    behind = pltpu.roll(values, HD // 2, 1)
    return jnp.where(turn_lanes(values.shape), -ahead, behind)


def turned_back(values):
    lanes = values.shape[1]
    ahead = pltpu.roll(values, lanes - HD // 2, 1)
    behind = pltpu.roll(values, HD // 2, 1)
    return jnp.where(turn_lanes(values.shape), ahead, -behind)


def soft(keys, query, key_pos, query_pos):
    scores = back_dot(keys, query) * HD ** (-0.5)
    scores = jnp.where(query_pos >= key_pos, scores, NEG)
    expo = jnp.exp(scores - jnp.max(scores, axis=0, keepdims=True))
    return expo / jnp.sum(expo, axis=0, keepdims=True)


def mix_kernel(
    chunk,
    query_unit,
    key_unit,
    value_proj,
    query_gain,
    key_gain,
    cosine,
    sine,
    key_pos,
    query_pos,
    queries,
    keys,
    values,
    mixed,
):
    def front(unit, gain):
        scaled = unit[...] * gain[...]
        return low(scaled * cosine[...] + turned(scaled) * sine[...])

    queries[...] = front(query_unit, query_gain)
    keys[...] = front(key_unit, key_gain)
    values[...] = low(value_proj[...])
    value_turned = values[...].astype(F32).T.astype(BF16)

    def step(i, carry):
        rows = rows_at(i, chunk)
        query = queries[rows, :]
        first = head_lanes(query.shape)
        nothing = jnp.zeros_like(query)
        outs = []
        for mask in (first, jnp.logical_not(first)):
            probs = soft(
                keys[...], jnp.where(mask, query, nothing), key_pos[...], query_pos[:, rows]
            )
            outs.append(dot(value_turned, low(probs)))
        both = jnp.concatenate([outs[0][:HD], outs[1][HD:]], axis=0)
        mixed[rows, :] = low(both.T)
        return carry

    lax.fori_loop(0, queries.shape[0] // chunk, step, 0)


def mix(query_unit, key_unit, value_proj, query_gain, key_gain, cosine, sine, positions, chunk=256):
    length, share = query_unit.shape
    lanes = 2 * HD
    columns = pl.BlockSpec((length, lanes), lambda i: (0, i))
    fixed = lambda shape: pl.BlockSpec(shape, lambda i: (0, 0))
    gain = pl.BlockSpec((1, lanes), lambda i: (0, i))
    return pl.pallas_call(
        functools.partial(mix_kernel, chunk),
        grid=(share // lanes,),
        out_shape=[jax.ShapeDtypeStruct((length, share), BF16)] * 4,
        in_specs=[columns] * 3
        + [gain] * 2
        + [fixed((length, lanes))] * 2
        + [fixed((length, 1)), fixed((1, length))],
        out_specs=[columns] * 4,
        compiler_params=pltpu.CompilerParams(vmem_limit_bytes=ROOM),
    )(
        query_unit,
        key_unit,
        value_proj,
        query_gain[None],
        key_gain[None],
        cosine,
        sine,
        positions[:, None],
        positions[None, :],
    )


def mix_back_kernel(
    chunk,
    queries,
    keys,
    values,
    mixed_grad,
    query_unit,
    key_unit,
    query_inv,
    key_inv,
    query_gain,
    key_gain,
    cosine,
    sine,
    key_pos,
    query_pos,
    block,
    qkv_low,
    terms,
    whole,
    query_turn,
    key_turn,
    value_sum,
    sums,
    sums_landed,
    landed,
    sent,
    came,
    local,
):
    group, copies, stores = Group("ctx"), Copies(sent, came), Stores(local)
    length, share = queries.shape
    lanes = 2 * HD
    others = [{"ctx": lax.rem(group.me + step, group.size)} for step in range(1, group.size)]
    meet(others)
    stream = ring_gather(group, copies, [(block, landed)])
    next(stream)
    stores.start(block, block_of(whole, group.size, group.me))
    key_turn[...] = jnp.zeros_like(key_turn)
    value_sum[...] = jnp.zeros_like(value_sum)

    def advance():
        for index in next(stream):
            stores.start(
                block_of(landed, group.size, index), block_of(whole, group.size, index)
            )

    for pair in range(share // lanes):
        span = pl.ds(pair * lanes, lanes)
        key_turned = keys[:, span].astype(F32).T.astype(BF16)

        def step(i, carry):
            rows = rows_at(i, chunk)
            query, grad = queries[rows, span], mixed_grad[rows, span]
            first = head_lanes(query.shape)
            nothing = jnp.zeros_like(query)
            outs = []
            for mask in (first, jnp.logical_not(first)):
                query_head = jnp.where(mask, query, nothing)
                grad_head = jnp.where(mask, grad, nothing)
                probs = soft(keys[:, span], query_head, key_pos[...], query_pos[:, rows])
                prob_grad = back_dot(values[:, span], grad_head)
                delta = jnp.sum(probs * prob_grad, axis=0, keepdims=True)
                score_low = low(probs * (prob_grad - delta))
                value_sum[:, span] += dot(low(probs), grad_head)
                key_turn[:, span] += dot(score_low, query_head)
                outs.append(dot(key_turned, score_low))
            both = jnp.concatenate([outs[0][:HD], outs[1][HD:]], axis=0) * HD ** (-0.5)
            query_rot = both.T
            query_turn[rows, span] = query_rot * cosine[rows, :] + turned_back(
                query_rot * sine[rows, :]
            )
            return carry

        steps = length // chunk
        lax.fori_loop(0, steps // 2, step, 0)
        advance()
        lax.fori_loop(steps // 2, steps, step, 0)
        advance()
        key_rot = key_turn[:, span] * HD ** (-0.5)
        key_turn[:, span] = key_rot * cosine[...] + turned_back(key_rot * sine[...])
    for indexes in stream:
        for index in indexes:
            stores.start(
                block_of(landed, group.size, index), block_of(whole, group.size, index)
            )
    firsts = lax.broadcasted_iota(jnp.int32, (8, share), 0) < 4
    for i, (turn, unit, gain) in enumerate(
        ((query_turn, query_unit, query_gain), (key_turn, key_unit, key_gain))
    ):
        product = turn[...] * unit[...]
        terms[pl.ds(i, 1), :] = jnp.sum(product, axis=0, keepdims=True)
        part = lax.dot_general(
            jnp.where(firsts == (i == 0), 1.0, 0.0),
            product * gain[...],
            (((1,), (1,)), ((), ())),
            precision=lax.Precision.HIGHEST,
            preferred_element_type=F32,
        )
        if i == 0:
            sums[...] = part
        else:
            sums[...] += part
    arrived([copies.start(sums, sums_landed.at[i], peer) for i, peer in enumerate(others)])
    width = group.size * share
    means = ((sums[...] + jnp.sum(sums_landed[...], axis=0)) * (1.0 / width)).T
    for i, (turn, unit, gain, inv) in enumerate(
        (
            (query_turn, query_unit, query_gain, query_inv),
            (key_turn, key_unit, key_gain, key_inv),
        )
    ):
        mean = means[:, 4 * i : 4 * i + 1]
        qkv_low[:, pl.ds(i * share, share)] = low(
            inv[...] * (turn[...] * gain[...] - unit[...] * mean)
        )
    qkv_low[:, pl.ds(2 * share, share)] = low(value_sum[...])
    copies.drain()
    stores.drain()


def mix_back(tensors, units, inverses, gains, cosine, sine, positions, block, number, chunk=256):
    length, share = tensors[0].shape
    ranks = lax.axis_size("ctx")
    near = [NEAR] * 15
    whole = (ranks * block.shape[0], block.shape[1])
    return run(
        functools.partial(mix_back_kernel, chunk),
        number,
        [
            *tensors,
            *units,
            *[inverse[:, None] for inverse in inverses],
            *[gain[None] for gain in gains],
            cosine,
            sine,
            positions[:, None],
            positions[None, :],
            block,
        ],
        near,
        [shape((length, 3 * share)), shape((2, share), F32), shape(whole)],
        [NEAR, NEAR, FAR],
        [
            pltpu.VMEM((length, share), F32),
            pltpu.VMEM((length, share), F32),
            pltpu.VMEM((length, share), F32),
            pltpu.VMEM((8, length), F32),
            pltpu.VMEM((ranks - 1, 8, length), F32),
            pltpu.VMEM(whole, BF16),
        ]
        + sem_scratch(9 + ranks - 1, 8),
        40e-6,
    )


def body(
    layer_input,
    cotangent,
    query_weight,
    key_weight,
    value_weight,
    out_weight,
    gate_weight,
    up_weight,
    down_weight,
    query_gain,
    key_gain,
    attention_gain,
    feed_gain,
    pair_table,
):
    row_count = layer_input.shape[1]
    block_len = row_count // 2
    rank = lax.axis_index("ctx")
    owner = lax.axis_index("fsdp")
    ranks = lax.axis_size("ctx")
    owners = lax.axis_size("fsdp")
    width = query_weight.shape[1]
    share = width // ranks
    strip = width // owners
    units = gate_weight.shape[1] // ranks
    room = -(-units // 256) * 256
    blocks = pair_table.reshape(-1)
    positions = (
        blocks[:, None] * block_len + jnp.arange(block_len, dtype=jnp.int32)[None, :]
    ).reshape(-1)
    cosine, sine = angles(positions)

    def cut(weight, size):
        return lax.dynamic_slice_in_dim(weight, rank * size, size, axis=1)

    def wide(weight):
        return jnp.pad(cut(weight, units), ((0, 0), (0, room - units)))

    inputs = layer_input[0]
    qkv_mine = jnp.concatenate(
        [cut(w, share) for w in (query_weight, key_weight, value_weight)], axis=1
    )
    gains_mine = jnp.pad(
        jnp.stack([query_gain, key_gain, attention_gain, feed_gain]), ((0, 28), (0, 0))
    )
    seq_inputs, qkv, all_gains, proj, squares = front(inputs, qkv_mine, gains_mine, 1)
    gains = all_gains.reshape(owners, -1, strip)[:, :4].transpose(1, 0, 2).reshape(4, -1).astype(F32)
    query_scale = lax.dynamic_slice_in_dim(gains[0], rank * share, share)
    key_scale = lax.dynamic_slice_in_dim(gains[1], rank * share, share)
    attn_scale, feed_scale = gains[2], gains[3]
    out_weight, down_weight, gate_weight, up_weight, squares = lax.optimization_barrier(
        (out_weight, down_weight, gate_weight, up_weight, squares)
    )
    flat = lambda c, f: c * owners + f
    odd = lax.rem(owner, 2)
    routes = [
        [
            (flat(c, 2 * d + j), flat(d, 2 * c + (j ^ k)))
            for c in range(ranks)
            for d in range(ranks)
            for j in range(2)
        ]
        for k in range(2)
    ]
    axes = ("ctx", "fsdp")
    tall = jnp.concatenate([out_weight, down_weight], axis=0)
    pieces = []
    for k, route in enumerate(routes):
        target = 2 * rank + (odd ^ k)
        strips = lax.dynamic_slice_in_dim(tall, target * strip, strip, axis=1)
        pieces.append(lax.ppermute(strips, axes, route))

    def in_order(pair):
        return jnp.where(odd == 0, pair[0], pair[1]), jnp.where(odd == 0, pair[1], pair[0])

    low_piece, high_piece = in_order(pieces)
    out_size = out_weight.shape[0]
    strips = jnp.concatenate(
        [
            low_piece[:out_size],
            high_piece[:out_size],
            low_piece[out_size:],
            high_piece[out_size:],
            jnp.zeros((room - units, strip), BF16),
        ],
        axis=0,
    )

    out_down = lax.all_gather(strips, "fsdp", axis=1, tiled=True)
    out_rows, down_rows = out_down[:share], out_down[share:]
    gate_up = lax.all_gather(
        jnp.concatenate([wide(gate_weight), wide(up_weight)], axis=1), "fsdp", axis=0, tiled=True
    )

    query_proj, key_proj, value_proj = (
        proj[:, :share],
        proj[:, share : 2 * share],
        proj[:, 2 * share :],
    )
    inverse = lax.rsqrt(jnp.stack([squares[0], squares[4]]) / width + EPSILON)
    query_inv, key_inv = inverse[0][:, None], inverse[1][:, None]
    query_unit, key_unit = query_proj * query_inv, key_proj * key_inv
    queries, keys, values, mixed = mix(
        query_unit, key_unit, value_proj, query_scale, key_scale, cosine, sine, positions
    )
    attn_raw = dot_scatter(mixed, out_rows, 3)
    hidden = inputs.astype(F32) + rms_scale(attn_raw, attn_scale)
    seq_hidden, pre = gather_dot(low(hidden), gate_up, 4, tile=512)
    gate_pre, up_pre = pre[:, :room], pre[:, room:]
    sigmoid = jax.nn.sigmoid(gate_pre)
    product = low(gate_pre * sigmoid * up_pre)
    down_pre = dot_scatter(product, down_rows, 5)
    result = hidden + rms_scale(down_pre, feed_scale)
    upstream = cotangent[0].astype(F32)
    _, pull_feed = jax.vjp(rms_scale, down_pre, feed_scale)
    down_grad, feed_term = pull_feed(upstream)
    seq_down, product_grad = gather_dot(low(down_grad), down_rows, 6, tile=256, transposed=True)
    gate_low = low(product_grad * up_pre * sigmoid * (1.0 + gate_pre * (1.0 - sigmoid)))
    up_low = low(product_grad * gate_pre * sigmoid)
    both_low = jnp.concatenate([gate_low, up_low], axis=1)
    gate_up_grad = low(outer_sum(seq_hidden, both_low))
    hidden_sum, gate_up_share = dot_scatter_sum(both_low, gate_up, [gate_up_grad], [], 7)
    hidden_grad = upstream + hidden_sum
    down_rows_grad = low(outer_sum(product, seq_down))
    _, pull_attn = jax.vjp(rms_scale, attn_raw, attn_scale)
    attn_grad, attn_term = pull_attn(hidden_grad)
    seq_attn, mixed_grad, down_share = gather_dot_sum(
        low(attn_grad), out_rows, down_rows_grad, 8, 256
    )
    out_rows_grad = low(outer_sum(mixed, seq_attn))
    qkv_low, terms, gate_up_all = mix_back(
        (queries, keys, values, mixed_grad),
        (query_unit, key_unit),
        inverse,
        (query_scale, key_scale),
        cosine,
        sine,
        positions,
        gate_up_share,
        9,
    )
    qkv_grad = low(outer_sum(seq_inputs, qkv_low))

    def placed(term):
        return lax.dynamic_update_slice_in_dim(
            jnp.zeros((width,), F32), term, rank * share, axis=0
        )

    gain_terms = low(jnp.stack([placed(terms[0]), placed(terms[1]), attn_term, feed_term]))
    strip_grads = jnp.concatenate([out_rows_grad, jnp.pad(gain_terms, ((0, 28), (0, 0)))], axis=0)
    input_sum, qkv_share, out_share = dot_scatter_sum(
        qkv_low, qkv, [qkv_grad], [strip_grads], 10
    )
    input_grad = hidden_grad + input_sum
    gains_share = out_share[share:]
    down_size = down_weight.shape[0]
    by_owner = [
        jnp.concatenate(
            [
                out_share[j * out_size : (j + 1) * out_size],
                down_share[j * down_size : (j + 1) * down_size],
            ],
            axis=0,
        )
        for j in range(2)
    ]
    by_route = in_order(by_owner)
    returned = [
        lax.ppermute(piece, axes, [(b, a) for a, b in route])
        for piece, route in zip(by_route, routes)
    ]
    tall_share = jnp.concatenate(in_order(returned), axis=1)

    qkv_all, tall_all, gains_all = spread([qkv_share, tall_share, gains_share], 11)

    def side_by_side(parts, size, at):
        columns = parts.reshape(ranks, -1, parts.shape[-1])[:, :, at : at + size]
        return columns.transpose(1, 0, 2).reshape(columns.shape[1], -1).astype(F32)

    gate_share, up_share = (side_by_side(gate_up_all, units, at) for at in (0, room))
    query_share, key_share, value_share = (
        side_by_side(qkv_all, share, i * share) for i in range(3)
    )
    tall_whole = side_by_side(tall_all, share, 0)
    out_share, down_share = tall_whole[:out_size], tall_whole[out_size:]

    mine = jnp.sum(gains_all.reshape(ranks, -1, strip)[:, :4].astype(F32), axis=0)
    return (
        low(result)[None],
        input_grad[None],
        query_share,
        key_share,
        value_share,
        out_share,
        gate_share,
        up_share,
        down_share,
        mine[0],
        mine[1],
        mine[2],
        mine[3],
    )


def solution(mesh):
    weights = (P("fsdp", None),) * 7
    gains = (P("fsdp"),) * 4
    tokens = P("fsdp", "ctx", None)
    in_specs = (tokens, tokens, *weights, *gains, P())
    out_specs = (tokens, tokens, *weights, *gains)
    return jax.shard_map(body, mesh=mesh, in_specs=in_specs, out_specs=out_specs, check_vma=False)
```

```python
import types

import jax
import jax.numpy as jnp
from jax import lax
from jax.experimental import pallas as pl
from jax.experimental.pallas import tpu as pltpu
from jax.sharding import PartitionSpec as P

HD = 64
EPSILON = 1e-06
THETA = 500000.0
MESH = pl.DeviceIdType.MESH
F32 = jnp.float32
BF16 = jnp.bfloat16
ROOM = 56 * 2**20
NEG = -1e30


def angles(positions):
    freqs = THETA ** (-jnp.arange(0, HD, 2, dtype=F32) / HD)
    phase = positions.astype(F32)[:, None] * jnp.tile(freqs, 4)[None, :]
    return jnp.cos(phase), jnp.sin(phase)


def dot(left, right):
    return jnp.dot(left, right, preferred_element_type=F32)


def outer_sum(left, right):
    return lax.dot_general(left, right, (((0,), (0,)), ((), ())), preferred_element_type=F32)


def back_dot(grad, weight):
    return lax.dot_general(grad, weight, (((1,), (1,)), ((), ())), preferred_element_type=F32)


def low(values):
    return values.astype(BF16)


class Group:
    def __init__(self, axis):
        me = lax.axis_index(axis)
        self.axis = axis
        self.size = lax.axis_size(axis)
        self.me = me
        if axis == "ctx":
            self.core, self.pair, self.place = 0, me // 4, lax.rem(me, 4)
        else:
            self.core, self.pair, self.place = lax.rem(me, 2), lax.rem(me, 4) // 2, me // 4
        self.sibling = me + 1 - 2 * self.core if axis == "fsdp" else None
        self.right, self.left, self.partner = self.at(False, 1), self.at(False, 3), self.at(True, 0)

    def at(self, other, step):
        pair = 1 - self.pair if other else self.pair
        place = lax.rem(self.place + step, 4)
        if self.axis == "ctx":
            return pair * 4 + place
        return place * 4 + pair * 2 + self.core

    def peers(self):
        near = [self.right, self.left, self.partner]
        if self.sibling is not None:
            near.append(self.sibling)
        return [{self.axis: peer} for peer in near]


def meet(peers):
    barrier = pltpu.get_barrier_semaphore()
    for peer in peers:
        pl.semaphore_signal(barrier, inc=1, device_id=peer, device_id_type=MESH)
    pl.semaphore_wait(barrier, len(peers))


class Copies:
    def __init__(self, sent, came):
        self.sent, self.came, self.count, self.all = sent, came, 0, []

    def start(self, src, dst, peer):
        copy = pltpu.make_async_remote_copy(
            src_ref=src,
            dst_ref=dst,
            send_sem=self.sent.at[self.count],
            recv_sem=self.came.at[self.count],
            device_id=peer,
            device_id_type=MESH,
        )
        self.count += 1
        self.all.append(copy)
        copy.start()
        return copy

    def drain(self):
        for copy in self.all:
            copy.wait_send()


class Once:
    def __init__(self, copy):
        self.copy, self.waited = copy, False

    def wait(self):
        if not self.waited:
            self.copy.wait()
        self.waited = True


class Stores:
    def __init__(self, sems):
        self.sems, self.count, self.all = sems, 0, []

    def start(self, src, dst):
        copy = pltpu.make_async_copy(src, dst, self.sems.at[self.count])
        self.count += 1
        copy.start()
        copy = Once(copy)
        self.all.append(copy)
        return copy

    def drain(self):
        for copy in self.all:
            copy.wait()
        self.all = []


def rows_at(index, size):
    return pl.ds(pl.multiple_of(index * size, size), size)


class Rows:
    def __init__(self, ref, blocks):
        self.ref, self.rows = ref, ref.shape[0] // blocks

    def block(self, index, low_row=0, high_row=None):
        high_row = self.rows if high_row is None else high_row
        start = pl.multiple_of(index * self.rows + low_row, 16)
        return self.ref.at[pl.ds(start, high_row - low_row)]


class Strips:
    def __init__(self, ref, blocks):
        self.ref, self.rows, self.width = ref, ref.shape[0], ref.shape[1] // blocks

    def block(self, index, low_row=0, high_row=None):
        high_row = self.rows if high_row is None else high_row
        return self.ref.at[pl.ds(low_row, high_row - low_row), rows_at(index, self.width)]


def arrived(copies):
    for copy in copies:
        copy.wait_recv()


class Cuts:
    def __init__(self, rows, edged):
        half = rows // 2
        start = rows // 8 // 16 * 16 if edged else 0
        stop = rows - rows // 4 // 16 * 16 if edged else rows
        self.all, self.first, self.second = [(0, rows)], [(0, half)], [(half, rows)]
        self.middle = [(start, stop)]
        self.middle_first, self.middle_second = [(start, half)], [(half, stop)]
        self.top = [(0, start)] if start else []
        self.bottom = [(stop, rows)] if stop < rows else []
        self.edges = self.top + self.bottom
        self.half = half


def ring_gather(group, copies, items, edged=False):
    at = group.at
    right, left, partner = ({group.axis: peer} for peer in (group.right, group.left, group.partner))

    def move(index, part, peer, own=False):
        started = []
        for mine, whole in items:
            for lo, hi in getattr(Cuts(whole.rows, edged), part):
                view = whole.block(index, lo, hi)
                started.append(copies.start(mine if own else view, view, peer))
        return started

    near_left = move(group.me, "all", right, True)
    near_right = move(group.me, "all", left, True)
    across = move(group.me, "all", partner, True)
    yield [group.me]
    arrived(near_left)
    far_left = move(group.left, "first", right)
    edges = move(group.left, "edges", partner)
    arrived(near_right)
    far_right = move(group.right, "second", left)
    edges += move(group.right, "edges", partner)
    arrived(across)
    other_left = move(group.partner, "middle", right)
    other_right = move(group.partner, "middle", left)
    yield [group.left, group.right, group.partner]
    arrived(far_left)
    last = move(at(False, 2), "top", partner)
    arrived(far_right)
    last += move(at(False, 2), "bottom", partner)
    yield [at(False, 2)]
    arrived(other_left)
    last += move(at(True, 3), "middle_first", right)
    arrived(other_right)
    last += move(at(True, 1), "middle_second", left)
    arrived(edges)
    yield [at(True, 3), at(True, 1)]
    arrived(last)
    yield [at(True, 2)]


def add(ref, others):
    value = ref[...].astype(F32)
    for other in others:
        value += other[...].astype(F32)
    ref[...] = low(value)


class Sum:
    def __init__(self, parts, far, side, cross, out=None):
        self.parts, self.far, self.side, self.cross, self.out = parts, far, side, cross, out

    def total(self, group):
        own = self.parts.block(group.me)[...].astype(F32)
        sides = self.side[0, 1].astype(F32) + self.side[1, 1].astype(F32)
        return own + sides + self.cross[0].astype(F32)


def landing(rows, columns, edged=False):
    return [
        pltpu.VMEM((2, 2, rows // 2, columns), BF16),
        pltpu.VMEM((2, 2, rows, columns), BF16),
        pltpu.VMEM((4 if edged else 1, rows, columns), BF16),
    ]


def ring_scatter(group, copies, items, prepare, edged=False):
    at = group.at
    right, left, partner = ({group.axis: peer} for peer in (group.right, group.left, group.partner))
    cuts = [Cuts(item.parts.rows, edged) for item in items]

    def window(ref, lead, lo, hi):
        return ref.at[(*lead, pl.ds(lo, hi - lo))]

    def send_edges(step):
        started = []
        for item, cut in zip(items, cuts):
            for lo, hi in cut.edges:
                view = item.parts.block(at(True, step), lo, hi)
                started.append(copies.start(view, window(item.cross, (step,), lo, hi), partner))
        return started

    def add_edges(step):
        for item, cut in zip(items, cuts):
            for lo, hi in cut.edges:
                add(item.parts.block(at(False, step), lo, hi), [window(item.cross, (step,), lo, hi)])

    def far_cut(cut, i, side):
        if side == 0:
            return (cut.middle_first if i == 0 else cut.first)[0]
        return (cut.middle_second if i == 0 else cut.second)[0]

    def far_window(item, cut, i, side):
        lo, hi = far_cut(cut, i, side)
        base = side * cut.half
        return window(item.far, (side, i), lo - base, hi - base)

    def send_far(i):
        started = ([], [])
        for item, cut in zip(items, cuts):
            for side, peer in enumerate((right, left)):
                view = item.parts.block(at(i == 0, 2), *far_cut(cut, i, side))
                started[side].append(copies.start(view, far_window(item, cut, i, side), peer))
        return started

    def send_near(i, far):
        started = []
        for side, (step, peer) in enumerate(((1, right), (3, left))):
            arrived(far[side])
            index = at(i == 0, step)
            for item, cut in zip(items, cuts):
                add(
                    item.parts.block(index, *far_cut(cut, i, side)),
                    [far_window(item, cut, i, side)],
                )
                lo, hi = (cut.middle if i == 0 else cut.all)[0]
                view = item.parts.block(index, lo, hi)
                started.append(copies.start(view, window(item.side, (side, i), lo, hi), peer))
        return started

    prepare(True, 2)
    far_other = send_far(0)
    edges = {2: send_edges(2)}
    yield
    prepare(False, 2)
    arrived(edges[2])
    add_edges(2)
    far_same = send_far(1)
    yield
    for step in (1, 3):
        prepare(True, step)
        edges[step] = send_edges(step)
    yield
    near_other = send_near(0, far_other)
    yield
    prepare(True, 0)
    edges[0] = send_edges(0)
    for step in (1, 3):
        prepare(False, step)
        arrived(edges[step])
        add_edges(step)
    near_same = send_near(1, far_same)
    yield
    arrived(near_other)
    across = []
    for item, cut in zip(items, cuts):
        lo, hi = cut.middle[0]
        view = item.parts.block(group.partner, lo, hi)
        add(view, [window(item.side, (0, 0), lo, hi), window(item.side, (1, 0), lo, hi)])
        across.append(copies.start(view, window(item.cross, (0,), lo, hi), partner))
    yield
    prepare(False, 0)
    yield
    arrived(near_same)
    arrived(across)
    arrived(edges[0])
    yield


def owner_gather(owner, copies, stores, items):
    sibling = {owner.axis: owner.sibling}
    passed, own = [], True
    for mine, whole in items:
        stores.start(mine, whole.block(owner.me))
    for indexes in ring_gather(owner, copies, items):
        for index in indexes:
            for mine, whole in items:
                view = whole.block(index)
                passed.append(copies.start(mine if own else view, view, sibling))
        own = False
        yield
    arrived(passed)
    yield


def owner_sum(owner, copies, stores, sources, sums, from_sibling):
    sibling = {owner.axis: owner.sibling}
    turn = 1 - 2 * owner.core
    waits = {}
    for step in (2, 1, 3, 0):
        for other in (True, False):
            index, number = owner.at(other, step), len(waits)
            waits[other, step] = [
                (
                    stores.start(source.block(index), item.parts.block(index)),
                    copies.start(source.block(index + turn), landed.at[number], sibling),
                    landed.at[number],
                )
                for source, item, landed in zip(sources, sums, from_sibling)
            ]

    def prepare(other, step):
        for (fetch, give, landed), item in zip(waits[other, step], sums):
            fetch.wait()
            give.wait_recv()
            add(item.parts.block(owner.at(other, step)), [landed])

    yield from ring_scatter(owner, copies, sums, prepare)
    for item in sums:
        item.out[...] = low(item.total(owner))
    yield


def sum_scratch(rows, columns, owners):
    return [
        pltpu.VMEM((owners * rows, columns), BF16),
        pltpu.VMEM((owners // 2, rows, columns), BF16),
        *landing(rows, columns),
    ]


FAR = pl.BlockSpec(memory_space=pl.ANY)
NEAR = pl.BlockSpec(memory_space=pltpu.VMEM)


def shape(dims, kind=BF16):
    return jax.ShapeDtypeStruct(dims, kind)


def launch(number, body, ins, outs, temps, remote, local):
    names, scratch, groups = [*ins, *outs], [], []
    for name, kind in temps.items():
        kinds = kind if isinstance(kind, list) else [kind]
        groups.append((name, len(kinds), isinstance(kind, list)))
        scratch += kinds
    dma = pltpu.SemaphoreType.DMA
    scratch += [dma((remote,)), dma((remote,)), dma((local,))]

    def kernel(*refs):
        named = dict(zip(names, refs))
        rest = list(refs[len(names) :])
        for name, count, many in groups:
            named[name] = rest[:count] if many else rest[0]
            del rest[:count]
        sent, came, near = rest
        body(types.SimpleNamespace(**named), Copies(sent, came), Stores(near))

    results = pl.pallas_call(
        kernel,
        out_shape=[out for out, _ in outs.values()],
        in_specs=[spec for _, spec in ins.values()],
        out_specs=[spec for _, spec in outs.values()],
        scratch_shapes=scratch,
        compiler_params=pltpu.CompilerParams(
            collective_id=number, has_side_effects=True, vmem_limit_bytes=ROOM
        ),
    )(*[array for array, _ in ins.values()])
    return types.SimpleNamespace(**dict(zip(outs, results)))


def near(**arrays):
    return {name: (array, NEAR) for name, array in arrays.items()}


def far(**arrays):
    return {name: (array, FAR) for name, array in arrays.items()}


def tiles(product, rows, value, weight, tile, transposed):
    def step(i, carry):
        span = rows_at(i, tile)
        if transposed:
            piece = back_dot(value, weight[span, :])
        else:
            piece = dot(value, weight[:, span])
        product[rows, span] = piece.astype(product.dtype)
        return carry

    lax.fori_loop(0, product.shape[1] // tile, step, 0)


def totals_by_row(select, value):
    return lax.dot_general(
        select,
        value,
        (((1,), (1,)), ((), ())),
        precision=lax.Precision.HIGHEST,
        preferred_element_type=F32,
    )


class Gathered:
    def __init__(self, group, copies, stores, block, landed, whole, use):
        self.group, self.stores, self.use = group, stores, use
        self.block, self.landed = block, Rows(landed, group.size)
        self.whole = Rows(whole, group.size)
        self.stream = ring_gather(group, copies, [(block, self.landed)], True)
        self.ready, self.fresh = [], True

    def step(self):
        self.ready += [(self.fresh, index) for index in next(self.stream)]
        self.fresh = False

    def consume(self):
        for own, index in self.ready:
            src = self.block if own else self.landed.block(index)
            self.stores.start(src, self.whole.block(index))
            self.use(src, index)
        self.ready = []


def gathered_all(gathered, pump):
    gathered.consume()
    for _ in range(4):
        pump()
        gathered.step()
        gathered.consume()


def ctx_sum(group, copies, act, weight, item, tile, transposed):
    parts = item.parts

    def prepare(other, step):
        rows = rows_at(group.at(other, step), parts.rows)
        tiles(parts.ref, rows, act[rows, :], weight, tile, transposed)

    return ring_scatter(group, copies, [item], prepare, True)


def weave(main, stream):
    for _ in main:
        if stream is not None:
            next(stream, None)


def finish(stream):
    for _ in stream:
        pass


def norm(values):
    inverse = lax.rsqrt(jnp.mean(values * values, axis=-1, keepdims=True) + EPSILON)
    return values * inverse, inverse


def norm_back(grad, unit, inverse, gain):
    pull = grad * gain
    return inverse * (pull - unit * jnp.mean(pull * unit, axis=-1, keepdims=True))


def head_lanes(shape):
    return lax.broadcasted_iota(jnp.int32, shape, 1) < HD


def turn_lanes(shape):
    return lax.rem(lax.broadcasted_iota(jnp.int32, shape, 1), HD) < HD // 2


def turned(values):
    lanes = values.shape[1]
    ahead = pltpu.roll(values, lanes - HD // 2, 1)
    behind = pltpu.roll(values, HD // 2, 1)
    return jnp.where(turn_lanes(values.shape), -ahead, behind)


def turned_back(values):
    lanes = values.shape[1]
    ahead = pltpu.roll(values, lanes - HD // 2, 1)
    behind = pltpu.roll(values, HD // 2, 1)
    return jnp.where(turn_lanes(values.shape), ahead, -behind)


def soft(keys, query, key_pos, query_pos):
    scores = back_dot(keys, query) * HD ** (-0.5)
    scores = jnp.where(query_pos >= key_pos, scores, NEG)
    expo = jnp.exp(scores - jnp.max(scores, axis=0, keepdims=True))
    return expo / jnp.sum(expo, axis=0, keepdims=True)


def heads_of(query):
    first = head_lanes(query.shape)
    return first, jnp.logical_not(first)


def pair_of(outs):
    return jnp.concatenate([outs[0][:HD], outs[1][HD:]], axis=0)


def attend(block, qkv_mine, gains_mine, out_mine, gate_up_mine, cosine, sine, positions, number):
    ranks, owners = lax.axis_size("ctx"), lax.axis_size("fsdp")
    (size, depth), columns = block.shape, qkv_mine.shape[1]
    length, share, chunk = ranks * size, columns // 3, 256
    lanes = 2 * HD

    def body(r, copies, stores):
        group, owner = Group("ctx"), Group("fsdp")
        others = [{"ctx": lax.rem(group.me + step, ranks)} for step in range(1, ranks)]
        meet(others + owner.peers())
        normed = 2 * share
        by_lane = lax.broadcasted_iota(jnp.int32, (8, normed), 1) < share
        by_row = lax.broadcasted_iota(jnp.int32, (8, normed), 0) < 4
        select = jnp.where(by_lane == by_row, 1.0, 0.0)

        def use(src, index):
            rows = rows_at(index, size)
            tiles(r.proj, rows, src[...], r.qkv_near, 256, False)
            value = r.proj[rows, pl.ds(0, normed)]
            r.sums[:, rows] = totals_by_row(select, value * value)

        gathered = Gathered(group, copies, stores, r.block, r.landed, r.whole, use)
        gains_all = Rows(r.gains_near, owners)
        first = owner_gather(
            owner,
            copies,
            stores,
            [(r.qkv_mine, Rows(r.qkv_near, owners)), (r.gains_mine, gains_all)],
        )
        second = owner_gather(
            owner,
            copies,
            stores,
            [
                (r.out_mine, Strips(r.out_near, owners)),
                (r.gate_up_mine, Rows(r.gate_up_near, owners)),
            ],
        )
        next(first)
        gathered.step()
        next(first)
        next(first)
        next(first)
        next(second)
        gathered.step()
        finish(first)
        stores.drain()
        stores.start(r.qkv_near, r.qkv)
        gathered.consume()
        for _ in range(3):
            next(second)
            gathered.step()
            gathered.consume()
        exchange = [copies.start(r.sums, r.sums_landed.at[i], to) for i, to in enumerate(others)]
        for i in range(owners):
            rows = r.gains_near[pl.ds(i * gains_all.rows, 16), :].astype(F32)
            r.scales[:, pl.ds(i * rows.shape[1], rows.shape[1])] = rows[:8]
        arrived(exchange)
        totals = r.sums[...] + jnp.sum(r.sums_landed[...], axis=0)
        r.inverse[...] = lax.rsqrt(totals * (1.0 / (ranks * share)) + EPSILON).T
        mine = rows_at(group.me, share)
        for i, (unit, out) in enumerate(((r.query_unit, r.queries), (r.key_unit, r.keys))):
            span = pl.ds(i * share, share)
            unit[...] = r.proj[:, span] * r.inverse[:, 4 * i : 4 * i + 1]
            gain = r.scales[i : i + 1, mine]
            for pair in range(share // lanes):
                part = pl.ds(pair * lanes, lanes)
                scaled = unit[:, part] * gain[:, pair * lanes : (pair + 1) * lanes]
                out[:, part] = low(scaled * r.cosine[...] + turned(scaled) * r.sine[...])
        r.values[...] = low(r.proj[:, pl.ds(2 * share, share)])

        for pair in range(share // lanes):
            span = pl.ds(pair * lanes, lanes)
            value_turned = r.values[:, span].astype(F32).T.astype(BF16)

            def step(i, carry):
                rows = rows_at(i, chunk)
                query = r.queries[rows, span]
                nothing = jnp.zeros_like(query)
                outs = []
                for mask in heads_of(query):
                    query_head = jnp.where(mask, query, nothing)
                    probs = soft(r.keys[:, span], query_head, r.key_pos[...], r.query_pos[:, rows])
                    outs.append(dot(value_turned, low(probs)))
                r.mixed[rows, span] = low(pair_of(outs).T)
                return carry

            steps = length // chunk
            lax.fori_loop(0, steps // 2, step, 0)
            next(second, None)
            lax.fori_loop(steps // 2, steps, step, 0)
            next(second, None)
        finish(second)
        stores.drain()
        stores.start(r.out_near, r.out_rows)
        stores.start(r.gate_up_near, r.gate_up)
        stores.drain()
        copies.drain()

    return launch(
        number,
        body,
        near(
            block=block,
            qkv_mine=qkv_mine,
            gains_mine=gains_mine,
            out_mine=out_mine,
            gate_up_mine=gate_up_mine,
            cosine=cosine,
            sine=sine,
            key_pos=positions[:, None],
            query_pos=positions[None, :],
        ),
        far(
            whole=shape((length, depth)),
            qkv=shape((depth, columns)),
            out_rows=shape((share, depth)),
            gate_up=shape((depth, gate_up_mine.shape[1])),
        )
        | near(
            scales=shape((8, depth), F32),
            inverse=shape((length, 8), F32),
            query_unit=shape((length, share), F32),
            key_unit=shape((length, share), F32),
            queries=shape((length, share)),
            keys=shape((length, share)),
            values=shape((length, share)),
            mixed=shape((length, share)),
        ),
        dict(
            landed=pltpu.VMEM((length, depth), BF16),
            qkv_near=pltpu.VMEM((depth, columns), BF16),
            gains_near=pltpu.VMEM((owners * gains_mine.shape[0], gains_mine.shape[1]), BF16),
            out_near=pltpu.VMEM((share, depth), BF16),
            gate_up_near=pltpu.VMEM((depth, gate_up_mine.shape[1]), BF16),
            proj=pltpu.VMEM((length, columns), F32),
            sums=pltpu.VMEM((8, length), F32),
            sums_landed=pltpu.VMEM((ranks - 1, 8, length), F32),
        ),
        15 + 34 + 34 + ranks - 1,
        20,
    )


def feed_in(mixed, out_rows, block, scales, gate_up, down_mine, number):
    ranks, owners = lax.axis_size("ctx"), lax.axis_size("fsdp")
    size, width = block.shape
    length, both = mixed.shape[0], gate_up.shape[1]
    room = both // 2

    def body(r, copies, stores):
        group, owner = Group("ctx"), Group("fsdp")
        fetches = [
            stores.start(r.mixed, r.act),
            stores.start(r.out_rows, r.out_near),
            stores.start(r.gate_up, r.gate_up_near),
        ]
        meet(group.peers() + owner.peers())
        item = Sum(Rows(r.part, ranks), *r.landings)
        fetches[0].wait()
        fetches[1].wait()
        summed = ctx_sum(group, copies, r.act, r.out_near, item, 512, False)
        down = owner_gather(
            owner, copies, stores, [(r.down_mine, Strips(r.down_near, owners))]
        )
        next(summed)
        weave(summed, down)
        attn_raw = item.total(group)
        r.attn_raw[...] = attn_raw
        unit, _ = norm(attn_raw)
        hidden = r.block[...].astype(F32) + unit * r.scales[2:3, :]
        r.hidden[...] = hidden
        r.hidden_low[...] = low(hidden)
        fetches[2].wait()

        def use(src, index):
            rows = rows_at(index, size)
            tiles(r.pre_near, rows, src[...], r.gate_up_near, 512, False)
            stores.start(r.pre_near.at[rows], r.pre.at[rows])
            gate, up = r.pre_near[rows, pl.ds(0, room)], r.pre_near[rows, pl.ds(room, room)]
            r.product[rows, :] = low(gate * jax.nn.sigmoid(gate) * up)

        gathered = Gathered(group, copies, stores, r.hidden_low, r.landed, r.whole, use)
        gathered.step()
        gathered_all(gathered, lambda: next(down, None))
        finish(down)
        stores.drain()
        stores.start(r.down_near, r.down_rows).wait()
        copies.drain()

    return launch(
        number,
        body,
        far(mixed=mixed, out_rows=out_rows, gate_up=gate_up)
        | near(block=block, scales=scales, down_mine=down_mine),
        far(
            whole=shape((length, width)),
            pre=shape((length, both), F32),
            down_rows=shape((room, width)),
        )
        | near(
            attn_raw=shape((size, width), F32),
            hidden=shape((size, width), F32),
            product=shape((length, room)),
        ),
        dict(
            act=pltpu.VMEM(mixed.shape, BF16),
            out_near=pltpu.VMEM(out_rows.shape, BF16),
            gate_up_near=pltpu.VMEM(gate_up.shape, BF16),
            down_near=pltpu.VMEM((room, width), BF16),
            part=pltpu.VMEM((length, width), BF16),
            landings=landing(size, width, True),
            landed=pltpu.VMEM((length, width), BF16),
            hidden_low=pltpu.VMEM((size, width), BF16),
            pre_near=pltpu.VMEM((length, both), F32),
        ),
        17 + 15 + 17,
        22,
    )


def feed_out(product, down_rows, pre, hidden, cotangent, scales, number):
    ranks = lax.axis_size("ctx")
    size, width = hidden.shape
    length, both = pre.shape
    room = both // 2

    def body(r, copies, stores):
        group = Group("ctx")
        fetches = [
            stores.start(r.product, r.act),
            stores.start(r.down_rows, r.down_near),
            stores.start(r.pre, r.pre_near),
        ]
        meet(group.peers())
        item = Sum(Rows(r.part, ranks), *r.landings)
        fetches[0].wait()
        fetches[1].wait()
        finish(ctx_sum(group, copies, r.act, r.down_near, item, 512, False))
        unit, inverse = norm(item.total(group))
        gain = r.scales[3:4, :]
        r.result[...] = low(r.hidden[...] + unit * gain)
        upstream = r.cotangent[...].astype(F32)
        r.feed_term[...] = jnp.sum(upstream * unit, axis=0, keepdims=True)
        r.down_low[...] = low(norm_back(upstream, unit, inverse, gain))
        fetches[2].wait()

        def use(src, index):
            rows = rows_at(index, size)
            tiles(r.product_grad, pl.ds(0, size), src[...], r.down_near, 256, True)
            gate, up = r.pre_near[rows, pl.ds(0, room)], r.pre_near[rows, pl.ds(room, room)]
            grad, sigmoid = r.product_grad[...], jax.nn.sigmoid(gate)
            r.both_low[rows, pl.ds(0, room)] = low(
                grad * up * sigmoid * (1.0 + gate * (1.0 - sigmoid))
            )
            r.both_low[rows, pl.ds(room, room)] = low(grad * gate * sigmoid)

        gathered = Gathered(group, copies, stores, r.down_low, r.landed, r.whole, use)
        gathered.step()
        gathered_all(gathered, lambda: None)
        stores.drain()
        copies.drain()

    return launch(
        number,
        body,
        far(product=product, down_rows=down_rows, pre=pre)
        | near(hidden=hidden, cotangent=cotangent, scales=scales),
        far(whole=shape((length, width)))
        | near(
            result=shape((size, width)),
            feed_term=shape((1, width), F32),
            both_low=shape((length, both)),
        ),
        dict(
            act=pltpu.VMEM(product.shape, BF16),
            down_near=pltpu.VMEM(down_rows.shape, BF16),
            pre_near=pltpu.VMEM((length, both), F32),
            part=pltpu.VMEM((length, width), BF16),
            landings=landing(size, width, True),
            landed=pltpu.VMEM((length, width), BF16),
            down_low=pltpu.VMEM((size, width), BF16),
            product_grad=pltpu.VMEM((size, room), F32),
        ),
        17 + 15,
        12,
    )


def hidden_back(
    both_low, gate_up, cotangent, attn_raw, scales, out_rows, gate_up_grad, down_grad, number
):
    ranks, owners = lax.axis_size("ctx"), lax.axis_size("fsdp")
    size, width = attn_raw.shape
    length, both = both_low.shape
    share = out_rows.shape[0]
    gate_up_block = (gate_up_grad.shape[0] // owners, both)
    down_block = (down_grad.shape[0], width // owners)

    def body(r, copies, stores):
        group, owner = Group("ctx"), Group("fsdp")
        fetches = [
            stores.start(r.both_low, r.act),
            stores.start(r.gate_up, r.gate_up_near),
            stores.start(r.out_rows, r.out_near),
        ]
        meet(group.peers() + owner.peers())
        item = Sum(Rows(r.part, ranks), *r.landings)
        owned = []
        for grad, out, scratch in (
            (Rows(r.gate_up_grad, owners), r.gate_up_share, r.gate_up_sum),
            (Strips(r.down_grad, owners), r.down_share, r.down_sum),
        ):
            part, from_sibling, *places = scratch
            own = Sum(Rows(part, owners), *places, out)
            owned.append(owner_sum(owner, copies, stores, [grad], [own], [from_sibling]))
        next(owned[0])
        fetches[0].wait()
        fetches[1].wait()
        weave(ctx_sum(group, copies, r.act, r.gate_up_near, item, 512, True), owned[0])
        hidden_grad = r.cotangent[...].astype(F32) + item.total(group)
        r.hidden_grad[...] = hidden_grad
        unit, inverse = norm(r.attn_raw[...])
        r.attn_term[...] = jnp.sum(hidden_grad * unit, axis=0, keepdims=True)
        r.attn_low[...] = low(norm_back(hidden_grad, unit, inverse, r.scales[2:3, :]))
        fetches[2].wait()

        def use(src, index):
            tiles(r.mixed_grad, rows_at(index, size), src[...], r.out_near, 256, True)

        gathered = Gathered(group, copies, stores, r.attn_low, r.landed, r.whole, use)
        gathered.step()
        finish(owned[0])

        def pump():
            next(owned[1], None)
            next(owned[1], None)

        gathered_all(gathered, pump)
        finish(owned[1])
        stores.drain()
        copies.drain()

    return launch(
        number,
        body,
        far(
            both_low=both_low,
            gate_up=gate_up,
            out_rows=out_rows,
            gate_up_grad=gate_up_grad,
            down_grad=down_grad,
        )
        | near(cotangent=cotangent, attn_raw=attn_raw, scales=scales),
        far(whole=shape((length, width)))
        | near(
            hidden_grad=shape((size, width), F32),
            attn_term=shape((1, width), F32),
            mixed_grad=shape((length, share)),
            gate_up_share=shape(gate_up_block),
            down_share=shape(down_block),
        ),
        dict(
            act=pltpu.VMEM(both_low.shape, BF16),
            gate_up_near=pltpu.VMEM(gate_up.shape, BF16),
            out_near=pltpu.VMEM(out_rows.shape, BF16),
            part=pltpu.VMEM((length, width), BF16),
            landings=landing(size, width, True),
            landed=pltpu.VMEM((length, width), BF16),
            attn_low=pltpu.VMEM((size, width), BF16),
            gate_up_sum=sum_scratch(*gate_up_block, owners),
            down_sum=sum_scratch(*down_block, owners),
        ),
        17 + 15 + 17 + 17,
        3 + 8 + 8 + 8,
    )


def attend_back(front, mixed_grad, cosine, sine, positions, gate_up_share, number):
    ranks = lax.axis_size("ctx")
    length, share = mixed_grad.shape
    lanes, chunk = 2 * HD, 256
    whole = (ranks * gate_up_share.shape[0], gate_up_share.shape[1])

    def body(r, copies, stores):
        group = Group("ctx")
        others = [{"ctx": lax.rem(group.me + step, ranks)} for step in range(1, ranks)]
        meet(others)
        all_shares, stored = Rows(r.landed, ranks), Rows(r.whole, ranks)
        stream = ring_gather(group, copies, [(r.block, all_shares)], True)
        next(stream)
        stores.start(r.block, stored.block(group.me))
        r.key_turn[...] = jnp.zeros_like(r.key_turn)
        r.value_sum[...] = jnp.zeros_like(r.value_sum)

        def advance():
            for index in next(stream, []):
                stores.start(all_shares.block(index), stored.block(index))

        for pair in range(share // lanes):
            span = pl.ds(pair * lanes, lanes)
            key_turned = r.keys[:, span].astype(F32).T.astype(BF16)

            def step(i, carry):
                rows = rows_at(i, chunk)
                query, grad = r.queries[rows, span], r.mixed_grad[rows, span]
                nothing = jnp.zeros_like(query)
                outs = []
                for mask in heads_of(query):
                    query_head = jnp.where(mask, query, nothing)
                    grad_head = jnp.where(mask, grad, nothing)
                    probs = soft(r.keys[:, span], query_head, r.key_pos[...], r.query_pos[:, rows])
                    prob_grad = back_dot(r.values[:, span], grad_head)
                    delta = jnp.sum(probs * prob_grad, axis=0, keepdims=True)
                    score_low = low(probs * (prob_grad - delta))
                    r.value_sum[:, span] += dot(low(probs), grad_head)
                    r.key_turn[:, span] += dot(score_low, query_head)
                    outs.append(dot(key_turned, score_low))
                query_rot = (pair_of(outs) * HD ** (-0.5)).T
                r.query_turn[rows, span] = query_rot * r.cosine[rows, :] + turned_back(
                    query_rot * r.sine[rows, :]
                )
                return carry

            steps = length // chunk
            lax.fori_loop(0, steps // 2, step, 0)
            advance()
            lax.fori_loop(steps // 2, steps, step, 0)
            advance()
            key_rot = r.key_turn[:, span] * HD ** (-0.5)
            r.key_turn[:, span] = key_rot * r.cosine[...] + turned_back(key_rot * r.sine[...])
        by_row = lax.broadcasted_iota(jnp.int32, (8, share), 0) < 4
        mine = rows_at(group.me, share)
        for i, (turn, unit) in enumerate(
            ((r.query_turn, r.query_unit), (r.key_turn, r.key_unit))
        ):
            product = turn[...] * unit[...]
            r.terms[pl.ds(i, 1), :] = jnp.sum(product, axis=0, keepdims=True)
            part = totals_by_row(
                jnp.where(by_row == (i == 0), 1.0, 0.0), product * r.scales[i : i + 1, mine]
            )
            r.sums[...] = part if i == 0 else r.sums[...] + part
        exchange = [copies.start(r.sums, r.sums_landed.at[i], to) for i, to in enumerate(others)]
        arrived(exchange)
        totals = r.sums[...] + jnp.sum(r.sums_landed[...], axis=0)
        means = (totals * (1.0 / (ranks * share))).T
        for i, (turn, unit) in enumerate(
            ((r.query_turn, r.query_unit), (r.key_turn, r.key_unit))
        ):
            column = slice(4 * i, 4 * i + 1)
            r.qkv_low[:, pl.ds(i * share, share)] = low(
                r.inverse[:, column]
                * (turn[...] * r.scales[i : i + 1, mine] - unit[...] * means[:, column])
            )
        r.qkv_low[:, pl.ds(2 * share, share)] = low(r.value_sum[...])
        for _ in range(5):
            advance()
        copies.drain()
        stores.drain()

    return launch(
        number,
        body,
        near(
            queries=front.queries,
            keys=front.keys,
            values=front.values,
            query_unit=front.query_unit,
            key_unit=front.key_unit,
            inverse=front.inverse,
            scales=front.scales,
            mixed_grad=mixed_grad,
            cosine=cosine,
            sine=sine,
            key_pos=positions[:, None],
            query_pos=positions[None, :],
            block=gate_up_share,
        ),
        near(qkv_low=shape((length, 3 * share)), terms=shape((2, share), F32))
        | far(whole=shape(whole)),
        dict(
            query_turn=pltpu.VMEM((length, share), F32),
            key_turn=pltpu.VMEM((length, share), F32),
            value_sum=pltpu.VMEM((length, share), F32),
            sums=pltpu.VMEM((8, length), F32),
            sums_landed=pltpu.VMEM((ranks - 1, 8, length), F32),
            landed=pltpu.VMEM(whole, BF16),
        ),
        15 + ranks - 1,
        8,
    )


def input_back(qkv_low, qkv, hidden_grad, qkv_grad, strip_grad, number):
    ranks, owners = lax.axis_size("ctx"), lax.axis_size("fsdp")
    size, width = hidden_grad.shape
    length = qkv_low.shape[0]
    qkv_block = (qkv_grad.shape[0] // owners, qkv_grad.shape[1])
    strip_block = (strip_grad.shape[0], width // owners)

    def body(r, copies, stores):
        group, owner = Group("ctx"), Group("fsdp")
        fetches = [stores.start(r.qkv_low, r.act), stores.start(r.qkv, r.qkv_near)]
        meet(group.peers() + owner.peers())
        item = Sum(Rows(r.part, ranks), *r.landings)
        sums = [
            Sum(Rows(scratch[0], owners), *scratch[2:], out)
            for scratch, out in ((r.qkv_sum, r.qkv_share), (r.strip_sum, r.strip_share))
        ]
        owned = owner_sum(
            owner,
            copies,
            stores,
            [Rows(r.qkv_grad, owners), Strips(r.strip_grad, owners)],
            sums,
            [r.qkv_sum[1], r.strip_sum[1]],
        )
        next(owned)
        for fetch in fetches:
            fetch.wait()
        weave(ctx_sum(group, copies, r.act, r.qkv_near, item, 512, True), owned)
        r.input_grad[...] = r.hidden_grad[...] + item.total(group)
        finish(owned)
        copies.drain()

    return launch(
        number,
        body,
        far(qkv_low=qkv_low, qkv=qkv, qkv_grad=qkv_grad, strip_grad=strip_grad)
        | near(hidden_grad=hidden_grad),
        near(
            input_grad=shape((size, width), F32),
            qkv_share=shape(qkv_block),
            strip_share=shape(strip_block),
        ),
        dict(
            act=pltpu.VMEM(qkv_low.shape, BF16),
            qkv_near=pltpu.VMEM(qkv.shape, BF16),
            part=pltpu.VMEM((length, width), BF16),
            landings=landing(size, width, True),
            qkv_sum=sum_scratch(*qkv_block, owners),
            strip_sum=sum_scratch(*strip_block, owners),
        ),
        17 + 34,
        2 + 16,
    )


def spread(parts, number):
    ranks, count = lax.axis_size("ctx"), len(parts)
    wholes = [(ranks * part.shape[0], part.shape[1]) for part in parts]
    names = [f"part_{i}" for i in range(count)]

    def body(r, copies, stores):
        group = Group("ctx")
        meet(group.peers())
        mine = [getattr(r, name) for name in names]
        stored = [Rows(getattr(r, "whole_" + name), ranks) for name in names]
        landed = [Rows(ref, ranks) for ref in r.landed]
        own = True
        for indexes in ring_gather(group, copies, list(zip(mine, landed)), True):
            for index in indexes:
                for block, all_blocks, to in zip(mine, landed, stored):
                    stores.start(block if own else all_blocks.block(index), to.block(index))
                own = False
        copies.drain()
        stores.drain()

    outs = launch(
        number,
        body,
        near(**dict(zip(names, parts))),
        far(**{"whole_" + name: shape(dims) for name, dims in zip(names, wholes)}),
        dict(landed=[pltpu.VMEM(dims, BF16) for dims in wholes]),
        15 * count,
        8 * count,
    )
    return [getattr(outs, "whole_" + name) for name in names]


def body(
    layer_input,
    cotangent,
    query_weight,
    key_weight,
    value_weight,
    out_weight,
    gate_weight,
    up_weight,
    down_weight,
    query_gain,
    key_gain,
    attention_gain,
    feed_gain,
    pair_table,
):
    row_count = layer_input.shape[1]
    block_len = row_count // 2
    rank = lax.axis_index("ctx")
    owner = lax.axis_index("fsdp")
    ranks = lax.axis_size("ctx")
    owners = lax.axis_size("fsdp")
    width = query_weight.shape[1]
    share = width // ranks
    strip = width // owners
    units = gate_weight.shape[1] // ranks
    room = -(-units // 256) * 256
    blocks = pair_table.reshape(-1)
    positions = (
        blocks[:, None] * block_len + jnp.arange(block_len, dtype=jnp.int32)[None, :]
    ).reshape(-1)
    cosine, sine = angles(positions)

    def cut(weight, size):
        return lax.dynamic_slice_in_dim(weight, rank * size, size, axis=1)

    def wide(weight):
        return jnp.pad(cut(weight, units), ((0, 0), (0, room - units)))

    inputs = layer_input[0]
    qkv_mine = jnp.concatenate(
        [cut(w, share) for w in (query_weight, key_weight, value_weight)], axis=1
    )
    gains_mine = jnp.pad(
        jnp.stack([query_gain, key_gain, attention_gain, feed_gain]), ((0, 28), (0, 0))
    )
    flat = lambda c, f: c * owners + f
    odd = lax.rem(owner, 2)
    routes = [
        [
            (flat(c, 2 * d + j), flat(d, 2 * c + (j ^ k)))
            for c in range(ranks)
            for d in range(ranks)
            for j in range(2)
        ]
        for k in range(2)
    ]
    axes = ("ctx", "fsdp")
    tall = jnp.concatenate([out_weight, down_weight], axis=0)
    pieces = []
    for k, route in enumerate(routes):
        target = 2 * rank + (odd ^ k)
        strips = lax.dynamic_slice_in_dim(tall, target * strip, strip, axis=1)
        pieces.append(lax.ppermute(strips, axes, route))

    def in_order(pair):
        return jnp.where(odd == 0, pair[0], pair[1]), jnp.where(odd == 0, pair[1], pair[0])

    low_piece, high_piece = in_order(pieces)
    out_size = out_weight.shape[0]
    strips = jnp.concatenate(
        [
            low_piece[:out_size],
            high_piece[:out_size],
            low_piece[out_size:],
            high_piece[out_size:],
            jnp.zeros((room - units, strip), BF16),
        ],
        axis=0,
    )

    front = attend(
        inputs,
        qkv_mine,
        gains_mine,
        strips[:share],
        jnp.concatenate([wide(gate_weight), wide(up_weight)], axis=1),
        cosine,
        sine,
        positions,
        1,
    )
    fed = feed_in(
        front.mixed, front.out_rows, inputs, front.scales, front.gate_up, strips[share:], 2
    )
    back = feed_out(
        fed.product, fed.down_rows, fed.pre, fed.hidden, cotangent[0], front.scales, 3
    )
    gate_up_grad = low(outer_sum(fed.whole, back.both_low))
    down_grad = low(outer_sum(fed.product, back.whole))
    inner = hidden_back(
        back.both_low,
        front.gate_up,
        cotangent[0],
        fed.attn_raw,
        front.scales,
        front.out_rows,
        gate_up_grad,
        down_grad,
        4,
    )
    out_rows_grad = low(outer_sum(front.mixed, inner.whole))
    outer = attend_back(
        front, inner.mixed_grad, cosine, sine, positions, inner.gate_up_share, 5
    )
    qkv_grad = low(outer_sum(front.whole, outer.qkv_low))

    def placed(term):
        return lax.dynamic_update_slice_in_dim(
            jnp.zeros((width,), F32), term, rank * share, axis=0
        )

    gain_terms = low(jnp.stack([placed(outer.terms[0]), placed(outer.terms[1]), inner.attn_term[0], back.feed_term[0]]))
    strip_grads = jnp.concatenate([out_rows_grad, jnp.pad(gain_terms, ((0, 28), (0, 0)))], axis=0)
    last = input_back(
        outer.qkv_low, front.qkv, inner.hidden_grad, qkv_grad, strip_grads, 6
    )
    out_share, gains_share = last.strip_share[:share], last.strip_share[share:]
    down_share = inner.down_share
    down_size = down_weight.shape[0]
    by_owner = [
        jnp.concatenate(
            [
                out_share[j * out_size : (j + 1) * out_size],
                down_share[j * down_size : (j + 1) * down_size],
            ],
            axis=0,
        )
        for j in range(2)
    ]
    by_route = in_order(by_owner)
    returned = [
        lax.ppermute(piece, axes, [(b, a) for a, b in route])
        for piece, route in zip(by_route, routes)
    ]
    tall_share = jnp.concatenate(in_order(returned), axis=1)

    qkv_all, tall_all, gains_all = spread([last.qkv_share, tall_share, gains_share], 7)

    def side_by_side(parts, size, at):
        columns = parts.reshape(ranks, -1, parts.shape[-1])[:, :, at : at + size]
        return columns.transpose(1, 0, 2).reshape(columns.shape[1], -1).astype(F32)

    gate_share, up_share = (side_by_side(outer.whole, units, at) for at in (0, room))
    query_share, key_share, value_share = (
        side_by_side(qkv_all, share, i * share) for i in range(3)
    )
    tall_whole = side_by_side(tall_all, share, 0)
    out_share, down_share = tall_whole[:out_size], tall_whole[out_size:]

    mine = jnp.sum(gains_all.reshape(ranks, -1, strip)[:, :4].astype(F32), axis=0)
    return (
        back.result[None],
        last.input_grad[None],
        query_share,
        key_share,
        value_share,
        out_share,
        gate_share,
        up_share,
        down_share,
        mine[0],
        mine[1],
        mine[2],
        mine[3],
    )


def solution(mesh):
    weights = (P("fsdp", None),) * 7
    gains = (P("fsdp"),) * 4
    tokens = P("fsdp", "ctx", None)
    in_specs = (tokens, tokens, *weights, *gains, P())
    out_specs = (tokens, tokens, *weights, *gains)
    return jax.shard_map(body, mesh=mesh, in_specs=in_specs, out_specs=out_specs, check_vma=False)
```

```python
import functools
import types

import jax
import jax.numpy as jnp
import numpy as np
from jax import lax
from jax.experimental import pallas as pl
from jax.experimental.pallas import tpu as pltpu
from jax.sharding import PartitionSpec as P

HD = 64
EPSILON = 1e-06
THETA = 500000.0
MESH = pl.DeviceIdType.MESH
F32 = jnp.float32
BF16 = jnp.bfloat16
ROOM = 56 * 2**20
NEG = -1e30


def angles(length):
    freqs = THETA ** (-np.arange(0, HD, 2, dtype=np.float32) / np.float32(HD))
    phase = np.arange(length, dtype=np.float32)[:, None] * np.tile(freqs, 4)[None, :]
    return jnp.asarray(np.cos(phase)), jnp.asarray(np.sin(phase))


def dot(left, right):
    return jnp.dot(left, right, preferred_element_type=F32)


def outer_sum(left, right):
    return lax.dot_general(left, right, (((0,), (0,)), ((), ())), preferred_element_type=F32)


def back_dot(grad, weight):
    return lax.dot_general(grad, weight, (((1,), (1,)), ((), ())), preferred_element_type=F32)


def low(values):
    return values.astype(BF16)


class Group:
    def __init__(self, axis):
        me = lax.axis_index(axis)
        self.axis = axis
        self.size = lax.axis_size(axis)
        self.me = me
        if axis == "ctx":
            self.core, self.pair, self.place = 0, me // 4, lax.rem(me, 4)
        else:
            self.core, self.pair, self.place = lax.rem(me, 2), lax.rem(me, 4) // 2, me // 4
        self.sibling = me + 1 - 2 * self.core if axis == "fsdp" else None
        self.right, self.left, self.partner = self.at(False, 1), self.at(False, 3), self.at(True, 0)

    def at(self, other, step):
        pair = 1 - self.pair if other else self.pair
        place = lax.rem(self.place + step, 4)
        if self.axis == "ctx":
            return pair * 4 + place
        return place * 4 + pair * 2 + self.core

    def peers(self):
        near = [self.right, self.left, self.partner]
        if self.sibling is not None:
            near.append(self.sibling)
        return [{self.axis: peer} for peer in near]


def meet(peers):
    barrier = pltpu.get_barrier_semaphore()
    for peer in peers:
        pl.semaphore_signal(barrier, inc=1, device_id=peer, device_id_type=MESH)
    pl.semaphore_wait(barrier, len(peers))


class Copies:
    def __init__(self, sent, came):
        self.sent, self.came, self.count, self.all = sent, came, 0, []

    def start(self, src, dst, peer):
        copy = pltpu.make_async_remote_copy(
            src_ref=src,
            dst_ref=dst,
            send_sem=self.sent.at[self.count],
            recv_sem=self.came.at[self.count],
            device_id=peer,
            device_id_type=MESH,
        )
        self.count += 1
        self.all.append(copy)
        copy.start()
        return copy

    def drain(self):
        for copy in self.all:
            copy.wait_send()


class Once:
    def __init__(self, copy):
        self.copy, self.waited = copy, False

    def wait(self):
        if not self.waited:
            self.copy.wait()
        self.waited = True


class Stores:
    def __init__(self, sems):
        self.sems, self.count, self.all = sems, 0, []

    def start(self, src, dst):
        copy = pltpu.make_async_copy(src, dst, self.sems.at[self.count])
        self.count += 1
        copy.start()
        copy = Once(copy)
        self.all.append(copy)
        return copy

    def drain(self):
        for copy in self.all:
            copy.wait()
        self.all = []


def rows_at(index, size):
    return pl.ds(pl.multiple_of(index * size, size), size)


class Rows:
    def __init__(self, ref, blocks):
        self.ref, self.rows = ref, ref.shape[0] // blocks

    def block(self, index, low_row=0, high_row=None):
        high_row = self.rows if high_row is None else high_row
        start = pl.multiple_of(index * self.rows + low_row, 16)
        return self.ref.at[pl.ds(start, high_row - low_row)]


class Chips(Rows):
    def __init__(self, ref, owners):
        super().__init__(ref, owners // 2)

    def block(self, index, low_row=0, high_row=None):
        return super().block(lax.div(index, 2), low_row, high_row)


class Strips:
    def __init__(self, ref, blocks):
        self.ref, self.rows, self.width = ref, ref.shape[0], ref.shape[1] // blocks

    def block(self, index, low_row=0, high_row=None):
        high_row = self.rows if high_row is None else high_row
        return self.ref.at[pl.ds(low_row, high_row - low_row), rows_at(index, self.width)]


def arrived(copies):
    for copy in copies:
        copy.wait_recv()


class Cuts:
    def __init__(self, rows, edged):
        half = rows // 2
        start = rows // 8 // 16 * 16 if edged else 0
        stop = rows - rows // 4 // 16 * 16 if edged else rows
        self.all, self.first, self.second = [(0, rows)], [(0, half)], [(half, rows)]
        self.middle = [(start, stop)]
        self.middle_first, self.middle_second = [(start, half)], [(half, stop)]
        self.top = [(0, start)] if start else []
        self.bottom = [(stop, rows)] if stop < rows else []
        self.edges = self.top + self.bottom
        self.half = half


def ring_gather(group, copies, items, edged=False):
    at = group.at
    right, left, partner = ({group.axis: peer} for peer in (group.right, group.left, group.partner))

    def move(index, part, peer, own=False):
        started = []
        for mine, whole in items:
            for lo, hi in getattr(Cuts(whole.rows, edged), part):
                view = whole.block(index, lo, hi)
                started.append(copies.start(mine if own else view, view, peer))
        return started

    near_left = move(group.me, "all", right, True)
    near_right = move(group.me, "all", left, True)
    across = move(group.me, "all", partner, True)
    yield [group.me]
    arrived(near_left)
    far_left = move(group.left, "first", right)
    edges = move(group.left, "edges", partner)
    arrived(near_right)
    far_right = move(group.right, "second", left)
    edges += move(group.right, "edges", partner)
    arrived(across)
    other_left = move(group.partner, "middle", right)
    other_right = move(group.partner, "middle", left)
    yield [group.left, group.right, group.partner]
    arrived(far_left)
    last = move(at(False, 2), "top", partner)
    arrived(far_right)
    last += move(at(False, 2), "bottom", partner)
    yield [at(False, 2)]
    arrived(other_left)
    last += move(at(True, 3), "middle_first", right)
    arrived(other_right)
    last += move(at(True, 1), "middle_second", left)
    arrived(edges)
    yield [at(True, 3), at(True, 1)]
    arrived(last)
    yield [at(True, 2)]


def add(ref, others):
    value = ref[...].astype(F32)
    for other in others:
        value += other[...].astype(F32)
    ref[...] = low(value)


class Sum:
    def __init__(self, parts, far, side, cross, out=None):
        self.parts, self.far, self.side, self.cross, self.out = parts, far, side, cross, out

    def total(self, group):
        own = self.parts.block(group.me)[...].astype(F32)
        sides = self.side[0, 1].astype(F32) + self.side[1, 1].astype(F32)
        return own + sides + self.cross[0].astype(F32)


def landing(rows, columns, edged=False):
    return [
        pltpu.VMEM((2, 2, rows // 2, columns), BF16),
        pltpu.VMEM((2, 2, rows, columns), BF16),
        pltpu.VMEM((4 if edged else 1, rows, columns), BF16),
    ]


def ring_scatter(group, copies, items, prepare, edged=False):
    at = group.at
    right, left, partner = ({group.axis: peer} for peer in (group.right, group.left, group.partner))
    cuts = [Cuts(item.parts.rows, edged) for item in items]

    def window(ref, lead, lo, hi):
        return ref.at[(*lead, pl.ds(lo, hi - lo))]

    def send_edges(step):
        started = []
        for item, cut in zip(items, cuts):
            for lo, hi in cut.edges:
                view = item.parts.block(at(True, step), lo, hi)
                started.append(copies.start(view, window(item.cross, (step,), lo, hi), partner))
        return started

    def add_edges(step):
        for item, cut in zip(items, cuts):
            for lo, hi in cut.edges:
                add(item.parts.block(at(False, step), lo, hi), [window(item.cross, (step,), lo, hi)])

    def far_cut(cut, i, side):
        if side == 0:
            return (cut.middle_first if i == 0 else cut.first)[0]
        return (cut.middle_second if i == 0 else cut.second)[0]

    def far_window(item, cut, i, side):
        lo, hi = far_cut(cut, i, side)
        base = side * cut.half
        return window(item.far, (side, i), lo - base, hi - base)

    def send_far(i):
        started = ([], [])
        for item, cut in zip(items, cuts):
            for side, peer in enumerate((right, left)):
                view = item.parts.block(at(i == 0, 2), *far_cut(cut, i, side))
                started[side].append(copies.start(view, far_window(item, cut, i, side), peer))
        return started

    def send_near(i, far):
        started = []
        for side, (step, peer) in enumerate(((1, right), (3, left))):
            arrived(far[side])
            index = at(i == 0, step)
            for item, cut in zip(items, cuts):
                add(
                    item.parts.block(index, *far_cut(cut, i, side)),
                    [far_window(item, cut, i, side)],
                )
                lo, hi = (cut.middle if i == 0 else cut.all)[0]
                view = item.parts.block(index, lo, hi)
                started.append(copies.start(view, window(item.side, (side, i), lo, hi), peer))
        return started

    prepare(True, 2)
    far_other = send_far(0)
    edges = {2: send_edges(2)}
    yield
    prepare(False, 2)
    arrived(edges[2])
    add_edges(2)
    far_same = send_far(1)
    yield
    for step in (1, 3):
        prepare(True, step)
        edges[step] = send_edges(step)
    yield
    near_other = send_near(0, far_other)
    yield
    prepare(True, 0)
    edges[0] = send_edges(0)
    for step in (1, 3):
        prepare(False, step)
        arrived(edges[step])
        add_edges(step)
    near_same = send_near(1, far_same)
    yield
    arrived(near_other)
    across = []
    for item, cut in zip(items, cuts):
        lo, hi = cut.middle[0]
        view = item.parts.block(group.partner, lo, hi)
        add(view, [window(item.side, (0, 0), lo, hi), window(item.side, (1, 0), lo, hi)])
        across.append(copies.start(view, window(item.cross, (0,), lo, hi), partner))
    yield
    prepare(False, 0)
    yield
    arrived(near_same)
    arrived(across)
    arrived(edges[0])
    yield


def owner_gather(owner, copies, stores, items):
    sibling = {owner.axis: owner.sibling}
    passed, own = [], True
    placed = [stores.start(mine, whole.block(owner.me)) for mine, whole in items]
    for indexes in ring_gather(owner, copies, items):
        for index in indexes:
            for mine, whole in items:
                view = whole.block(index)
                passed.append(copies.start(mine if own else view, view, sibling))
        own = False
        yield
    arrived(passed)
    for copy in placed:
        copy.wait()
    yield


def owner_sum(owner, copies, stores, sources, sums, from_sibling):
    sibling = {owner.axis: owner.sibling}
    turn = 1 - 2 * owner.core
    waits = {}
    for step in (2, 1, 3, 0):
        for other in (True, False):
            index, number = owner.at(other, step), len(waits)
            waits[other, step] = [
                (
                    stores.start(source.block(index), item.parts.block(index)),
                    copies.start(source.block(index + turn), landed.at[number], sibling),
                    landed.at[number],
                )
                for source, item, landed in zip(sources, sums, from_sibling)
            ]

    def prepare(other, step):
        for (fetch, give, landed), item in zip(waits[other, step], sums):
            fetch.wait()
            give.wait_recv()
            add(item.parts.block(owner.at(other, step)), [landed])

    yield
    yield from ring_scatter(owner, copies, sums, prepare)
    for item in sums:
        item.out[...] = low(item.total(owner))
    yield


def sum_scratch(rows, columns, owners):
    return [
        pltpu.VMEM((owners // 2 * rows, columns), BF16),
        pltpu.VMEM((owners // 2, rows, columns), BF16),
        *landing(rows, columns),
    ]


FAR = pl.BlockSpec(memory_space=pl.ANY)
NEAR = pl.BlockSpec(memory_space=pltpu.VMEM)


def shape(dims, kind=BF16):
    return jax.ShapeDtypeStruct(dims, kind)


def launch(number, body, ins, outs, temps, remote, local):
    names, scratch, groups = [*ins, *outs], [], []
    for name, kind in temps.items():
        kinds = kind if isinstance(kind, list) else [kind]
        groups.append((name, len(kinds), isinstance(kind, list)))
        scratch += kinds
    dma = pltpu.SemaphoreType.DMA
    scratch += [dma((remote,)), dma((remote,)), dma((local,))]

    def kernel(*refs):
        named = dict(zip(names, refs))
        rest = list(refs[len(names) :])
        for name, count, many in groups:
            named[name] = rest[:count] if many else rest[0]
            del rest[:count]
        sent, came, near = rest
        body(types.SimpleNamespace(**named), Copies(sent, came), Stores(near))

    results = pl.pallas_call(
        kernel,
        out_shape=[out for out, _ in outs.values()],
        in_specs=[spec for _, spec in ins.values()],
        out_specs=[spec for _, spec in outs.values()],
        scratch_shapes=scratch,
        compiler_params=pltpu.CompilerParams(
            collective_id=number, has_side_effects=True, vmem_limit_bytes=ROOM
        ),
    )(*[array for array, _ in ins.values()])
    return types.SimpleNamespace(**dict(zip(outs, results)))


def near(**arrays):
    return {name: (array, NEAR) for name, array in arrays.items()}


def far(**arrays):
    return {name: (array, FAR) for name, array in arrays.items()}


def tiles(product, rows, values, weight, tile, transposed):
    size = values[0].shape[0]
    value = values[0] if len(values) == 1 else jnp.concatenate(values, axis=0)

    def step(i, carry):
        span = rows_at(i, tile)
        if transposed:
            piece = back_dot(value, weight[span, :])
        else:
            piece = dot(value, weight[:, span])
        piece = piece.astype(product.dtype)
        for k, at in enumerate(rows):
            product[at, span] = piece[k * size : (k + 1) * size]
        return carry

    lax.fori_loop(0, product.shape[1] // tile, step, 0)


def totals_by_row(select, value):
    return lax.dot_general(
        select,
        value,
        (((1,), (1,)), ((), ())),
        precision=lax.Precision.HIGHEST,
        preferred_element_type=F32,
    )


class Gathered:
    def __init__(self, group, copies, stores, block, landed, whole, use):
        self.group, self.stores, self.use = group, stores, use
        self.block, self.landed = block, Rows(landed, group.size)
        self.whole = Rows(whole, group.size)
        self.stream = ring_gather(group, copies, [(block, self.landed)], True)
        self.ready, self.fresh = [], True

    def step(self):
        self.ready += [(self.fresh, index) for index in next(self.stream)]
        self.fresh = False

    def consume(self, last=True):
        while len(self.ready) > (0 if last else 1):
            pair, self.ready = self.ready[:2], self.ready[2:]
            sources = [self.block if own else self.landed.block(index) for own, index in pair]
            for src, (_, index) in zip(sources, pair):
                self.stores.start(src, self.whole.block(index))
            self.use(sources, [rows_at(index, self.landed.rows) for _, index in pair])


def gathered_all(gathered):
    for _ in range(4):
        gathered.consume(False)
        gathered.step()
    gathered.consume()


def ctx_sum(group, copies, act, weight, items, tile, transposed):
    parts = items[0].parts

    def prepare(other, step):
        rows = rows_at(group.at(other, step), parts.rows)
        tiles(parts.ref, [rows], [act[rows, :]], weight, tile, transposed)

    return ring_scatter(group, copies, items, prepare, True)


def weave(main, stream):
    for step in "000110101010101":
        next(stream if step == "1" else main)


def finish(stream):
    for _ in stream:
        pass


def norm(values):
    inverse = lax.rsqrt(jnp.mean(values * values, axis=-1, keepdims=True) + EPSILON)
    return values * inverse, inverse


def norm_back(grad, unit, inverse, gain):
    pull = grad * gain
    return inverse * (pull - unit * jnp.mean(pull * unit, axis=-1, keepdims=True))


def turn_lanes(shape):
    return lax.rem(lax.broadcasted_iota(jnp.int32, shape, 1), HD) < HD // 2


def turned(values):
    lanes = values.shape[1]
    ahead = pltpu.roll(values, lanes - HD // 2, 1)
    behind = pltpu.roll(values, HD // 2, 1)
    return jnp.where(turn_lanes(values.shape), -ahead, behind)


def turned_back(values):
    lanes = values.shape[1]
    ahead = pltpu.roll(values, lanes - HD // 2, 1)
    behind = pltpu.roll(values, HD // 2, 1)
    return jnp.where(turn_lanes(values.shape), ahead, -behind)


def heads_of(query):
    first = lax.broadcasted_iota(jnp.int32, query.shape, 1) < HD
    return first, jnp.logical_not(first)


def pair_of(outs):
    return jnp.concatenate([outs[0][:HD], outs[1][HD:]], axis=0)


def soft(keys, span, query, start):
    chunk = query.shape[0]
    own = back_dot(keys[pl.ds(start, chunk), span], query)
    behind = lax.broadcasted_iota(jnp.int32, own.shape, 0) <= lax.broadcasted_iota(
        jnp.int32, own.shape, 1
    )
    pieces = [jnp.where(behind, own, NEG)]
    if start:
        pieces.insert(0, back_dot(keys[pl.ds(0, start), span], query))
    top = jnp.max(pieces[-1], axis=0, keepdims=True)
    for piece in pieces[:-1]:
        top = jnp.maximum(top, jnp.max(piece, axis=0, keepdims=True))
    pieces = [jnp.exp(piece - top) for piece in pieces]
    total = sum(jnp.sum(piece, axis=0, keepdims=True) for piece in pieces)
    places = [pl.ds(0, start), pl.ds(start, chunk)][-len(pieces) :]
    return list(zip(places, pieces)), 1.0 / total


def placing(query_pos):
    length = query_pos.shape[1]
    row = lax.broadcasted_iota(jnp.int32, (length, length), 0)
    return low(jnp.where(row == query_pos[...], 1.0, 0.0))


def dealing(key_pos):
    length = key_pos.shape[0]
    column = lax.broadcasted_iota(jnp.int32, (length, length), 1)
    return low(jnp.where(column == key_pos[...], 1.0, 0.0))


def split(values):
    high = low(values)
    return high, low(values - high.astype(F32))


def attend(block, qkv_mine, gains_mine, out_mine, gate_mine, cosine, sine, orders, number):
    ranks, owners = lax.axis_size("ctx"), lax.axis_size("fsdp")
    (size, depth), columns = block.shape, qkv_mine.shape[1]
    length, share, chunk = ranks * size, columns // 3, 256
    lanes = 2 * HD

    def body(r, copies, stores):
        group, owner = Group("ctx"), Group("fsdp")
        others = [lax.rem(group.me + step, ranks) for step in (2, 6, 4, 1, 3, 5, 7)]
        meet([{"ctx": other} for other in others] + owner.peers())
        normed = 2 * share
        by_lane = lax.broadcasted_iota(jnp.int32, (8, normed), 1) < share
        by_row = lax.broadcasted_iota(jnp.int32, (8, normed), 0) < 4
        select = jnp.where(by_lane == by_row, 1.0, 0.0)

        def use(sources, places):
            tiles(r.proj, places, [src[...] for src in sources], r.qkv_near, columns, False)
            for rows in places:
                value = r.proj[rows, pl.ds(0, normed)]
                r.sums[:, rows] = totals_by_row(select, value * value)

        gathered = Gathered(group, copies, stores, r.block, r.landed, r.whole, use)
        gains_all = Rows(r.gains_near, owners)
        first = owner_gather(
            owner,
            copies,
            stores,
            [(r.qkv_mine, Rows(r.qkv_near, owners)), (r.gains_mine, gains_all)],
        )
        second = owner_gather(owner, copies, stores, [(r.out_mine, Rows(r.out_near, owners))])
        third = owner_gather(owner, copies, stores, [(r.gate_mine, Rows(r.gate_near, owners))])

        next(first)
        gathered.step()
        next(first)
        next(first)
        next(first)
        next(second)
        gathered.step()
        finish(first)
        gathered.step()
        stores.drain()
        stores.start(r.qkv_near, r.qkv)
        gathered.consume(False)
        next(second)
        gathered.step()
        gathered.consume(False)
        gathered.step()
        gathered.consume()
        exchange = [
            copies.start(r.sums, r.sums_landed.at[i], {"ctx": other})
            for i, other in enumerate(others)
        ]
        next(second)
        for i in range(owners):
            rows = r.gains_near[pl.ds(i * gains_all.rows, 16), :].astype(F32)
            r.scales[:, pl.ds(i * rows.shape[1], rows.shape[1])] = rows[:8]
        next(second)
        next(third)
        arrived(exchange)
        totals = r.sums[...] + jnp.sum(r.sums_landed[...], axis=0)
        r.inverse_dealt[...] = lax.rsqrt(totals * (1.0 / (ranks * share)) + EPSILON).T
        mine = rows_at(group.me, share)

        wide = r.stack.shape[1] - share
        for k in range(2):
            span = pl.ds(k * share, share)
            unit = r.proj[:, span] * r.inverse_dealt[:, 4 * k : 4 * k + 1]
            for half, part in enumerate(split(unit)):
                r.stack[:, pl.ds((2 * k + half) * share, share)] = part
        r.stack[:, pl.ds(wide, share)] = low(r.proj[:, pl.ds(2 * share, share)])
        order = placing(r.query_pos)
        high, rest = split(r.inverse_dealt[...])
        r.inverse[...] = dot(order, high) + dot(order, rest)
        for k, (unit, out) in enumerate(((r.query_unit, r.queries), (r.key_unit, r.keys))):
            both = dot(order, r.stack[:, pl.ds(2 * k * share, 2 * share)])
            unit[...] = both[:, :share] + both[:, share:]
            scaled = unit[...] * r.scales[k : k + 1, mine]
            for pair in range(share // lanes):
                part = scaled[:, pair * lanes : (pair + 1) * lanes]
                out[:, pl.ds(pair * lanes, lanes)] = low(
                    part * r.cosine[...] + turned(part) * r.sine[...]
                )
        r.values[...] = low(dot(order, r.stack[:, pl.ds(wide, share)]))
        r.deal[...] = dealing(r.key_pos)
        crossing = []
        for pair in range(share // lanes):
            span = pl.ds(pair * lanes, lanes)
            value_turned = r.values[:, span].astype(F32).T.astype(BF16)
            for start in range(0, length, chunk):
                rows = pl.ds(start, chunk)
                query = r.queries[rows, span] * BF16(HD ** (-0.5))
                nothing = jnp.zeros_like(query)
                outs = []
                for mask in heads_of(query):
                    pieces, over = soft(r.keys, span, jnp.where(mask, query, nothing), start)
                    out = sum(
                        dot(value_turned[:, at.start : at.start + at.size], low(piece))
                        for at, piece in pieces
                    )
                    outs.append(out * over)
                r.mixed[rows, :] = low(pair_of(outs).T)
                if start == length // 2:
                    next(second if pair == 0 else third)

            r.mixed_dealt[:, span] = low(dot(r.deal[...], r.mixed[...]))
            at = pl.ds(pl.multiple_of(group.me * share + pair * lanes, lanes), lanes)
            for other in others:
                src = r.mixed_dealt.at[rows_at(other, size), span]
                crossing.append(copies.start(src, r.mixed_landed.at[:, at], {"ctx": other}))
            r.mixed_landed[:, at] = r.mixed_dealt[rows_at(group.me, size), span]
            next(third)
        finish(second)
        arrived(crossing)
        stores.drain()
        stores.start(r.out_near, r.out_whole)
        r.mixed_rows[...] = r.mixed_landed[...]
        tiles(r.attn_raw, [pl.ds(0, size)], [r.mixed_landed[...]], r.out_near, 512, False)
        unit, _ = norm(r.attn_raw[...])
        hidden = r.block[...].astype(F32) + unit * r.scales[2:3, :]
        r.hidden[...] = hidden
        r.hidden_low[...] = low(hidden)
        finish(third)
        stores.start(r.gate_near, r.gate)
        stores.drain()
        copies.drain()

    return launch(
        number,
        body,
        near(
            block=block,
            qkv_mine=qkv_mine,
            gains_mine=gains_mine,
            out_mine=out_mine,
            gate_mine=gate_mine,
            cosine=cosine,
            sine=sine,
        )
        | near(**orders),
        far(
            whole=shape((length, depth)),
            qkv=shape((depth, columns)),
            out_whole=shape((depth, depth)),
            gate=shape((depth, gate_mine.shape[1])),
        )
        | near(
            scales=shape((8, depth), F32),
            inverse=shape((length, 8), F32),
            query_unit=shape((length, share), F32),
            key_unit=shape((length, share), F32),
            queries=shape((length, share)),
            keys=shape((length, share)),
            values=shape((length, share)),
            mixed_rows=shape((size, depth)),
            attn_raw=shape((size, depth), F32),
            hidden=shape((size, depth), F32),
            hidden_low=shape((size, depth)),
        ),
        dict(
            landed=pltpu.VMEM((length, depth), BF16),
            qkv_near=pltpu.VMEM((depth, columns), BF16),
            gains_near=pltpu.VMEM((owners * gains_mine.shape[0], gains_mine.shape[1]), BF16),
            out_near=pltpu.VMEM((depth, depth), BF16),
            gate_near=pltpu.VMEM((depth, gate_mine.shape[1]), BF16),
            proj=pltpu.VMEM((length, columns), F32),
            sums=pltpu.VMEM((8, length), F32),
            sums_landed=pltpu.VMEM((ranks - 1, 8, length), F32),
            inverse_dealt=pltpu.VMEM((length, 8), F32),
            stack=pltpu.VMEM((length, 5 * share), BF16),
            deal=pltpu.VMEM((length, length), BF16),
            mixed=pltpu.VMEM((length, lanes), BF16),
            mixed_dealt=pltpu.VMEM((length, share), BF16),
            mixed_landed=pltpu.VMEM((size, depth), BF16),
        ),
        15 + 34 + 17 + 17 + 3 * (ranks - 1),
        24,
    )


def feed(hidden, hidden_low, gate, up_mine, down_mine, cotangent, scales, number):
    ranks, owners = lax.axis_size("ctx"), lax.axis_size("fsdp")
    size, width = hidden.shape
    length, room = ranks * size, gate.shape[1]
    both = 2 * room

    def body(r, copies, stores):
        group, owner = Group("ctx"), Group("fsdp")
        gate_fetch = stores.start(r.gate, r.gate_near)
        meet(group.peers() + owner.peers())
        first, second = pl.ds(0, room), pl.ds(room, room)

        def forward(sources, places):
            values = [src[...] for src in sources]
            tiles(r.pre.at[:, first], places, values, r.gate_near, room, False)
            tiles(r.pre.at[:, second], places, values, r.up_near, room, False)
            for rows in places:
                gate, up = r.pre[rows, first], r.pre[rows, second]
                r.product[rows, :] = low(gate * jax.nn.sigmoid(gate) * up)

        gathered = Gathered(group, copies, stores, r.hidden_low, r.landed, r.whole_hidden, forward)
        up = owner_gather(owner, copies, stores, [(r.up_mine, Rows(r.up_near, owners))])
        down = owner_gather(
            owner, copies, stores, [(r.down_mine, Strips(r.down_near, owners))]
        )
        next(up)
        gathered.step()
        next(up)
        next(up)
        gathered.step()
        next(up)
        next(down)
        gathered.step()
        finish(up)
        gate_fetch.wait()
        gathered.step()
        next(down)
        gathered.consume(False)
        next(down)
        gathered.step()
        next(down)
        gathered.consume()
        finish(down)
        stores.drain()
        stores.start(r.up_near, r.up)
        stores.start(r.down_near, r.down_rows)
        item = Sum(Rows(r.part, ranks), *r.landings)
        finish(ctx_sum(group, copies, r.product, r.down_near, [item], 512, False))
        unit, inverse = norm(item.total(group))
        gain = r.scales[3:4, :]
        r.result[...] = low(r.hidden[...] + unit * gain)
        upstream = r.cotangent[...].astype(F32)
        r.feed_term[...] = jnp.sum(upstream * unit, axis=0, keepdims=True)
        r.down_low[...] = low(norm_back(upstream, unit, inverse, gain))

        def backward(sources, places):
            values = [src[...] for src in sources]
            tiles(r.product_grad, places, values, r.down_near, room, True)
            for rows in places:
                gate, up = r.pre[rows, first], r.pre[rows, second]
                grad, sigmoid = r.product_grad[rows, :], jax.nn.sigmoid(gate)
                r.both_low[rows, first] = low(
                    grad * up * sigmoid * (1.0 + gate * (1.0 - sigmoid))
                )
                r.both_low[rows, second] = low(grad * gate * sigmoid)

        gathered = Gathered(group, copies, stores, r.down_low, r.landed_down, r.whole_down, backward)
        gathered.step()
        gathered_all(gathered)
        stores.drain()
        copies.drain()

    return launch(
        number,
        body,
        far(gate=gate)
        | near(
            hidden=hidden,
            hidden_low=hidden_low,
            up_mine=up_mine,
            down_mine=down_mine,
            cotangent=cotangent,
            scales=scales,
        ),
        far(
            whole_hidden=shape((length, width)),
            whole_down=shape((length, width)),
            up=shape((width, room)),
            down_rows=shape((room, width)),
        )
        | near(
            result=shape((size, width)),
            feed_term=shape((1, width), F32),
            product=shape((length, room)),
            both_low=shape((length, both)),
        ),
        dict(
            gate_near=pltpu.VMEM((width, room), BF16),
            up_near=pltpu.VMEM((width, room), BF16),
            down_near=pltpu.VMEM((room, width), BF16),
            landed=pltpu.VMEM((length, width), BF16),
            pre=pltpu.VMEM((length, both), F32),
            part=pltpu.VMEM((length, width), BF16),
            landings=landing(size, width, True),
            landed_down=pltpu.VMEM((length, width), BF16),
            down_low=pltpu.VMEM((size, width), BF16),
            product_grad=pltpu.VMEM((length, room), F32),
        ),
        15 + 15 + 17 + 34,
        24,
    )


def hidden_back(both_low, gate, up, cotangent, attn_raw, scales, out_whole, gate_up_grad, number):
    ranks, owners = lax.axis_size("ctx"), lax.axis_size("fsdp")
    size, width = attn_raw.shape
    length, both = both_low.shape
    room, share = both // 2, width // ranks
    gate_up_block = (gate_up_grad.shape[0] // owners, both)

    def body(r, copies, stores):
        group, owner = Group("ctx"), Group("fsdp")
        others = [lax.rem(group.me + step, ranks) for step in (2, 6, 4, 1, 3, 5, 7)]
        fetches = [
            stores.start(r.both_low, r.act),
            stores.start(r.gate, r.gate_up_near.at[:, pl.ds(0, room)]),
            stores.start(r.up, r.gate_up_near.at[:, pl.ds(room, room)]),
        ]
        out_fetch = stores.start(r.out_whole, r.out_near)
        meet([{"ctx": other} for other in others] + owner.peers())
        item = Sum(Rows(r.part, ranks), *r.landings)
        part, from_sibling, *places = r.gate_up_sum
        own = Sum(Chips(part, owners), *places, r.gate_up_share)
        owned = owner_sum(
            owner, copies, stores, [Rows(r.gate_up_grad, owners)], [own], [from_sibling]
        )
        for fetch in fetches:
            fetch.wait()
        next(owned)
        weave(ctx_sum(group, copies, r.act, r.gate_up_near, [item], 512, True), owned)
        hidden_grad = r.cotangent[...].astype(F32) + item.total(group)
        r.hidden_grad[...] = hidden_grad
        unit, inverse = norm(r.attn_raw[...])
        r.attn_term[...] = jnp.sum(hidden_grad * unit, axis=0, keepdims=True)
        r.attn_low[...] = low(norm_back(hidden_grad, unit, inverse, r.scales[2:3, :]))
        out_fetch.wait()
        value = r.attn_low[...]
        mine = rows_at(group.me, size)
        crossing = []
        for i, other in enumerate(others):
            r.mixed_out[i] = low(back_dot(value, r.out_near[rows_at(other, share), :]))
            crossing.append(
                copies.start(r.mixed_out.at[i], r.mixed_landed.at[mine], {"ctx": other})
            )
        r.mixed_landed[mine, :] = low(back_dot(value, r.out_near[rows_at(group.me, share), :]))
        finish(owned)
        arrived(crossing)
        r.mixed_grad[...] = r.mixed_landed[...]
        stores.drain()
        copies.drain()

    return launch(
        number,
        body,
        far(both_low=both_low, gate=gate, up=up, out_whole=out_whole, gate_up_grad=gate_up_grad)
        | near(cotangent=cotangent, attn_raw=attn_raw, scales=scales),
        near(
            hidden_grad=shape((size, width), F32),
            attn_term=shape((1, width), F32),
            attn_low=shape((size, width)),
            mixed_grad=shape((length, share)),
            gate_up_share=shape(gate_up_block),
        ),
        dict(
            act=pltpu.VMEM(both_low.shape, BF16),
            gate_up_near=pltpu.VMEM((width, both), BF16),
            out_near=pltpu.VMEM(out_whole.shape, BF16),
            part=pltpu.VMEM((length, width), BF16),
            landings=landing(size, width, True),
            mixed_out=pltpu.VMEM((ranks - 1, size, share), BF16),
            mixed_landed=pltpu.VMEM((length, share), BF16),
            gate_up_sum=sum_scratch(*gate_up_block, owners),
        ),
        17 + 17 + ranks - 1,
        4 + 8,
    )


def attend_back(front, mixed_grad, cosine, sine, orders, gate_up_share, out_grad, number):
    ranks, owners = lax.axis_size("ctx"), lax.axis_size("fsdp")
    length, share = mixed_grad.shape
    lanes, chunk = 2 * HD, 256
    whole = (ranks * gate_up_share.shape[0], gate_up_share.shape[1])
    out_block = (out_grad.shape[0] // owners, out_grad.shape[1])

    def body(r, copies, stores):
        group, owner = Group("ctx"), Group("fsdp")
        others = [{"ctx": lax.rem(group.me + step, ranks)} for step in range(1, ranks)]
        meet(others + owner.peers())
        all_shares, stored = Rows(r.landed, ranks), Rows(r.whole, ranks)
        stream = ring_gather(group, copies, [(r.block, all_shares)], True)
        next(stream)
        stores.start(r.block, stored.block(group.me))
        part, from_sibling, *places = r.out_sum
        own = Sum(Chips(part, owners), *places, r.out_share)
        owned = owner_sum(owner, copies, stores, [Rows(r.out_grad, owners)], [own], [from_sibling])
        next(owned)
        next(owned)
        r.key_turn[...] = jnp.zeros_like(r.key_turn)
        r.value_sum[...] = jnp.zeros_like(r.value_sum)

        r.grads[...] = low(dot(placing(r.query_pos), r.mixed_grad[...]))

        def advance():
            for index in next(stream, []):
                stores.start(all_shares.block(index), stored.block(index))
            next(owned, None)

        for pair in range(share // lanes):
            span = pl.ds(pair * lanes, lanes)
            key_turned = r.keys[:, span].astype(F32).T.astype(BF16)
            for start in range(0, length, chunk):
                rows = pl.ds(start, chunk)
                query, grad = r.queries[rows, span] * BF16(HD ** (-0.5)), r.grads[rows, span]
                nothing = jnp.zeros_like(query)
                outs = []
                for mask in heads_of(query):
                    query_head = jnp.where(mask, query, nothing)
                    grad_head = jnp.where(mask, grad, nothing)
                    pieces, over = soft(r.keys, span, query_head, start)
                    probs = [piece * over for _, piece in pieces]
                    prob_grads = [back_dot(r.values[at, span], grad_head) for at, _ in pieces]
                    delta = sum(
                        jnp.sum(prob * prob_grad, axis=0, keepdims=True)
                        for prob, prob_grad in zip(probs, prob_grads)
                    )
                    out = 0.0
                    for (at, _), prob, prob_grad in zip(pieces, probs, prob_grads):
                        score_low = low(prob * (prob_grad - delta))
                        r.value_sum[at, span] += dot(low(prob), grad_head)
                        r.key_turn[at, span] += dot(score_low, query_head)
                        out += dot(key_turned[:, at.start : at.start + at.size], score_low)
                    outs.append(out)
                query_rot = (pair_of(outs) * HD ** (-0.5)).T
                r.query_turn[rows, span] = query_rot * r.cosine[rows, :] + turned_back(
                    query_rot * r.sine[rows, :]
                )
                if start % (2 * chunk):
                    advance()
            key_rot = r.key_turn[:, span]
            r.key_turn[:, span] = key_rot * r.cosine[...] + turned_back(key_rot * r.sine[...])
        by_row = lax.broadcasted_iota(jnp.int32, (8, share), 0) < 4
        mine = rows_at(group.me, share)
        for i, (turn, unit) in enumerate(
            ((r.query_turn, r.query_unit), (r.key_turn, r.key_unit))
        ):
            product = turn[...] * unit[...]
            r.terms[pl.ds(i, 1), :] = jnp.sum(product, axis=0, keepdims=True)
            part = totals_by_row(
                jnp.where(by_row == (i == 0), 1.0, 0.0), product * r.scales[i : i + 1, mine]
            )
            r.sums[...] = part if i == 0 else r.sums[...] + part
        exchange = [copies.start(r.sums, r.sums_landed.at[i], to) for i, to in enumerate(others)]
        advance()
        arrived(exchange)
        totals = r.sums[...] + jnp.sum(r.sums_landed[...], axis=0)
        means = (totals * (1.0 / (ranks * share))).T
        for i, (turn, unit) in enumerate(
            ((r.query_turn, r.query_unit), (r.key_turn, r.key_unit))
        ):
            column = slice(4 * i, 4 * i + 1)
            r.placed_low[:, pl.ds(i * share, share)] = low(
                r.inverse[:, column]
                * (turn[...] * r.scales[i : i + 1, mine] - unit[...] * means[:, column])
            )
        r.placed_low[:, pl.ds(2 * share, share)] = low(r.value_sum[...])

        r.qkv_low[...] = low(dot(dealing(r.key_pos), r.placed_low[...]))
        for _ in range(10):
            advance()
        copies.drain()
        stores.drain()

    return launch(
        number,
        body,
        near(
            queries=front.queries,
            keys=front.keys,
            values=front.values,
            query_unit=front.query_unit,
            key_unit=front.key_unit,
            inverse=front.inverse,
            scales=front.scales,
            mixed_grad=mixed_grad,
            cosine=cosine,
            sine=sine,
            block=gate_up_share,
        )
        | far(out_grad=out_grad)
        | near(**orders),
        near(
            qkv_low=shape((length, 3 * share)),
            terms=shape((2, share), F32),
            out_share=shape(out_block),
        )
        | far(whole=shape(whole)),
        dict(
            grads=pltpu.VMEM((length, share), BF16),
            placed_low=pltpu.VMEM((length, 3 * share), BF16),
            query_turn=pltpu.VMEM((length, share), F32),
            key_turn=pltpu.VMEM((length, share), F32),
            value_sum=pltpu.VMEM((length, share), F32),
            sums=pltpu.VMEM((8, length), F32),
            sums_landed=pltpu.VMEM((ranks - 1, 8, length), F32),
            landed=pltpu.VMEM(whole, BF16),
            out_sum=sum_scratch(*out_block, owners),
        ),
        15 + 17 + ranks - 1,
        16,
    )


def input_back(qkv_low, qkv, hidden_grad, out_share, qkv_grad, strip_grad, number):
    ranks, owners = lax.axis_size("ctx"), lax.axis_size("fsdp")
    size, width = hidden_grad.shape
    length = qkv_low.shape[0]
    height = out_share.shape[0]
    qkv_block = (qkv_grad.shape[0] // owners, qkv_grad.shape[1])
    strip_block = (strip_grad.shape[0], width // owners)

    def body(r, copies, stores):
        group, owner = Group("ctx"), Group("fsdp")
        fetches = [
            stores.start(r.qkv_low, r.act),
            stores.start(r.qkv, r.qkv_near),
            stores.start(r.out_share, r.out_part),
        ]
        meet(group.peers() + owner.peers())
        item = Sum(Rows(r.part, ranks), *r.landings)
        out_item = Sum(Strips(r.out_part, ranks), *r.out_landings)
        sums = [
            Sum(Chips(scratch[0], owners), *scratch[2:], out)
            for scratch, out in ((r.strip_sum, r.strip_share), (r.qkv_sum, r.qkv_share))
        ]
        owned = owner_sum(
            owner,
            copies,
            stores,
            [Strips(r.strip_grad, owners), Rows(r.qkv_grad, owners)],
            sums,
            [r.strip_sum[1], r.qkv_sum[1]],
        )
        for fetch in fetches:
            fetch.wait()
        next(owned)
        weave(ctx_sum(group, copies, r.act, r.qkv_near, [item, out_item], 512, True), owned)
        r.input_grad[...] = r.hidden_grad[...] + item.total(group)
        r.out_mine[...] = low(out_item.total(group))
        finish(owned)
        copies.drain()

    return launch(
        number,
        body,
        far(
            qkv_low=qkv_low, qkv=qkv, out_share=out_share, qkv_grad=qkv_grad, strip_grad=strip_grad
        )
        | near(hidden_grad=hidden_grad),
        near(
            input_grad=shape((size, width), F32),
            out_mine=shape((height, width // ranks)),
            qkv_share=shape(qkv_block),
            strip_share=shape(strip_block),
        ),
        dict(
            act=pltpu.VMEM(qkv_low.shape, BF16),
            qkv_near=pltpu.VMEM(qkv.shape, BF16),
            part=pltpu.VMEM((length, width), BF16),
            landings=landing(size, width, True),
            out_part=pltpu.VMEM(out_share.shape, BF16),
            out_landings=landing(height, width // ranks, True),
            qkv_sum=sum_scratch(*qkv_block, owners),
            strip_sum=sum_scratch(*strip_block, owners),
        ),
        34 + 34,
        3 + 16,
    )


def spread(parts, number):
    ranks, count = lax.axis_size("ctx"), len(parts)
    wholes = [(ranks * part.shape[0], part.shape[1]) for part in parts]
    names = [f"part_{i}" for i in range(count)]

    def body(r, copies, stores):
        group = Group("ctx")
        meet(group.peers())
        mine = [getattr(r, name) for name in names]
        stored = [Rows(getattr(r, "whole_" + name), ranks) for name in names]
        landed = [Rows(ref, ranks) for ref in r.landed]
        own = True
        for indexes in ring_gather(group, copies, list(zip(mine, landed)), True):
            for index in indexes:
                for block, all_blocks, to in zip(mine, landed, stored):
                    stores.start(block if own else all_blocks.block(index), to.block(index))
                own = False
        copies.drain()
        stores.drain()

    outs = launch(
        number,
        body,
        near(**dict(zip(names, parts))),
        far(**{"whole_" + name: shape(dims) for name, dims in zip(names, wholes)}),
        dict(landed=[pltpu.VMEM(dims, BF16) for dims in wholes]),
        15 * count,
        8 * count,
    )
    return [getattr(outs, "whole_" + name) for name in names]


def unfold_kernel(units, shares, gate, up):
    size, room = gate.shape[0], shares.shape[1] // 2
    tail = units // 128 * 128
    for i, out in enumerate((gate, up)):
        span = pl.ds(i * room, room)
        left = shares[pl.ds(0, size), span].astype(F32)
        right = pltpu.roll(shares[pl.ds(size, size), span].astype(F32), units - tail, 1)
        inside = lax.broadcasted_iota(jnp.int32, (size, 128), 1) < units - tail
        out[:, pl.ds(0, tail)] = left[:, :tail]
        out[:, pl.ds(tail, 128)] = jnp.where(inside, left[:, tail : tail + 128], right[:, :128])
        out[:, pl.ds(tail + 128, tail)] = right[:, 128 : tail + 128]


def unfold(shares, units):
    ranks = lax.axis_size("ctx")
    size = shares.shape[0] // ranks
    return pl.pallas_call(
        functools.partial(unfold_kernel, units),
        grid=(ranks // 2,),
        in_specs=[pl.BlockSpec((2 * size, shares.shape[1]), lambda i: (i, 0))],
        out_specs=[pl.BlockSpec((size, 2 * units), lambda i: (0, i))] * 2,
        out_shape=[shape((size, ranks * units), F32)] * 2,
        compiler_params=pltpu.CompilerParams(vmem_limit_bytes=ROOM),
    )(shares)


def widen_kernel(qkv, out, down, query_out, key_out, value_out, out_out, down_out):
    share = out.shape[1]
    for i, ref in enumerate((query_out, key_out, value_out)):
        ref[...] = qkv[:, pl.ds(i * share, share)].astype(F32)
    out_out[...] = out[...].astype(F32)
    down_out[...] = down[...].astype(F32)


def widen(qkv, out, down):
    ranks = lax.axis_size("ctx")
    share = out.shape[1]
    heights = [part.shape[0] // ranks for part in (qkv, qkv, qkv, out, down)]
    return pl.pallas_call(
        widen_kernel,
        grid=(ranks,),
        in_specs=[
            pl.BlockSpec((part.shape[0] // ranks, part.shape[1]), lambda i: (i, 0))
            for part in (qkv, out, down)
        ],
        out_specs=[pl.BlockSpec((height, share), lambda i: (0, i)) for height in heights],
        out_shape=[shape((height, ranks * share), F32) for height in heights],
        compiler_params=pltpu.CompilerParams(vmem_limit_bytes=ROOM),
    )(qkv, out, down)


def body(
    layer_input,
    cotangent,
    query_weight,
    key_weight,
    value_weight,
    out_weight,
    gate_weight,
    up_weight,
    down_weight,
    query_gain,
    key_gain,
    attention_gain,
    feed_gain,
    pair_table,
):
    row_count = layer_input.shape[1]
    block_len = row_count // 2
    rank = lax.axis_index("ctx")
    owner = lax.axis_index("fsdp")
    ranks = lax.axis_size("ctx")
    owners = lax.axis_size("fsdp")
    width = query_weight.shape[1]
    share = width // ranks
    strip = width // owners
    units = gate_weight.shape[1] // ranks
    room = -(-units // 256) * 256
    blocks = pair_table.reshape(-1)
    positions = (
        blocks[:, None] * block_len + jnp.arange(block_len, dtype=jnp.int32)[None, :]
    ).reshape(-1)
    orders = dict(key_pos=positions[:, None], query_pos=positions[None, :])
    cosine, sine = angles(2 * ranks * block_len)

    def cut(weight, size):
        return lax.dynamic_slice_in_dim(weight, rank * size, size, axis=1)

    def wide(weight):
        return jnp.pad(cut(weight, units), ((0, 0), (0, room - units)))

    inputs = layer_input[0]
    qkv_mine = jnp.concatenate(
        [cut(w, share) for w in (query_weight, key_weight, value_weight)], axis=1
    )
    gains_mine = jnp.pad(
        jnp.stack([query_gain, key_gain, attention_gain, feed_gain]), ((0, 28), (0, 0))
    )
    flat = lambda c, f: c * owners + f
    odd = lax.rem(owner, 2)
    routes = [
        [
            (flat(c, 2 * d + j), flat(d, 2 * c + (j ^ k)))
            for c in range(ranks)
            for d in range(ranks)
            for j in range(2)
        ]
        for k in range(2)
    ]
    axes = ("ctx", "fsdp")
    pieces = []
    for k, route in enumerate(routes):
        target = 2 * rank + (odd ^ k)
        strips = lax.dynamic_slice_in_dim(down_weight, target * strip, strip, axis=1)
        pieces.append(lax.ppermute(strips, axes, route))

    def in_order(pair):
        return jnp.where(odd == 0, pair[0], pair[1]), jnp.where(odd == 0, pair[1], pair[0])

    low_piece, high_piece = in_order(pieces)
    strips = jnp.concatenate(
        [low_piece, high_piece, jnp.zeros((room - units, strip), BF16)], axis=0
    )

    front = attend(
        inputs, qkv_mine, gains_mine, out_weight, wide(gate_weight), cosine, sine, orders, 1
    )
    fed = feed(
        front.hidden,
        front.hidden_low,
        front.gate,
        wide(up_weight),
        strips,
        cotangent[0],
        front.scales,
        2,
    )
    gate_up_grad = low(outer_sum(fed.whole_hidden, fed.both_low))
    inner = hidden_back(
        fed.both_low,
        front.gate,
        fed.up,
        cotangent[0],
        front.attn_raw,
        front.scales,
        front.out_whole,
        gate_up_grad,
        3,
    )
    out_grad = low(outer_sum(front.mixed_rows, inner.attn_low))
    outer = attend_back(
        front, inner.mixed_grad, cosine, sine, orders, inner.gate_up_share, out_grad, 4
    )
    down_grad = low(outer_sum(fed.product, fed.whole_down))
    qkv_grad = low(outer_sum(front.whole, outer.qkv_low))

    def placed(term):
        return lax.dynamic_update_slice_in_dim(
            jnp.zeros((width,), F32), term, rank * share, axis=0
        )

    gain_terms = low(jnp.stack([placed(outer.terms[0]), placed(outer.terms[1]), inner.attn_term[0], fed.feed_term[0]]))
    strip_grads = jnp.concatenate([down_grad, jnp.pad(gain_terms, ((0, 28), (0, 0)))], axis=0)
    last = input_back(
        outer.qkv_low, front.qkv, inner.hidden_grad, outer.out_share, qkv_grad, strip_grads, 5
    )
    down_size = down_weight.shape[0]
    by_owner = [last.strip_share[j * down_size : (j + 1) * down_size] for j in range(2)]
    gains_share = last.strip_share[room:]
    by_route = in_order(by_owner)
    returned = [
        lax.ppermute(piece, axes, [(b, a) for a, b in route])
        for piece, route in zip(by_route, routes)
    ]
    down_share = jnp.concatenate(in_order(returned), axis=1)

    qkv_all, out_all, down_all, gains_all = spread(
        [last.qkv_share, last.out_mine, down_share, gains_share], 6
    )

    gate_share, up_share = unfold(outer.whole, units)
    query_share, key_share, value_share, out_share, down_share = widen(qkv_all, out_all, down_all)
    mine = jnp.sum(gains_all.reshape(ranks, -1, strip)[:, :4].astype(F32), axis=0)
    return (
        fed.result[None],
        last.input_grad[None],
        query_share,
        key_share,
        value_share,
        out_share,
        gate_share,
        up_share,
        down_share,
        mine[0],
        mine[1],
        mine[2],
        mine[3],
    )


def solution(mesh):
    weights = (P("fsdp", None),) * 7
    gains = (P("fsdp"),) * 4
    tokens = P("fsdp", "ctx", None)
    in_specs = (tokens, tokens, *weights, *gains, P())
    out_specs = (tokens, tokens, *weights, *gains)
    return jax.shard_map(body, mesh=mesh, in_specs=in_specs, out_specs=out_specs, check_vma=False)
```

```python
import functools
import types

import jax
import jax.numpy as jnp
import numpy as np
from jax import lax
from jax.experimental import pallas as pl
from jax.experimental.pallas import tpu as pltpu
from jax.sharding import PartitionSpec as P

HD = 64
EPSILON = 1e-06
THETA = 500000.0
MESH = pl.DeviceIdType.MESH
F32 = jnp.float32
BF16 = jnp.bfloat16
ROOM = 56 * 2**20
NEG = -1e30


def angles(length):
    freqs = THETA ** (-np.arange(0, HD, 2, dtype=np.float32) / np.float32(HD))
    phase = np.arange(length, dtype=np.float32)[:, None] * np.tile(freqs, 4)[None, :]
    return jnp.asarray(np.cos(phase)), jnp.asarray(np.sin(phase))


def dot(left, right):
    return jnp.dot(left, right, preferred_element_type=F32)


def outer_sum(left, right):
    return lax.dot_general(left, right, (((0,), (0,)), ((), ())), preferred_element_type=F32)


def back_dot(grad, weight):
    return lax.dot_general(grad, weight, (((1,), (1,)), ((), ())), preferred_element_type=F32)


def low(values):
    return values.astype(BF16)


class Group:
    def __init__(self, axis):
        me = lax.axis_index(axis)
        self.axis = axis
        self.size = lax.axis_size(axis)
        self.me = me
        if axis == "ctx":
            self.core, self.pair, self.place = 0, me // 4, lax.rem(me, 4)
        else:
            self.core, self.pair, self.place = lax.rem(me, 2), lax.rem(me, 4) // 2, me // 4
        self.sibling = me + 1 - 2 * self.core if axis == "fsdp" else None
        self.right, self.left, self.partner = self.at(False, 1), self.at(False, 3), self.at(True, 0)

    def at(self, other, step):
        pair = 1 - self.pair if other else self.pair
        place = lax.rem(self.place + step, 4)
        if self.axis == "ctx":
            return pair * 4 + place
        return place * 4 + pair * 2 + self.core

    def peers(self):
        near = [self.right, self.left, self.partner]
        if self.sibling is not None:
            near.append(self.sibling)
        return [{self.axis: peer} for peer in near]


def meet(peers):
    barrier = pltpu.get_barrier_semaphore()
    for peer in peers:
        pl.semaphore_signal(barrier, inc=1, device_id=peer, device_id_type=MESH)
    pl.semaphore_wait(barrier, len(peers))


class Copies:
    def __init__(self, sent, came):
        self.sent, self.came, self.count, self.all = sent, came, 0, []

    def start(self, src, dst, peer):
        copy = pltpu.make_async_remote_copy(
            src_ref=src,
            dst_ref=dst,
            send_sem=self.sent.at[self.count],
            recv_sem=self.came.at[self.count],
            device_id=peer,
            device_id_type=MESH,
        )
        self.count += 1
        self.all.append(copy)
        copy.start()
        return copy

    def drain(self):
        for copy in self.all:
            copy.wait_send()


class Once:
    def __init__(self, copy):
        self.copy, self.waited = copy, False

    def wait(self):
        if not self.waited:
            self.copy.wait()
        self.waited = True


class Stores:
    def __init__(self, sems):
        self.sems, self.count, self.all = sems, 0, []

    def start(self, src, dst):
        copy = pltpu.make_async_copy(src, dst, self.sems.at[self.count])
        self.count += 1
        copy.start()
        copy = Once(copy)
        self.all.append(copy)
        return copy

    def drain(self):
        for copy in self.all:
            copy.wait()
        self.all = []


def rows_at(index, size):
    return pl.ds(pl.multiple_of(index * size, size), size)


class Rows:
    def __init__(self, ref, blocks):
        self.ref, self.rows = ref, ref.shape[0] // blocks

    def block(self, index, low_row=0, high_row=None):
        high_row = self.rows if high_row is None else high_row
        start = pl.multiple_of(index * self.rows + low_row, 16)
        return self.ref.at[pl.ds(start, high_row - low_row)]


class Chips(Rows):
    def __init__(self, ref, owners):
        super().__init__(ref, owners // 2)

    def block(self, index, low_row=0, high_row=None):
        return super().block(lax.div(index, 2), low_row, high_row)


class Strips:
    def __init__(self, ref, blocks):
        self.ref, self.rows, self.width = ref, ref.shape[0], ref.shape[1] // blocks

    def block(self, index, low_row=0, high_row=None):
        high_row = self.rows if high_row is None else high_row
        return self.ref.at[pl.ds(low_row, high_row - low_row), rows_at(index, self.width)]


def arrived(copies):
    for copy in copies:
        copy.wait_recv()


class Cuts:
    def __init__(self, rows, edged):
        half = rows // 2
        start = rows // 8 // 16 * 16 if edged else 0
        stop = rows - rows // 4 // 16 * 16 if edged else rows
        self.all, self.first, self.second = [(0, rows)], [(0, half)], [(half, rows)]
        self.middle = [(start, stop)]
        self.middle_first, self.middle_second = [(start, half)], [(half, stop)]
        self.top = [(0, start)] if start else []
        self.bottom = [(stop, rows)] if stop < rows else []
        self.edges = self.top + self.bottom
        self.half = half


def ring_gather(group, copies, items, edged=False):
    at = group.at
    right, left, partner = ({group.axis: peer} for peer in (group.right, group.left, group.partner))

    def move(index, part, peer, own=False):
        started = []
        for mine, whole in items:
            for lo, hi in getattr(Cuts(whole.rows, edged), part):
                view = whole.block(index, lo, hi)
                started.append(copies.start(mine if own else view, view, peer))
        return started

    near_left = move(group.me, "all", right, True)
    near_right = move(group.me, "all", left, True)
    across = move(group.me, "all", partner, True)
    yield [group.me]
    arrived(near_left)
    far_left = move(group.left, "first", right)
    edges = move(group.left, "edges", partner)
    arrived(near_right)
    far_right = move(group.right, "second", left)
    edges += move(group.right, "edges", partner)
    arrived(across)
    other_left = move(group.partner, "middle", right)
    other_right = move(group.partner, "middle", left)
    yield [group.left, group.right, group.partner]
    arrived(far_left)
    last = move(at(False, 2), "top", partner)
    arrived(far_right)
    last += move(at(False, 2), "bottom", partner)
    yield [at(False, 2)]
    arrived(other_left)
    last += move(at(True, 3), "middle_first", right)
    arrived(other_right)
    last += move(at(True, 1), "middle_second", left)
    arrived(edges)
    yield [at(True, 3), at(True, 1)]
    arrived(last)
    yield [at(True, 2)]


def add(ref, others):
    value = ref[...].astype(F32)
    for other in others:
        value += other[...].astype(F32)
    ref[...] = low(value)


class Sum:
    def __init__(self, parts, far, side, cross, out=None):
        self.parts, self.far, self.side, self.cross, self.out = parts, far, side, cross, out

    def total(self, group):
        own = self.parts.block(group.me)[...].astype(F32)
        sides = self.side[0, 1].astype(F32) + self.side[1, 1].astype(F32)
        return own + sides + self.cross[0].astype(F32)


def landing(rows, columns, edged=False):
    return [
        pltpu.VMEM((2, 2, rows // 2, columns), BF16),
        pltpu.VMEM((2, 2, rows, columns), BF16),
        pltpu.VMEM((4 if edged else 1, rows, columns), BF16),
    ]


def ring_scatter(group, copies, items, prepare, edged=False):
    at = group.at
    right, left, partner = ({group.axis: peer} for peer in (group.right, group.left, group.partner))
    cuts = [Cuts(item.parts.rows, edged) for item in items]

    def window(ref, lead, lo, hi):
        return ref.at[(*lead, pl.ds(lo, hi - lo))]

    def send_edges(step):
        started = []
        for item, cut in zip(items, cuts):
            for lo, hi in cut.edges:
                view = item.parts.block(at(True, step), lo, hi)
                started.append(copies.start(view, window(item.cross, (step,), lo, hi), partner))
        return started

    def add_edges(step):
        for item, cut in zip(items, cuts):
            for lo, hi in cut.edges:
                add(item.parts.block(at(False, step), lo, hi), [window(item.cross, (step,), lo, hi)])

    def far_cut(cut, i, side):
        if side == 0:
            return (cut.middle_first if i == 0 else cut.first)[0]
        return (cut.middle_second if i == 0 else cut.second)[0]

    def far_window(item, cut, i, side):
        lo, hi = far_cut(cut, i, side)
        base = side * cut.half
        return window(item.far, (side, i), lo - base, hi - base)

    def send_far(i):
        started = ([], [])
        for item, cut in zip(items, cuts):
            for side, peer in enumerate((right, left)):
                view = item.parts.block(at(i == 0, 2), *far_cut(cut, i, side))
                started[side].append(copies.start(view, far_window(item, cut, i, side), peer))
        return started

    def send_near(i, far):
        started = []
        for side, (step, peer) in enumerate(((1, right), (3, left))):
            arrived(far[side])
            index = at(i == 0, step)
            for item, cut in zip(items, cuts):
                add(
                    item.parts.block(index, *far_cut(cut, i, side)),
                    [far_window(item, cut, i, side)],
                )
                lo, hi = (cut.middle if i == 0 else cut.all)[0]
                view = item.parts.block(index, lo, hi)
                started.append(copies.start(view, window(item.side, (side, i), lo, hi), peer))
        return started

    prepare((True, 2))
    far_other = send_far(0)
    edges = {2: send_edges(2)}
    yield
    prepare((False, 2))
    arrived(edges[2])
    add_edges(2)
    far_same = send_far(1)
    yield
    prepare((True, 1), (True, 3))
    for step in (1, 3):
        edges[step] = send_edges(step)
    yield
    near_other = send_near(0, far_other)
    yield
    prepare((True, 0))
    edges[0] = send_edges(0)
    prepare((False, 1), (False, 3))
    for step in (1, 3):
        arrived(edges[step])
        add_edges(step)
    near_same = send_near(1, far_same)
    yield
    arrived(near_other)
    across = []
    for item, cut in zip(items, cuts):
        lo, hi = cut.middle[0]
        view = item.parts.block(group.partner, lo, hi)
        add(view, [window(item.side, (0, 0), lo, hi), window(item.side, (1, 0), lo, hi)])
        across.append(copies.start(view, window(item.cross, (0,), lo, hi), partner))
    yield
    prepare((False, 0))
    yield
    arrived(near_same)
    arrived(across)
    arrived(edges[0])
    yield


def owner_gather(owner, copies, stores, items):
    sibling = {owner.axis: owner.sibling}
    passed, own = [], True
    placed = [stores.start(mine, whole.block(owner.me)) for mine, whole in items]
    for indexes in ring_gather(owner, copies, items):
        for index in indexes:
            for mine, whole in items:
                view = whole.block(index)
                passed.append(copies.start(mine if own else view, view, sibling))
        own = False
        yield
    arrived(passed)
    for copy in placed:
        copy.wait()
    yield


class Made:
    def __init__(self, left, right, given, owners):
        self.left, self.right, self.given = left, right, given
        self.width = left.shape[1] // owners

    def block(self, index):
        return low(outer_sum(self.left[:, rows_at(index, self.width)], self.right[...]))


def owner_sum(owner, copies, stores, sources, sums, from_sibling):
    sibling = {owner.axis: owner.sibling}
    turn = 1 - 2 * owner.core
    waits = {}
    for step in (2, 1, 3, 0):
        for other in (True, False):
            index, number = owner.at(other, step), len(waits)
            waits[other, step] = []
            for source, item, landed in zip(sources, sums, from_sibling):
                fetch, place = None, landed.at[number]
                if isinstance(source, Made):
                    given = source.given.at[number]
                    given[...] = source.block(index + turn)
                    give = copies.start(given, place, sibling)
                    item.parts.block(index)[...] = source.block(index)
                else:
                    fetch = stores.start(source.block(index), item.parts.block(index))
                    give = copies.start(source.block(index + turn), place, sibling)
                waits[other, step].append((fetch, give, place))

    def prepare(*places):
        for place in places:
            for (fetch, give, landed), item in zip(waits[place], sums):
                if fetch is not None:
                    fetch.wait()
                give.wait_recv()
                add(item.parts.block(owner.at(*place)), [landed])

    yield
    yield from ring_scatter(owner, copies, sums, prepare)
    for item in sums:
        item.out[...] = low(item.total(owner))
    yield


def sum_scratch(rows, columns, owners):
    return [
        pltpu.VMEM((owners // 2 * rows, columns), BF16),
        pltpu.VMEM((owners // 2, rows, columns), BF16),
        *landing(rows, columns),
    ]


FAR = pl.BlockSpec(memory_space=pl.ANY)
NEAR = pl.BlockSpec(memory_space=pltpu.VMEM)


def shape(dims, kind=BF16):
    return jax.ShapeDtypeStruct(dims, kind)


def launch(number, body, ins, outs, temps, remote, local):
    names, scratch, groups = [*ins, *outs], [], []
    for name, kind in temps.items():
        kinds = kind if isinstance(kind, list) else [kind]
        groups.append((name, len(kinds), isinstance(kind, list)))
        scratch += kinds
    dma = pltpu.SemaphoreType.DMA
    scratch += [dma((remote,)), dma((remote,)), dma((local,))]

    def kernel(*refs):
        named = dict(zip(names, refs))
        rest = list(refs[len(names) :])
        for name, count, many in groups:
            named[name] = rest[:count] if many else rest[0]
            del rest[:count]
        sent, came, near = rest
        body(types.SimpleNamespace(**named), Copies(sent, came), Stores(near))

    results = pl.pallas_call(
        kernel,
        out_shape=[out for out, _ in outs.values()],
        in_specs=[spec for _, spec in ins.values()],
        out_specs=[spec for _, spec in outs.values()],
        scratch_shapes=scratch,
        compiler_params=pltpu.CompilerParams(
            collective_id=number, has_side_effects=True, vmem_limit_bytes=ROOM
        ),
    )(*[array for array, _ in ins.values()])
    return types.SimpleNamespace(**dict(zip(outs, results)))


def near(**arrays):
    return {name: (array, NEAR) for name, array in arrays.items()}


def far(**arrays):
    return {name: (array, FAR) for name, array in arrays.items()}


def tiles(product, rows, values, weight, tile, transposed):
    size = values[0].shape[0]
    value = values[0] if len(values) == 1 else jnp.concatenate(values, axis=0)

    def step(i, carry):
        span = rows_at(i, tile)
        if transposed:
            piece = back_dot(value, weight[span, :])
        else:
            piece = dot(value, weight[:, span])
        piece = piece.astype(product.dtype)
        for k, at in enumerate(rows):
            product[at, span] = piece[k * size : (k + 1) * size]
        return carry

    lax.fori_loop(0, product.shape[1] // tile, step, 0)


def totals_by_row(select, value):
    return lax.dot_general(
        select,
        value,
        (((1,), (1,)), ((), ())),
        precision=lax.Precision.HIGHEST,
        preferred_element_type=F32,
    )


class Gathered:
    def __init__(self, group, copies, stores, block, landed, whole, use):
        self.group, self.stores, self.use = group, stores, use
        self.block, self.landed = block, Rows(landed, group.size)
        self.whole = Rows(whole, group.size)
        self.stream = ring_gather(group, copies, [(block, self.landed)], True)
        self.ready, self.fresh = [], True

    def step(self):
        self.ready += [(self.fresh, index) for index in next(self.stream)]
        self.fresh = False

    def consume(self, last=True):
        while len(self.ready) > (0 if last else 1):
            pair, self.ready = self.ready[:2], self.ready[2:]
            sources = [self.block if own else self.landed.block(index) for own, index in pair]
            for src, (_, index) in zip(sources, pair):
                self.stores.start(src, self.whole.block(index))
            self.use(sources, [rows_at(index, self.landed.rows) for _, index in pair])


def gathered_all(gathered):
    for _ in range(4):
        gathered.consume(False)
        gathered.step()
    gathered.consume()


def ctx_sum(group, copies, act, weight, items, tile, transposed):
    parts = items[0].parts

    def prepare(*places):
        rows = [rows_at(group.at(other, step), parts.rows) for other, step in places]
        tiles(parts.ref, rows, [act[at, :] for at in rows], weight, tile, transposed)

    return ring_scatter(group, copies, items, prepare, True)


def weave(main, stream):
    for step in "0001110101010101":
        next(stream if step == "1" else main)


def finish(stream):
    for _ in stream:
        pass


def norm(values):
    inverse = lax.rsqrt(jnp.mean(values * values, axis=-1, keepdims=True) + EPSILON)
    return values * inverse, inverse


def norm_back(grad, unit, inverse, gain):
    pull = grad * gain
    return inverse * (pull - unit * jnp.mean(pull * unit, axis=-1, keepdims=True))


def turn_lanes(shape):
    return lax.rem(lax.broadcasted_iota(jnp.int32, shape, 1), HD) < HD // 2


def turned(values):
    lanes = values.shape[1]
    ahead = pltpu.roll(values, lanes - HD // 2, 1)
    behind = pltpu.roll(values, HD // 2, 1)
    return jnp.where(turn_lanes(values.shape), -ahead, behind)


def turned_back(values):
    lanes = values.shape[1]
    ahead = pltpu.roll(values, lanes - HD // 2, 1)
    behind = pltpu.roll(values, HD // 2, 1)
    return jnp.where(turn_lanes(values.shape), ahead, -behind)


def heads_of(query):
    first = lax.broadcasted_iota(jnp.int32, query.shape, 1) < HD
    return first, jnp.logical_not(first)


def pair_of(outs):
    return jnp.concatenate([outs[0][:HD], outs[1][HD:]], axis=0)


def soft(keys, span, query, start):
    chunk = query.shape[0]
    own = back_dot(keys[pl.ds(start, chunk), span], query)
    behind = lax.broadcasted_iota(jnp.int32, own.shape, 0) <= lax.broadcasted_iota(
        jnp.int32, own.shape, 1
    )
    pieces = [jnp.where(behind, own, NEG)]
    if start:
        pieces.insert(0, back_dot(keys[pl.ds(0, start), span], query))
    top = jnp.max(pieces[-1], axis=0, keepdims=True)
    for piece in pieces[:-1]:
        top = jnp.maximum(top, jnp.max(piece, axis=0, keepdims=True))
    pieces = [jnp.exp(piece - top) for piece in pieces]
    total = sum(jnp.sum(piece, axis=0, keepdims=True) for piece in pieces)
    places = [pl.ds(0, start), pl.ds(start, chunk)][-len(pieces) :]
    return list(zip(places, pieces)), 1.0 / total


def placing(query_pos):
    length = query_pos.shape[1]
    row = lax.broadcasted_iota(jnp.int32, (length, length), 0)
    return low(jnp.where(row == query_pos[...], 1.0, 0.0))


def dealing(key_pos):
    length = key_pos.shape[0]
    column = lax.broadcasted_iota(jnp.int32, (length, length), 1)
    return low(jnp.where(column == key_pos[...], 1.0, 0.0))


def split(values):
    high = low(values)
    return high, low(values - high.astype(F32))


def attend(block, qkv_mine, gains_mine, out_mine, gate_mine, cosine, sine, orders, number):
    ranks, owners = lax.axis_size("ctx"), lax.axis_size("fsdp")
    (size, depth), columns = block.shape, qkv_mine.shape[1]
    length, share, chunk = ranks * size, columns // 3, 256
    lanes = 2 * HD

    def body(r, copies, stores):
        group, owner = Group("ctx"), Group("fsdp")
        others = [lax.rem(group.me + step, ranks) for step in (2, 6, 4, 1, 3, 5, 7)]
        meet([{"ctx": other} for other in others] + owner.peers())
        normed = 2 * share
        by_lane = lax.broadcasted_iota(jnp.int32, (8, normed), 1) < share
        by_row = lax.broadcasted_iota(jnp.int32, (8, normed), 0) < 4
        select = jnp.where(by_lane == by_row, 1.0, 0.0)

        def use(sources, places):
            tiles(r.proj, places, [src[...] for src in sources], r.qkv_near, columns, False)
            for rows in places:
                value = r.proj[rows, pl.ds(0, normed)]
                r.sums[:, rows] = totals_by_row(select, value * value)

        gathered = Gathered(group, copies, stores, r.block, r.landed, r.whole, use)
        gains_all = Rows(r.gains_near, owners)
        first = owner_gather(
            owner,
            copies,
            stores,
            [(r.qkv_mine, Rows(r.qkv_near, owners)), (r.gains_mine, gains_all)],
        )
        second = owner_gather(owner, copies, stores, [(r.out_mine, Rows(r.out_near, owners))])
        third = owner_gather(owner, copies, stores, [(r.gate_mine, Rows(r.gate_near, owners))])

        next(first)
        gathered.step()
        next(first)
        next(first)
        next(first)
        next(second)
        gathered.step()
        finish(first)
        gathered.step()
        stores.drain()
        stores.start(r.qkv_near, r.qkv)
        gathered.consume(False)
        next(second)
        gathered.step()
        gathered.consume(False)
        gathered.step()
        gathered.consume()
        exchange = [
            copies.start(r.sums, r.sums_landed.at[i], {"ctx": other})
            for i, other in enumerate(others)
        ]
        next(second)
        for i in range(owners):
            rows = r.gains_near[pl.ds(i * gains_all.rows, 16), :].astype(F32)
            r.scales[:, pl.ds(i * rows.shape[1], rows.shape[1])] = rows[:8]
        next(second)
        next(third)
        arrived(exchange)
        totals = r.sums[...] + jnp.sum(r.sums_landed[...], axis=0)
        r.inverse_dealt[...] = lax.rsqrt(totals * (1.0 / (ranks * share)) + EPSILON).T
        mine = rows_at(group.me, share)

        wide = r.stack.shape[1] - share
        for k in range(2):
            span = pl.ds(k * share, share)
            unit = r.proj[:, span] * r.inverse_dealt[:, 4 * k : 4 * k + 1]
            for half, part in enumerate(split(unit)):
                r.stack[:, pl.ds((2 * k + half) * share, share)] = part
        r.stack[:, pl.ds(wide, share)] = low(r.proj[:, pl.ds(2 * share, share)])
        order = placing(r.query_pos)
        high, rest = split(r.inverse_dealt[...])
        r.inverse[...] = dot(order, high) + dot(order, rest)
        for k, (unit, out) in enumerate(((r.query_unit, r.queries), (r.key_unit, r.keys))):
            both = dot(order, r.stack[:, pl.ds(2 * k * share, 2 * share)])
            unit[...] = both[:, :share] + both[:, share:]
            scaled = unit[...] * r.scales[k : k + 1, mine]
            for pair in range(share // lanes):
                part = scaled[:, pair * lanes : (pair + 1) * lanes]
                out[:, pl.ds(pair * lanes, lanes)] = low(
                    part * r.cosine[...] + turned(part) * r.sine[...]
                )
        r.values[...] = low(dot(order, r.stack[:, pl.ds(wide, share)]))
        r.deal[...] = dealing(r.key_pos)
        crossing = []
        for pair in range(share // lanes):
            span = pl.ds(pair * lanes, lanes)
            value_turned = r.values[:, span].astype(F32).T.astype(BF16)
            for start in range(0, length, chunk):
                rows = pl.ds(start, chunk)
                query = r.queries[rows, span] * BF16(HD ** (-0.5))
                nothing = jnp.zeros_like(query)
                outs = []
                for mask in heads_of(query):
                    pieces, over = soft(r.keys, span, jnp.where(mask, query, nothing), start)
                    out = sum(
                        dot(value_turned[:, at.start : at.start + at.size], low(piece))
                        for at, piece in pieces
                    )
                    outs.append(out * over)
                r.mixed[rows, :] = low(pair_of(outs).T)
                if start == length // 2:
                    next(second if pair == 0 else third)

            r.mixed_dealt[:, span] = low(dot(r.deal[...], r.mixed[...]))
            at = pl.ds(pl.multiple_of(group.me * share + pair * lanes, lanes), lanes)
            for other in others:
                src = r.mixed_dealt.at[rows_at(other, size), span]
                crossing.append(copies.start(src, r.mixed_landed.at[:, at], {"ctx": other}))
            r.mixed_landed[:, at] = r.mixed_dealt[rows_at(group.me, size), span]
            next(third)
        finish(second)
        arrived(crossing)
        stores.drain()
        stores.start(r.out_near, r.out_whole)
        r.mixed_rows[...] = r.mixed_landed[...]
        tiles(r.attn_raw, [pl.ds(0, size)], [r.mixed_landed[...]], r.out_near, 512, False)
        unit, _ = norm(r.attn_raw[...])
        hidden = r.block[...].astype(F32) + unit * r.scales[2:3, :]
        r.hidden[...] = hidden
        r.hidden_low[...] = low(hidden)
        finish(third)
        stores.start(r.gate_near, r.gate)
        stores.drain()
        copies.drain()

    return launch(
        number,
        body,
        near(
            block=block,
            qkv_mine=qkv_mine,
            gains_mine=gains_mine,
            out_mine=out_mine,
            gate_mine=gate_mine,
            cosine=cosine,
            sine=sine,
        )
        | near(**orders),
        far(
            whole=shape((length, depth)),
            qkv=shape((depth, columns)),
            out_whole=shape((depth, depth)),
            gate=shape((depth, gate_mine.shape[1])),
        )
        | near(
            scales=shape((8, depth), F32),
            inverse=shape((length, 8), F32),
            query_unit=shape((length, share), F32),
            key_unit=shape((length, share), F32),
            queries=shape((length, share)),
            keys=shape((length, share)),
            values=shape((length, share)),
            mixed_rows=shape((size, depth)),
            attn_raw=shape((size, depth), F32),
            hidden=shape((size, depth), F32),
            hidden_low=shape((size, depth)),
        ),
        dict(
            landed=pltpu.VMEM((length, depth), BF16),
            qkv_near=pltpu.VMEM((depth, columns), BF16),
            gains_near=pltpu.VMEM((owners * gains_mine.shape[0], gains_mine.shape[1]), BF16),
            out_near=pltpu.VMEM((depth, depth), BF16),
            gate_near=pltpu.VMEM((depth, gate_mine.shape[1]), BF16),
            proj=pltpu.VMEM((length, columns), F32),
            sums=pltpu.VMEM((8, length), F32),
            sums_landed=pltpu.VMEM((ranks - 1, 8, length), F32),
            inverse_dealt=pltpu.VMEM((length, 8), F32),
            stack=pltpu.VMEM((length, 5 * share), BF16),
            deal=pltpu.VMEM((length, length), BF16),
            mixed=pltpu.VMEM((length, lanes), BF16),
            mixed_dealt=pltpu.VMEM((length, share), BF16),
            mixed_landed=pltpu.VMEM((size, depth), BF16),
        ),
        15 + 34 + 17 + 17 + 3 * (ranks - 1),
        24,
    )


def feed(hidden, hidden_low, gate, up_mine, down_mine, cotangent, scales, number):
    ranks, owners = lax.axis_size("ctx"), lax.axis_size("fsdp")
    size, width = hidden.shape
    length, room = ranks * size, gate.shape[1]
    both = 2 * room

    def body(r, copies, stores):
        group, owner = Group("ctx"), Group("fsdp")
        gate_fetch = stores.start(r.gate, r.gate_near)
        meet(group.peers() + owner.peers())
        first, second = pl.ds(0, room), pl.ds(room, room)

        def forward(sources, places):
            values = [src[...] for src in sources]
            tiles(r.pre.at[:, first], places, values, r.gate_near, room, False)
            tiles(r.pre.at[:, second], places, values, r.up_near, room, False)
            for rows in places:
                gate, up = r.pre[rows, first], r.pre[rows, second]
                r.product[rows, :] = low(gate * jax.nn.sigmoid(gate) * up)

        gathered = Gathered(group, copies, stores, r.hidden_low, r.landed, r.whole_hidden, forward)
        up = owner_gather(owner, copies, stores, [(r.up_mine, Rows(r.up_near, owners))])
        down = owner_gather(
            owner, copies, stores, [(r.down_mine, Strips(r.down_near, owners))]
        )
        next(up)
        gathered.step()
        next(up)
        next(up)
        gathered.step()
        next(up)
        next(down)
        gathered.step()
        finish(up)
        gate_fetch.wait()
        gathered.step()
        next(down)
        gathered.consume(False)
        next(down)
        gathered.step()
        next(down)
        gathered.consume()
        finish(down)
        stores.drain()
        stores.start(r.up_near, r.up)
        stores.start(r.down_near, r.down_rows)
        item = Sum(Rows(r.part, ranks), *r.landings)
        finish(ctx_sum(group, copies, r.product, r.down_near, [item], 512, False))
        unit, inverse = norm(item.total(group))
        gain = r.scales[3:4, :]
        r.result[...] = low(r.hidden[...] + unit * gain)
        upstream = r.cotangent[...].astype(F32)
        r.feed_term[...] = jnp.sum(upstream * unit, axis=0, keepdims=True)
        r.down_low[...] = low(norm_back(upstream, unit, inverse, gain))

        def backward(sources, places):
            values = [src[...] for src in sources]
            tiles(r.product_grad, places, values, r.down_near, room, True)
            for rows in places:
                gate, up = r.pre[rows, first], r.pre[rows, second]
                grad, sigmoid = r.product_grad[rows, :], jax.nn.sigmoid(gate)
                r.both_low[rows, first] = low(
                    grad * up * sigmoid * (1.0 + gate * (1.0 - sigmoid))
                )
                r.both_low[rows, second] = low(grad * gate * sigmoid)

        gathered = Gathered(group, copies, stores, r.down_low, r.landed_down, r.whole_down, backward)
        gathered.step()
        gathered_all(gathered)
        stores.drain()
        copies.drain()

    return launch(
        number,
        body,
        far(gate=gate)
        | near(
            hidden=hidden,
            hidden_low=hidden_low,
            up_mine=up_mine,
            down_mine=down_mine,
            cotangent=cotangent,
            scales=scales,
        ),
        far(
            whole_hidden=shape((length, width)),
            whole_down=shape((length, width)),
            up=shape((width, room)),
            down_rows=shape((room, width)),
        )
        | near(
            result=shape((size, width)),
            feed_term=shape((1, width), F32),
            product=shape((length, room)),
            both_low=shape((length, both)),
        ),
        dict(
            gate_near=pltpu.VMEM((width, room), BF16),
            up_near=pltpu.VMEM((width, room), BF16),
            down_near=pltpu.VMEM((room, width), BF16),
            landed=pltpu.VMEM((length, width), BF16),
            pre=pltpu.VMEM((length, both), F32),
            part=pltpu.VMEM((length, width), BF16),
            landings=landing(size, width, True),
            landed_down=pltpu.VMEM((length, width), BF16),
            down_low=pltpu.VMEM((size, width), BF16),
            product_grad=pltpu.VMEM((length, room), F32),
        ),
        15 + 15 + 17 + 34,
        24,
    )


def hidden_back(both_low, gate, up, cotangent, attn_raw, scales, out_whole, whole_hidden, number):
    ranks, owners = lax.axis_size("ctx"), lax.axis_size("fsdp")
    size, width = attn_raw.shape
    length, both = both_low.shape
    room, share = both // 2, width // ranks
    gate_up_block = (width // owners, both)

    def body(r, copies, stores):
        group, owner = Group("ctx"), Group("fsdp")
        others = [lax.rem(group.me + step, ranks) for step in (2, 6, 4, 1, 3, 5, 7)]
        fetches = [
            stores.start(r.both_low, r.act),
            stores.start(r.gate, r.gate_up_near.at[:, pl.ds(0, room)]),
            stores.start(r.up, r.gate_up_near.at[:, pl.ds(room, room)]),
        ]
        rows_fetch = stores.start(r.whole_hidden, r.rows_near)
        out_fetch = stores.start(r.out_whole, r.out_near)
        meet([{"ctx": other} for other in others] + owner.peers())
        item = Sum(Rows(r.part, ranks), *r.landings)
        part, from_sibling, *places = r.gate_up_sum
        own = Sum(Chips(part, owners), *places, r.gate_up_share)
        owned = owner_sum(
            owner,
            copies,
            stores,
            [Made(r.rows_near, r.act, r.given, owners)],
            [own],
            [from_sibling],
        )
        for fetch in fetches:
            fetch.wait()
        rows_fetch.wait()
        main = ctx_sum(group, copies, r.act, r.gate_up_near, [item], 512, True)
        weave(main, owned)
        hidden_grad = r.cotangent[...].astype(F32) + item.total(group)
        r.hidden_grad[...] = hidden_grad
        unit, inverse = norm(r.attn_raw[...])
        r.attn_term[...] = jnp.sum(hidden_grad * unit, axis=0, keepdims=True)
        r.attn_low[...] = low(norm_back(hidden_grad, unit, inverse, r.scales[2:3, :]))
        out_fetch.wait()
        value = r.attn_low[...]
        mine = rows_at(group.me, size)
        crossing = []
        for i, other in enumerate(others):
            r.mixed_out[i] = low(back_dot(value, r.out_near[rows_at(other, share), :]))
            crossing.append(
                copies.start(r.mixed_out.at[i], r.mixed_landed.at[mine], {"ctx": other})
            )
        r.mixed_landed[mine, :] = low(back_dot(value, r.out_near[rows_at(group.me, share), :]))
        finish(owned)
        arrived(crossing)
        r.mixed_grad[...] = r.mixed_landed[...]
        stores.drain()
        copies.drain()

    return launch(
        number,
        body,
        far(both_low=both_low, gate=gate, up=up, out_whole=out_whole, whole_hidden=whole_hidden)
        | near(cotangent=cotangent, attn_raw=attn_raw, scales=scales),
        near(
            hidden_grad=shape((size, width), F32),
            attn_term=shape((1, width), F32),
            attn_low=shape((size, width)),
            mixed_grad=shape((length, share)),
            gate_up_share=shape(gate_up_block),
        ),
        dict(
            act=pltpu.VMEM(both_low.shape, BF16),
            gate_up_near=pltpu.VMEM((width, both), BF16),
            out_near=pltpu.VMEM(out_whole.shape, BF16),
            part=pltpu.VMEM((length, width), BF16),
            landings=landing(size, width, True),
            rows_near=pltpu.VMEM((length, width), BF16),
            given=pltpu.VMEM((owners // 2, *gate_up_block), BF16),
            mixed_out=pltpu.VMEM((ranks - 1, size, share), BF16),
            mixed_landed=pltpu.VMEM((length, share), BF16),
            gate_up_sum=sum_scratch(*gate_up_block, owners),
        ),
        17 + 17 + ranks - 1,
        4 + 8,
    )


def attend_back(front, mixed_grad, cosine, sine, orders, gate_up_share, attn_low, number):
    ranks, owners = lax.axis_size("ctx"), lax.axis_size("fsdp")
    length, share = mixed_grad.shape
    lanes, chunk = 2 * HD, 256
    whole = (ranks * gate_up_share.shape[0], gate_up_share.shape[1])
    size, width = attn_low.shape
    out_block = (width // owners, width)

    def body(r, copies, stores):
        group, owner = Group("ctx"), Group("fsdp")
        others = [{"ctx": lax.rem(group.me + step, ranks)} for step in range(1, ranks)]
        meet(others + owner.peers())
        all_shares, stored = Rows(r.landed, ranks), Rows(r.whole, ranks)
        stream = ring_gather(group, copies, [(r.block, all_shares)], True)
        next(stream)
        stores.start(r.block, stored.block(group.me))
        part, from_sibling, *places = r.out_sum
        own = Sum(Chips(part, owners), *places, r.out_share)
        owned = owner_sum(
            owner,
            copies,
            stores,
            [Made(r.mixed_rows, r.attn_low, r.given, owners)],
            [own],
            [from_sibling],
        )
        next(owned)
        next(owned)
        r.key_turn[...] = jnp.zeros_like(r.key_turn)
        r.value_sum[...] = jnp.zeros_like(r.value_sum)

        r.grads[...] = low(dot(placing(r.query_pos), r.mixed_grad[...]))

        def advance():
            for index in next(stream, []):
                stores.start(all_shares.block(index), stored.block(index))
            next(owned, None)

        for pair in range(share // lanes):
            span = pl.ds(pair * lanes, lanes)
            key_turned = r.keys[:, span].astype(F32).T.astype(BF16)
            for start in range(0, length, chunk):
                rows = pl.ds(start, chunk)
                query, grad = r.queries[rows, span] * BF16(HD ** (-0.5)), r.grads[rows, span]
                nothing = jnp.zeros_like(query)
                outs = []
                for mask in heads_of(query):
                    query_head = jnp.where(mask, query, nothing)
                    grad_head = jnp.where(mask, grad, nothing)
                    pieces, over = soft(r.keys, span, query_head, start)
                    probs = [piece * over for _, piece in pieces]
                    prob_grads = [back_dot(r.values[at, span], grad_head) for at, _ in pieces]
                    delta = sum(
                        jnp.sum(prob * prob_grad, axis=0, keepdims=True)
                        for prob, prob_grad in zip(probs, prob_grads)
                    )
                    out = 0.0
                    for (at, _), prob, prob_grad in zip(pieces, probs, prob_grads):
                        score_low = low(prob * (prob_grad - delta))
                        r.value_sum[at, span] += dot(low(prob), grad_head)
                        r.key_turn[at, span] += dot(score_low, query_head)
                        out += dot(key_turned[:, at.start : at.start + at.size], score_low)
                    outs.append(out)
                query_rot = (pair_of(outs) * HD ** (-0.5)).T
                r.query_turn[rows, span] = query_rot * r.cosine[rows, :] + turned_back(
                    query_rot * r.sine[rows, :]
                )
                if start % (2 * chunk):
                    advance()
            key_rot = r.key_turn[:, span]
            r.key_turn[:, span] = key_rot * r.cosine[...] + turned_back(key_rot * r.sine[...])
        by_row = lax.broadcasted_iota(jnp.int32, (8, share), 0) < 4
        mine = rows_at(group.me, share)
        for i, (turn, unit) in enumerate(
            ((r.query_turn, r.query_unit), (r.key_turn, r.key_unit))
        ):
            product = turn[...] * unit[...]
            r.terms[pl.ds(i, 1), :] = jnp.sum(product, axis=0, keepdims=True)
            part = totals_by_row(
                jnp.where(by_row == (i == 0), 1.0, 0.0), product * r.scales[i : i + 1, mine]
            )
            r.sums[...] = part if i == 0 else r.sums[...] + part
        exchange = [copies.start(r.sums, r.sums_landed.at[i], to) for i, to in enumerate(others)]
        advance()
        arrived(exchange)
        totals = r.sums[...] + jnp.sum(r.sums_landed[...], axis=0)
        means = (totals * (1.0 / (ranks * share))).T
        for i, (turn, unit) in enumerate(
            ((r.query_turn, r.query_unit), (r.key_turn, r.key_unit))
        ):
            column = slice(4 * i, 4 * i + 1)
            r.placed_low[:, pl.ds(i * share, share)] = low(
                r.inverse[:, column]
                * (turn[...] * r.scales[i : i + 1, mine] - unit[...] * means[:, column])
            )
        r.placed_low[:, pl.ds(2 * share, share)] = low(r.value_sum[...])

        r.qkv_low[...] = low(dot(dealing(r.key_pos), r.placed_low[...]))
        for _ in range(10):
            advance()
        copies.drain()
        stores.drain()

    return launch(
        number,
        body,
        near(
            queries=front.queries,
            keys=front.keys,
            values=front.values,
            query_unit=front.query_unit,
            key_unit=front.key_unit,
            inverse=front.inverse,
            scales=front.scales,
            mixed_grad=mixed_grad,
            cosine=cosine,
            sine=sine,
            block=gate_up_share,
            mixed_rows=front.mixed_rows,
            attn_low=attn_low,
        )
        | near(**orders),
        near(
            qkv_low=shape((length, 3 * share)),
            terms=shape((2, share), F32),
            out_share=shape(out_block),
        )
        | far(whole=shape(whole)),
        dict(
            given=pltpu.VMEM((owners // 2, *out_block), BF16),
            grads=pltpu.VMEM((length, share), BF16),
            placed_low=pltpu.VMEM((length, 3 * share), BF16),
            query_turn=pltpu.VMEM((length, share), F32),
            key_turn=pltpu.VMEM((length, share), F32),
            value_sum=pltpu.VMEM((length, share), F32),
            sums=pltpu.VMEM((8, length), F32),
            sums_landed=pltpu.VMEM((ranks - 1, 8, length), F32),
            landed=pltpu.VMEM(whole, BF16),
            out_sum=sum_scratch(*out_block, owners),
        ),
        15 + 17 + ranks - 1,
        16,
    )


def input_back(qkv_low, qkv, hidden_grad, out_share, whole, strip_grad, number):
    ranks, owners = lax.axis_size("ctx"), lax.axis_size("fsdp")
    size, width = hidden_grad.shape
    length = qkv_low.shape[0]
    height = out_share.shape[0]
    qkv_block = (width // owners, qkv_low.shape[1])
    strip_block = (strip_grad.shape[0], width // owners)

    def body(r, copies, stores):
        group, owner = Group("ctx"), Group("fsdp")
        fetches = [
            stores.start(r.qkv_low, r.act),
            stores.start(r.qkv, r.qkv_near),
            stores.start(r.out_share, r.out_part),
            stores.start(r.whole, r.rows_near),
        ]
        meet(group.peers() + owner.peers())
        item = Sum(Rows(r.part, ranks), *r.landings)
        out_item = Sum(Strips(r.out_part, ranks), *r.out_landings)
        sums = [
            Sum(Chips(scratch[0], owners), *scratch[2:], out)
            for scratch, out in ((r.strip_sum, r.strip_share), (r.qkv_sum, r.qkv_share))
        ]
        owned = owner_sum(
            owner,
            copies,
            stores,
            [Strips(r.strip_grad, owners), Made(r.rows_near, r.act, r.given, owners)],
            sums,
            [r.strip_sum[1], r.qkv_sum[1]],
        )
        for fetch in fetches:
            fetch.wait()
        weave(ctx_sum(group, copies, r.act, r.qkv_near, [item, out_item], 512, True), owned)
        r.input_grad[...] = r.hidden_grad[...] + item.total(group)
        r.out_mine[...] = low(out_item.total(group))
        finish(owned)
        copies.drain()

    return launch(
        number,
        body,
        far(
            qkv_low=qkv_low, qkv=qkv, out_share=out_share, whole=whole, strip_grad=strip_grad
        )
        | near(hidden_grad=hidden_grad),
        near(
            input_grad=shape((size, width), F32),
            out_mine=shape((height, width // ranks)),
            qkv_share=shape(qkv_block),
            strip_share=shape(strip_block),
        ),
        dict(
            act=pltpu.VMEM(qkv_low.shape, BF16),
            qkv_near=pltpu.VMEM(qkv.shape, BF16),
            part=pltpu.VMEM((length, width), BF16),
            landings=landing(size, width, True),
            rows_near=pltpu.VMEM((length, width), BF16),
            given=pltpu.VMEM((owners // 2, *qkv_block), BF16),
            out_part=pltpu.VMEM(out_share.shape, BF16),
            out_landings=landing(height, width // ranks, True),
            qkv_sum=sum_scratch(*qkv_block, owners),
            strip_sum=sum_scratch(*strip_block, owners),
        ),
        34 + 34,
        4 + 16,
    )


def spread(parts, number):
    ranks, count = lax.axis_size("ctx"), len(parts)
    wholes = [(ranks * part.shape[0], part.shape[1]) for part in parts]
    names = [f"part_{i}" for i in range(count)]

    def body(r, copies, stores):
        group = Group("ctx")
        meet(group.peers())
        mine = [getattr(r, name) for name in names]
        stored = [Rows(getattr(r, "whole_" + name), ranks) for name in names]
        landed = [Rows(ref, ranks) for ref in r.landed]
        own = True
        for indexes in ring_gather(group, copies, list(zip(mine, landed)), True):
            for index in indexes:
                for block, all_blocks, to in zip(mine, landed, stored):
                    stores.start(block if own else all_blocks.block(index), to.block(index))
                own = False
        copies.drain()
        stores.drain()

    outs = launch(
        number,
        body,
        near(**dict(zip(names, parts))),
        far(**{"whole_" + name: shape(dims) for name, dims in zip(names, wholes)}),
        dict(landed=[pltpu.VMEM(dims, BF16) for dims in wholes]),
        15 * count,
        8 * count,
    )
    return [getattr(outs, "whole_" + name) for name in names]


def unfold_kernel(units, shares, gate, up):
    size, room = gate.shape[0], shares.shape[1] // 2
    tail = units // 128 * 128
    for i, out in enumerate((gate, up)):
        span = pl.ds(i * room, room)
        left = shares[pl.ds(0, size), span].astype(F32)
        right = pltpu.roll(shares[pl.ds(size, size), span].astype(F32), units - tail, 1)
        inside = lax.broadcasted_iota(jnp.int32, (size, 128), 1) < units - tail
        out[:, pl.ds(0, tail)] = left[:, :tail]
        out[:, pl.ds(tail, 128)] = jnp.where(inside, left[:, tail : tail + 128], right[:, :128])
        out[:, pl.ds(tail + 128, tail)] = right[:, 128 : tail + 128]


def unfold(shares, units):
    ranks = lax.axis_size("ctx")
    size = shares.shape[0] // ranks
    return pl.pallas_call(
        functools.partial(unfold_kernel, units),
        grid=(ranks // 2,),
        in_specs=[pl.BlockSpec((2 * size, shares.shape[1]), lambda i: (i, 0))],
        out_specs=[pl.BlockSpec((size, 2 * units), lambda i: (0, i))] * 2,
        out_shape=[shape((size, ranks * units), F32)] * 2,
        compiler_params=pltpu.CompilerParams(vmem_limit_bytes=ROOM),
    )(shares)


def widen_kernel(qkv, out, down, query_out, key_out, value_out, out_out, down_out):
    share = out.shape[1]
    for i, ref in enumerate((query_out, key_out, value_out)):
        ref[...] = qkv[:, pl.ds(i * share, share)].astype(F32)
    out_out[...] = out[...].astype(F32)
    down_out[...] = down[...].astype(F32)


def widen(qkv, out, down):
    ranks = lax.axis_size("ctx")
    share = out.shape[1]
    heights = [part.shape[0] // ranks for part in (qkv, qkv, qkv, out, down)]
    return pl.pallas_call(
        widen_kernel,
        grid=(ranks,),
        in_specs=[
            pl.BlockSpec((part.shape[0] // ranks, part.shape[1]), lambda i: (i, 0))
            for part in (qkv, out, down)
        ],
        out_specs=[pl.BlockSpec((height, share), lambda i: (0, i)) for height in heights],
        out_shape=[shape((height, ranks * share), F32) for height in heights],
        compiler_params=pltpu.CompilerParams(vmem_limit_bytes=ROOM),
    )(qkv, out, down)


def body(
    layer_input,
    cotangent,
    query_weight,
    key_weight,
    value_weight,
    out_weight,
    gate_weight,
    up_weight,
    down_weight,
    query_gain,
    key_gain,
    attention_gain,
    feed_gain,
    pair_table,
):
    row_count = layer_input.shape[1]
    block_len = row_count // 2
    rank = lax.axis_index("ctx")
    owner = lax.axis_index("fsdp")
    ranks = lax.axis_size("ctx")
    owners = lax.axis_size("fsdp")
    width = query_weight.shape[1]
    share = width // ranks
    strip = width // owners
    units = gate_weight.shape[1] // ranks
    room = -(-units // 256) * 256
    blocks = pair_table.reshape(-1)
    positions = (
        blocks[:, None] * block_len + jnp.arange(block_len, dtype=jnp.int32)[None, :]
    ).reshape(-1)
    orders = dict(key_pos=positions[:, None], query_pos=positions[None, :])
    cosine, sine = angles(2 * ranks * block_len)

    def cut(weight, size):
        return lax.dynamic_slice_in_dim(weight, rank * size, size, axis=1)

    def wide(weight):
        return jnp.pad(cut(weight, units), ((0, 0), (0, room - units)))

    inputs = layer_input[0]
    qkv_mine = jnp.concatenate(
        [cut(w, share) for w in (query_weight, key_weight, value_weight)], axis=1
    )
    gains_mine = jnp.pad(
        jnp.stack([query_gain, key_gain, attention_gain, feed_gain]), ((0, 28), (0, 0))
    )
    flat = lambda c, f: c * owners + f
    odd = lax.rem(owner, 2)
    routes = [
        [
            (flat(c, 2 * d + j), flat(d, 2 * c + (j ^ k)))
            for c in range(ranks)
            for d in range(ranks)
            for j in range(2)
        ]
        for k in range(2)
    ]
    axes = ("ctx", "fsdp")
    pieces = []
    for k, route in enumerate(routes):
        target = 2 * rank + (odd ^ k)
        strips = lax.dynamic_slice_in_dim(down_weight, target * strip, strip, axis=1)
        pieces.append(lax.ppermute(strips, axes, route))

    def in_order(pair):
        return jnp.where(odd == 0, pair[0], pair[1]), jnp.where(odd == 0, pair[1], pair[0])

    low_piece, high_piece = in_order(pieces)
    strips = jnp.concatenate(
        [low_piece, high_piece, jnp.zeros((room - units, strip), BF16)], axis=0
    )

    front = attend(
        inputs, qkv_mine, gains_mine, out_weight, wide(gate_weight), cosine, sine, orders, 1
    )
    fed = feed(
        front.hidden,
        front.hidden_low,
        front.gate,
        wide(up_weight),
        strips,
        cotangent[0],
        front.scales,
        2,
    )
    inner = hidden_back(
        fed.both_low,
        front.gate,
        fed.up,
        cotangent[0],
        front.attn_raw,
        front.scales,
        front.out_whole,
        fed.whole_hidden,
        3,
    )
    outer = attend_back(
        front, inner.mixed_grad, cosine, sine, orders, inner.gate_up_share, inner.attn_low, 4
    )
    down_grad = low(outer_sum(fed.product, fed.whole_down))

    def placed(term):
        return lax.dynamic_update_slice_in_dim(
            jnp.zeros((width,), F32), term, rank * share, axis=0
        )

    gain_terms = low(jnp.stack([placed(outer.terms[0]), placed(outer.terms[1]), inner.attn_term[0], fed.feed_term[0]]))
    strip_grads = jnp.concatenate([down_grad, jnp.pad(gain_terms, ((0, 28), (0, 0)))], axis=0)
    last = input_back(
        outer.qkv_low, front.qkv, inner.hidden_grad, outer.out_share, front.whole, strip_grads, 5
    )
    down_size = down_weight.shape[0]
    by_owner = [last.strip_share[j * down_size : (j + 1) * down_size] for j in range(2)]
    gains_share = last.strip_share[room:]
    by_route = in_order(by_owner)
    returned = [
        lax.ppermute(piece, axes, [(b, a) for a, b in route])
        for piece, route in zip(by_route, routes)
    ]
    down_share = jnp.concatenate(in_order(returned), axis=1)

    qkv_all, out_all, down_all, gains_all = spread(
        [last.qkv_share, last.out_mine, down_share, gains_share], 6
    )

    gate_share, up_share = unfold(outer.whole, units)
    query_share, key_share, value_share, out_share, down_share = widen(qkv_all, out_all, down_all)
    mine = jnp.sum(gains_all.reshape(ranks, -1, strip)[:, :4].astype(F32), axis=0)
    return (
        fed.result[None],
        last.input_grad[None],
        query_share,
        key_share,
        value_share,
        out_share,
        gate_share,
        up_share,
        down_share,
        mine[0],
        mine[1],
        mine[2],
        mine[3],
    )


def solution(mesh):
    weights = (P("fsdp", None),) * 7
    gains = (P("fsdp"),) * 4
    tokens = P("fsdp", "ctx", None)
    in_specs = (tokens, tokens, *weights, *gains, P())
    out_specs = (tokens, tokens, *weights, *gains)
    return jax.shard_map(body, mesh=mesh, in_specs=in_specs, out_specs=out_specs, check_vma=False)
```

```python
import functools
import types

import jax
import jax.numpy as jnp
import numpy as np
from jax import lax
from jax.experimental import pallas as pl
from jax.experimental.pallas import tpu as pltpu
from jax.sharding import PartitionSpec as P

HD = 64
EPSILON = 1e-06
THETA = 500000.0
MESH = pl.DeviceIdType.MESH
F32 = jnp.float32
BF16 = jnp.bfloat16
ROOM = 56 * 2**20
NEG = -1e30


def angles(length):
    freqs = THETA ** (-np.arange(0, HD, 2, dtype=np.float32) / np.float32(HD))
    phase = np.arange(length, dtype=np.float32)[:, None] * np.tile(freqs, 4)[None, :]
    return jnp.asarray(np.cos(phase)), jnp.asarray(np.sin(phase))


def dot(left, right):
    return jnp.dot(left, right, preferred_element_type=F32)


def outer_sum(left, right):
    return lax.dot_general(left, right, (((0,), (0,)), ((), ())), preferred_element_type=F32)


def back_dot(grad, weight):
    return lax.dot_general(grad, weight, (((1,), (1,)), ((), ())), preferred_element_type=F32)


def low(values):
    return values.astype(BF16)


class Group:
    def __init__(self, axis):
        me = lax.axis_index(axis)
        self.axis = axis
        self.size = lax.axis_size(axis)
        self.me = me
        if axis == "ctx":
            self.core, self.pair, self.place = 0, me // 4, lax.rem(me, 4)
        else:
            self.core, self.pair, self.place = lax.rem(me, 2), lax.rem(me, 4) // 2, me // 4
        self.sibling = me + 1 - 2 * self.core if axis == "fsdp" else None
        self.right, self.left, self.partner = self.at(False, 1), self.at(False, 3), self.at(True, 0)

    def at(self, other, step):
        pair = 1 - self.pair if other else self.pair
        place = lax.rem(self.place + step, 4)
        if self.axis == "ctx":
            return pair * 4 + place
        return place * 4 + pair * 2 + self.core

    def peers(self):
        near = [self.right, self.left, self.partner]
        if self.sibling is not None:
            near.append(self.sibling)
        return [{self.axis: peer} for peer in near]


def meet(peers):
    barrier = pltpu.get_barrier_semaphore()
    for peer in peers:
        pl.semaphore_signal(barrier, inc=1, device_id=peer, device_id_type=MESH)
    pl.semaphore_wait(barrier, len(peers))


class Copies:
    def __init__(self, sent, came):
        self.sent, self.came, self.count, self.all = sent, came, 0, []

    def start(self, src, dst, peer):
        copy = pltpu.make_async_remote_copy(
            src_ref=src,
            dst_ref=dst,
            send_sem=self.sent.at[self.count],
            recv_sem=self.came.at[self.count],
            device_id=peer,
            device_id_type=MESH,
        )
        self.count += 1
        self.all.append(copy)
        copy.start()
        return copy

    def drain(self):
        for copy in self.all:
            copy.wait_send()


class Once:
    def __init__(self, copy):
        self.copy, self.waited = copy, False

    def wait(self):
        if not self.waited:
            self.copy.wait()
        self.waited = True


class Stores:
    def __init__(self, sems):
        self.sems, self.count, self.all = sems, 0, []

    def start(self, src, dst):
        copy = pltpu.make_async_copy(src, dst, self.sems.at[self.count])
        self.count += 1
        copy.start()
        copy = Once(copy)
        self.all.append(copy)
        return copy

    def drain(self):
        for copy in self.all:
            copy.wait()
        self.all = []


def rows_at(index, size):
    return pl.ds(pl.multiple_of(index * size, size), size)


class Rows:
    def __init__(self, ref, blocks):
        self.ref, self.rows = ref, ref.shape[0] // blocks

    def block(self, index, low_row=0, high_row=None):
        high_row = self.rows if high_row is None else high_row
        start = pl.multiple_of(index * self.rows + low_row, 16)
        return self.ref.at[pl.ds(start, high_row - low_row)]


class Chips(Rows):
    def __init__(self, ref, owners):
        super().__init__(ref, owners // 2)

    def block(self, index, low_row=0, high_row=None):
        return super().block(lax.div(index, 2), low_row, high_row)


class Strips:
    def __init__(self, ref, blocks):
        self.ref, self.rows, self.width = ref, ref.shape[0], ref.shape[1] // blocks

    def block(self, index, low_row=0, high_row=None):
        high_row = self.rows if high_row is None else high_row
        return self.ref.at[pl.ds(low_row, high_row - low_row), rows_at(index, self.width)]


def arrived(copies):
    for copy in copies:
        copy.wait_recv()


class Cuts:
    def __init__(self, rows, edged):
        half = rows // 2
        start = rows // 8 // 16 * 16 if edged else 0
        stop = rows - rows // 4 // 16 * 16 if edged else rows
        self.all, self.first, self.second = [(0, rows)], [(0, half)], [(half, rows)]
        self.middle = [(start, stop)]
        self.middle_first, self.middle_second = [(start, half)], [(half, stop)]
        self.top = [(0, start)] if start else []
        self.bottom = [(stop, rows)] if stop < rows else []
        self.edges = self.top + self.bottom
        self.half = half


def ring_gather(group, copies, items, edged=False):
    at = group.at
    right, left, partner = ({group.axis: peer} for peer in (group.right, group.left, group.partner))

    def move(index, part, peer, own=False):
        started = []
        for mine, whole in items:
            for lo, hi in getattr(Cuts(whole.rows, edged), part):
                view = whole.block(index, lo, hi)
                started.append(copies.start(mine if own else view, view, peer))
        return started

    near_left = move(group.me, "all", right, True)
    near_right = move(group.me, "all", left, True)
    across = move(group.me, "all", partner, True)
    yield [group.me]
    arrived(near_left)
    far_left = move(group.left, "first", right)
    edges = move(group.left, "edges", partner)
    arrived(near_right)
    far_right = move(group.right, "second", left)
    edges += move(group.right, "edges", partner)
    arrived(across)
    other_left = move(group.partner, "middle", right)
    other_right = move(group.partner, "middle", left)
    yield [group.left, group.right, group.partner]
    arrived(far_left)
    last = move(at(False, 2), "top", partner)
    arrived(far_right)
    last += move(at(False, 2), "bottom", partner)
    yield [at(False, 2)]
    arrived(other_left)
    last += move(at(True, 3), "middle_first", right)
    arrived(other_right)
    last += move(at(True, 1), "middle_second", left)
    arrived(edges)
    yield [at(True, 3), at(True, 1)]
    arrived(last)
    yield [at(True, 2)]


def add(ref, others):
    value = ref[...].astype(F32)
    for other in others:
        value += other[...].astype(F32)
    ref[...] = low(value)


class Sum:
    def __init__(self, parts, far, side, cross, out=None):
        self.parts, self.far, self.side, self.cross, self.out = parts, far, side, cross, out

    def total(self, group):
        own = self.parts.block(group.me)[...].astype(F32)
        sides = self.side[0, 1].astype(F32) + self.side[1, 1].astype(F32)
        return own + sides + self.cross[0].astype(F32)


def landing(rows, columns, edged=False):
    return [
        pltpu.VMEM((2, 2, rows // 2, columns), BF16),
        pltpu.VMEM((2, 2, rows, columns), BF16),
        pltpu.VMEM((4 if edged else 1, rows, columns), BF16),
    ]


def ring_scatter(group, copies, items, prepare, edged=False):
    at = group.at
    right, left, partner = ({group.axis: peer} for peer in (group.right, group.left, group.partner))
    cuts = [Cuts(item.parts.rows, edged) for item in items]

    def window(ref, lead, lo, hi):
        return ref.at[(*lead, pl.ds(lo, hi - lo))]

    def send_edges(step):
        started = []
        for item, cut in zip(items, cuts):
            for lo, hi in cut.edges:
                view = item.parts.block(at(True, step), lo, hi)
                started.append(copies.start(view, window(item.cross, (step,), lo, hi), partner))
        return started

    def add_edges(step):
        for item, cut in zip(items, cuts):
            for lo, hi in cut.edges:
                add(item.parts.block(at(False, step), lo, hi), [window(item.cross, (step,), lo, hi)])

    def far_cut(cut, i, side):
        if side == 0:
            return (cut.middle_first if i == 0 else cut.first)[0]
        return (cut.middle_second if i == 0 else cut.second)[0]

    def far_window(item, cut, i, side):
        lo, hi = far_cut(cut, i, side)
        base = side * cut.half
        return window(item.far, (side, i), lo - base, hi - base)

    def send_far(i):
        started = ([], [])
        for item, cut in zip(items, cuts):
            for side, peer in enumerate((right, left)):
                view = item.parts.block(at(i == 0, 2), *far_cut(cut, i, side))
                started[side].append(copies.start(view, far_window(item, cut, i, side), peer))
        return started

    def send_near(i, far):
        started = []
        for side, (step, peer) in enumerate(((1, right), (3, left))):
            arrived(far[side])
            index = at(i == 0, step)
            for item, cut in zip(items, cuts):
                add(
                    item.parts.block(index, *far_cut(cut, i, side)),
                    [far_window(item, cut, i, side)],
                )
                lo, hi = (cut.middle if i == 0 else cut.all)[0]
                view = item.parts.block(index, lo, hi)
                started.append(copies.start(view, window(item.side, (side, i), lo, hi), peer))
        return started

    prepare((True, 2))
    far_other = send_far(0)
    edges = {2: send_edges(2)}
    yield
    prepare((False, 2))
    arrived(edges[2])
    add_edges(2)
    far_same = send_far(1)
    yield
    prepare((True, 1), (True, 3))
    for step in (1, 3):
        edges[step] = send_edges(step)
    yield
    near_other = send_near(0, far_other)
    yield
    prepare((True, 0))
    edges[0] = send_edges(0)
    prepare((False, 1), (False, 3))
    for step in (1, 3):
        arrived(edges[step])
        add_edges(step)
    near_same = send_near(1, far_same)
    yield
    arrived(near_other)
    across = []
    for item, cut in zip(items, cuts):
        lo, hi = cut.middle[0]
        view = item.parts.block(group.partner, lo, hi)
        add(view, [window(item.side, (0, 0), lo, hi), window(item.side, (1, 0), lo, hi)])
        across.append(copies.start(view, window(item.cross, (0,), lo, hi), partner))
    yield
    prepare((False, 0))
    yield
    arrived(near_same)
    arrived(across)
    arrived(edges[0])
    yield


def owner_gather(owner, copies, stores, items):
    sibling = {owner.axis: owner.sibling}
    passed, own = [], True
    placed = [stores.start(mine, whole.block(owner.me)) for mine, whole in items]
    for indexes in ring_gather(owner, copies, items):
        for index in indexes:
            for mine, whole in items:
                view = whole.block(index)
                passed.append(copies.start(mine if own else view, view, sibling))
        own = False
        yield
    arrived(passed)
    for copy in placed:
        copy.wait()
    yield


class Made:
    def __init__(self, left, right, given, owners):
        self.left, self.right, self.given = left, right, given
        self.width = left.shape[1] // owners

    def block(self, index):
        return low(outer_sum(self.left[:, rows_at(index, self.width)], self.right[...]))


def owner_sum(owner, copies, stores, sources, sums, from_sibling):
    sibling = {owner.axis: owner.sibling}
    turn = 1 - 2 * owner.core
    waits = {}
    for step in (2, 1, 3, 0):
        for other in (True, False):
            index, number = owner.at(other, step), len(waits)
            waits[other, step] = []
            for source, item, landed in zip(sources, sums, from_sibling):
                fetch, place = None, landed.at[number]
                if isinstance(source, Made):
                    given = source.given.at[number]
                    given[...] = source.block(index + turn)
                    give = copies.start(given, place, sibling)
                    item.parts.block(index)[...] = source.block(index)
                else:
                    fetch = stores.start(source.block(index), item.parts.block(index))
                    give = copies.start(source.block(index + turn), place, sibling)
                waits[other, step].append((fetch, give, place))

    def prepare(*places):
        for place in places:
            for (fetch, give, landed), item in zip(waits[place], sums):
                if fetch is not None:
                    fetch.wait()
                give.wait_recv()
                add(item.parts.block(owner.at(*place)), [landed])

    yield
    yield from ring_scatter(owner, copies, sums, prepare)
    for item in sums:
        item.out[...] = low(item.total(owner))
    yield


def sum_scratch(rows, columns, owners):
    return [
        pltpu.VMEM((owners // 2 * rows, columns), BF16),
        pltpu.VMEM((owners // 2, rows, columns), BF16),
        *landing(rows, columns),
    ]


FAR = pl.BlockSpec(memory_space=pl.ANY)
NEAR = pl.BlockSpec(memory_space=pltpu.VMEM)


def shape(dims, kind=BF16):
    return jax.ShapeDtypeStruct(dims, kind)


def launch(number, body, ins, outs, temps, remote, local):
    names, scratch, groups = [*ins, *outs], [], []
    for name, kind in temps.items():
        kinds = kind if isinstance(kind, list) else [kind]
        groups.append((name, len(kinds), isinstance(kind, list)))
        scratch += kinds
    dma = pltpu.SemaphoreType.DMA
    scratch += [dma((remote,)), dma((remote,)), dma((local,))]

    def kernel(*refs):
        named = dict(zip(names, refs))
        rest = list(refs[len(names) :])
        for name, count, many in groups:
            named[name] = rest[:count] if many else rest[0]
            del rest[:count]
        sent, came, near = rest
        body(types.SimpleNamespace(**named), Copies(sent, came), Stores(near))

    results = pl.pallas_call(
        kernel,
        out_shape=[out for out, _ in outs.values()],
        in_specs=[spec for _, spec in ins.values()],
        out_specs=[spec for _, spec in outs.values()],
        scratch_shapes=scratch,
        compiler_params=pltpu.CompilerParams(
            collective_id=number, has_side_effects=True, vmem_limit_bytes=ROOM
        ),
    )(*[array for array, _ in ins.values()])
    return types.SimpleNamespace(**dict(zip(outs, results)))


def near(**arrays):
    return {name: (array, NEAR) for name, array in arrays.items()}


def far(**arrays):
    return {name: (array, FAR) for name, array in arrays.items()}


def tiles(product, rows, values, weight, tile, transposed):
    size = values[0].shape[0]
    value = values[0] if len(values) == 1 else jnp.concatenate(values, axis=0)

    def step(i, carry):
        span = rows_at(i, tile)
        if transposed:
            piece = back_dot(value, weight[span, :])
        else:
            piece = dot(value, weight[:, span])
        piece = piece.astype(product.dtype)
        for k, at in enumerate(rows):
            product[at, span] = piece[k * size : (k + 1) * size]
        return carry

    lax.fori_loop(0, product.shape[1] // tile, step, 0)


def totals_by_row(select, value):
    return lax.dot_general(
        select,
        value,
        (((1,), (1,)), ((), ())),
        precision=lax.Precision.HIGHEST,
        preferred_element_type=F32,
    )


class Gathered:
    def __init__(self, group, copies, stores, block, landed, whole, use):
        self.group, self.stores, self.use = group, stores, use
        self.block, self.landed = block, Rows(landed, group.size)
        self.whole = Rows(whole, group.size)
        self.stream = ring_gather(group, copies, [(block, self.landed)], True)
        self.ready, self.fresh = [], True

    def step(self):
        self.ready += [(self.fresh, index) for index in next(self.stream)]
        self.fresh = False

    def consume(self, last=True):
        while len(self.ready) > (0 if last else 1):
            pair, self.ready = self.ready[:2], self.ready[2:]
            sources = [self.block if own else self.landed.block(index) for own, index in pair]
            for src, (_, index) in zip(sources, pair):
                self.stores.start(src, self.whole.block(index))
            self.use(sources, [rows_at(index, self.landed.rows) for _, index in pair])


def gathered_all(gathered):
    for _ in range(4):
        gathered.consume(False)
        gathered.step()
    gathered.consume()


def ctx_sum(group, copies, act, weight, items, tile, transposed):
    parts = items[0].parts

    def prepare(*places):
        rows = [rows_at(group.at(other, step), parts.rows) for other, step in places]
        tiles(parts.ref, rows, [act[at, :] for at in rows], weight, tile, transposed)

    return ring_scatter(group, copies, items, prepare, True)


def weave(main, stream):
    for step in "0001110101010101":
        next(stream if step == "1" else main)


def finish(stream):
    for _ in stream:
        pass


def norm(values):
    inverse = lax.rsqrt(jnp.mean(values * values, axis=-1, keepdims=True) + EPSILON)
    return values * inverse, inverse


def norm_back(grad, unit, inverse, gain):
    pull = grad * gain
    return inverse * (pull - unit * jnp.mean(pull * unit, axis=-1, keepdims=True))


def turn_lanes(shape):
    return lax.rem(lax.broadcasted_iota(jnp.int32, shape, 1), HD) < HD // 2


def turned(values):
    lanes = values.shape[1]
    ahead = pltpu.roll(values, lanes - HD // 2, 1)
    behind = pltpu.roll(values, HD // 2, 1)
    return jnp.where(turn_lanes(values.shape), -ahead, behind)


def turned_back(values):
    lanes = values.shape[1]
    ahead = pltpu.roll(values, lanes - HD // 2, 1)
    behind = pltpu.roll(values, HD // 2, 1)
    return jnp.where(turn_lanes(values.shape), ahead, -behind)


def heads_of(query):
    first = lax.broadcasted_iota(jnp.int32, query.shape, 1) < HD
    return first, jnp.logical_not(first)


def pair_of(outs):
    return jnp.concatenate([outs[0][:HD], outs[1][HD:]], axis=0)


def soft(keys, span, query, start):
    chunk = query.shape[0]
    own = back_dot(keys[pl.ds(start, chunk), span], query)
    behind = lax.broadcasted_iota(jnp.int32, own.shape, 0) <= lax.broadcasted_iota(
        jnp.int32, own.shape, 1
    )
    pieces = [jnp.where(behind, own, NEG)]
    if start:
        pieces.insert(0, back_dot(keys[pl.ds(0, start), span], query))
    top = jnp.max(pieces[-1], axis=0, keepdims=True)
    for piece in pieces[:-1]:
        top = jnp.maximum(top, jnp.max(piece, axis=0, keepdims=True))
    pieces = [jnp.exp(piece - top) for piece in pieces]
    total = sum(jnp.sum(piece, axis=0, keepdims=True) for piece in pieces)
    places = [pl.ds(0, start), pl.ds(start, chunk)][-len(pieces) :]
    return list(zip(places, pieces)), 1.0 / total


def placing(query_pos):
    length = query_pos.shape[1]
    row = lax.broadcasted_iota(jnp.int32, (length, length), 0)
    return low(jnp.where(row == query_pos[...], 1.0, 0.0))


def dealing(key_pos):
    length = key_pos.shape[0]
    column = lax.broadcasted_iota(jnp.int32, (length, length), 1)
    return low(jnp.where(column == key_pos[...], 1.0, 0.0))


def split(values):
    high = low(values)
    return high, low(values - high.astype(F32))


def attend(block, qkv_mine, gains_mine, out_mine, gate_mine, cosine, sine, orders, number):
    ranks, owners = lax.axis_size("ctx"), lax.axis_size("fsdp")
    (size, depth), columns = block.shape, qkv_mine.shape[1]
    length, share, chunk = ranks * size, columns // 3, 256
    lanes = 2 * HD

    def body(r, copies, stores):
        group, owner = Group("ctx"), Group("fsdp")
        others = [lax.rem(group.me + step, ranks) for step in (2, 6, 4, 1, 3, 5, 7)]
        meet([{"ctx": other} for other in others] + owner.peers())
        normed = 2 * share
        by_lane = lax.broadcasted_iota(jnp.int32, (8, normed), 1) < share
        by_row = lax.broadcasted_iota(jnp.int32, (8, normed), 0) < 4
        select = jnp.where(by_lane == by_row, 1.0, 0.0)

        def use(sources, places):
            tiles(r.proj, places, [src[...] for src in sources], r.qkv_near, columns, False)
            for rows in places:
                value = r.proj[rows, pl.ds(0, normed)]
                r.sums[:, rows] = totals_by_row(select, value * value)

        gathered = Gathered(group, copies, stores, r.block, r.landed, r.whole, use)
        gains_all = Rows(r.gains_near, owners)
        first = owner_gather(
            owner,
            copies,
            stores,
            [(r.qkv_mine, Rows(r.qkv_near, owners)), (r.gains_mine, gains_all)],
        )
        second = owner_gather(owner, copies, stores, [(r.out_mine, Rows(r.out_near, owners))])
        third = owner_gather(owner, copies, stores, [(r.gate_mine, Rows(r.gate_near, owners))])

        next(first)
        gathered.step()
        next(first)
        next(first)
        next(first)
        next(second)
        gathered.step()
        finish(first)
        gathered.step()
        stores.drain()
        stores.start(r.qkv_near, r.qkv)
        gathered.consume(False)
        next(second)
        gathered.step()
        gathered.consume(False)
        gathered.step()
        gathered.consume()
        exchange = [
            copies.start(r.sums, r.sums_landed.at[i], {"ctx": other})
            for i, other in enumerate(others)
        ]
        next(second)
        for i in range(owners):
            rows = r.gains_near[pl.ds(i * gains_all.rows, 16), :].astype(F32)
            r.scales[:, pl.ds(i * rows.shape[1], rows.shape[1])] = rows[:8]
        next(second)
        next(third)
        arrived(exchange)
        totals = r.sums[...] + jnp.sum(r.sums_landed[...], axis=0)
        r.inverse_dealt[...] = lax.rsqrt(totals * (1.0 / (ranks * share)) + EPSILON).T
        mine = rows_at(group.me, share)

        wide = r.stack.shape[1] - share
        for k in range(2):
            span = pl.ds(k * share, share)
            unit = r.proj[:, span] * r.inverse_dealt[:, 4 * k : 4 * k + 1]
            for half, part in enumerate(split(unit)):
                r.stack[:, pl.ds((2 * k + half) * share, share)] = part
        r.stack[:, pl.ds(wide, share)] = low(r.proj[:, pl.ds(2 * share, share)])
        order = placing(r.query_pos)
        high, rest = split(r.inverse_dealt[...])
        r.inverse[...] = dot(order, high) + dot(order, rest)
        for k, (unit, out) in enumerate(((r.query_unit, r.queries), (r.key_unit, r.keys))):
            both = dot(order, r.stack[:, pl.ds(2 * k * share, 2 * share)])
            unit[...] = both[:, :share] + both[:, share:]
            scaled = unit[...] * r.scales[k : k + 1, mine]
            for pair in range(share // lanes):
                part = scaled[:, pair * lanes : (pair + 1) * lanes]
                out[:, pl.ds(pair * lanes, lanes)] = low(
                    part * r.cosine[...] + turned(part) * r.sine[...]
                )
        r.values[...] = low(dot(order, r.stack[:, pl.ds(wide, share)]))
        r.deal[...] = dealing(r.key_pos)
        crossing = []
        for pair in range(share // lanes):
            span = pl.ds(pair * lanes, lanes)
            value_turned = r.values[:, span].astype(F32).T.astype(BF16)
            for start in range(0, length, chunk):
                rows = pl.ds(start, chunk)
                query = r.queries[rows, span] * BF16(HD ** (-0.5))
                nothing = jnp.zeros_like(query)
                outs = []
                for mask in heads_of(query):
                    pieces, over = soft(r.keys, span, jnp.where(mask, query, nothing), start)
                    out = sum(
                        dot(value_turned[:, at.start : at.start + at.size], low(piece))
                        for at, piece in pieces
                    )
                    outs.append(out * over)
                r.mixed[rows, :] = low(pair_of(outs).T)
                if start == length // 2:
                    next(second if pair == 0 else third)

            r.mixed_dealt[:, span] = low(dot(r.deal[...], r.mixed[...]))
            at = pl.ds(pl.multiple_of(group.me * share + pair * lanes, lanes), lanes)
            for other in others:
                src = r.mixed_dealt.at[rows_at(other, size), span]
                crossing.append(copies.start(src, r.mixed_landed.at[:, at], {"ctx": other}))
            r.mixed_landed[:, at] = r.mixed_dealt[rows_at(group.me, size), span]
            next(third)
        finish(second)
        arrived(crossing)
        stores.drain()
        stores.start(r.out_near, r.out_whole)
        r.mixed_rows[...] = r.mixed_landed[...]
        tiles(r.attn_raw, [pl.ds(0, size)], [r.mixed_landed[...]], r.out_near, 512, False)
        unit, _ = norm(r.attn_raw[...])
        hidden = r.block[...].astype(F32) + unit * r.scales[2:3, :]
        r.hidden[...] = hidden
        r.hidden_low[...] = low(hidden)
        finish(third)
        stores.start(r.gate_near, r.gate)
        stores.drain()
        copies.drain()

    return launch(
        number,
        body,
        near(
            block=block,
            qkv_mine=qkv_mine,
            gains_mine=gains_mine,
            out_mine=out_mine,
            gate_mine=gate_mine,
            cosine=cosine,
            sine=sine,
        )
        | near(**orders),
        far(
            whole=shape((length, depth)),
            qkv=shape((depth, columns)),
            out_whole=shape((depth, depth)),
            gate=shape((depth, gate_mine.shape[1])),
        )
        | near(
            scales=shape((8, depth), F32),
            inverse=shape((length, 8), F32),
            query_unit=shape((length, share), F32),
            key_unit=shape((length, share), F32),
            queries=shape((length, share)),
            keys=shape((length, share)),
            values=shape((length, share)),
            mixed_rows=shape((size, depth)),
            attn_raw=shape((size, depth), F32),
            hidden=shape((size, depth), F32),
            hidden_low=shape((size, depth)),
        ),
        dict(
            landed=pltpu.VMEM((length, depth), BF16),
            qkv_near=pltpu.VMEM((depth, columns), BF16),
            gains_near=pltpu.VMEM((owners * gains_mine.shape[0], gains_mine.shape[1]), BF16),
            out_near=pltpu.VMEM((depth, depth), BF16),
            gate_near=pltpu.VMEM((depth, gate_mine.shape[1]), BF16),
            proj=pltpu.VMEM((length, columns), F32),
            sums=pltpu.VMEM((8, length), F32),
            sums_landed=pltpu.VMEM((ranks - 1, 8, length), F32),
            inverse_dealt=pltpu.VMEM((length, 8), F32),
            stack=pltpu.VMEM((length, 5 * share), BF16),
            deal=pltpu.VMEM((length, length), BF16),
            mixed=pltpu.VMEM((length, lanes), BF16),
            mixed_dealt=pltpu.VMEM((length, share), BF16),
            mixed_landed=pltpu.VMEM((size, depth), BF16),
        ),
        15 + 34 + 17 + 17 + 3 * (ranks - 1),
        24,
    )


def feed(hidden, hidden_low, gate, up_mine, down_mine, cotangent, scales, number):
    ranks, owners = lax.axis_size("ctx"), lax.axis_size("fsdp")
    size, width = hidden.shape
    length, room = ranks * size, gate.shape[1]
    both = 2 * room

    def body(r, copies, stores):
        group, owner = Group("ctx"), Group("fsdp")
        gate_fetch = stores.start(r.gate, r.gate_near)
        meet(group.peers() + owner.peers())
        first, second = pl.ds(0, room), pl.ds(room, room)

        def forward(sources, places):
            values = [src[...] for src in sources]
            tiles(r.pre.at[:, first], places, values, r.gate_near, room, False)
            tiles(r.pre.at[:, second], places, values, r.up_near, room, False)
            for rows in places:
                gate, up = r.pre[rows, first], r.pre[rows, second]
                r.product[rows, :] = low(gate * jax.nn.sigmoid(gate) * up)

        gathered = Gathered(group, copies, stores, r.hidden_low, r.landed, r.whole_hidden, forward)
        up = owner_gather(owner, copies, stores, [(r.up_mine, Rows(r.up_near, owners))])
        down = owner_gather(
            owner, copies, stores, [(r.down_mine, Strips(r.down_near, owners))]
        )
        next(up)
        gathered.step()
        next(up)
        next(up)
        gathered.step()
        next(up)
        next(down)
        gathered.step()
        finish(up)
        gate_fetch.wait()
        gathered.step()
        next(down)
        gathered.consume(False)
        next(down)
        gathered.step()
        next(down)
        gathered.consume()
        finish(down)
        stores.drain()
        stores.start(r.up_near, r.up)
        stores.start(r.down_near, r.down_rows)
        item = Sum(Rows(r.part, ranks), *r.landings)
        finish(ctx_sum(group, copies, r.product, r.down_near, [item], 512, False))
        unit, inverse = norm(item.total(group))
        gain = r.scales[3:4, :]
        r.result[...] = low(r.hidden[...] + unit * gain)
        upstream = r.cotangent[...].astype(F32)
        r.feed_term[...] = jnp.sum(upstream * unit, axis=0, keepdims=True)
        r.down_low[...] = low(norm_back(upstream, unit, inverse, gain))

        def backward(sources, places):
            values = [src[...] for src in sources]
            tiles(r.product_grad, places, values, r.down_near, room, True)
            for rows in places:
                gate, up = r.pre[rows, first], r.pre[rows, second]
                grad, sigmoid = r.product_grad[rows, :], jax.nn.sigmoid(gate)
                r.both_low[rows, first] = low(
                    grad * up * sigmoid * (1.0 + gate * (1.0 - sigmoid))
                )
                r.both_low[rows, second] = low(grad * gate * sigmoid)

        gathered = Gathered(group, copies, stores, r.down_low, r.landed_down, r.whole_down, backward)
        gathered.step()
        gathered_all(gathered)
        stores.drain()
        copies.drain()

    return launch(
        number,
        body,
        far(gate=gate)
        | near(
            hidden=hidden,
            hidden_low=hidden_low,
            up_mine=up_mine,
            down_mine=down_mine,
            cotangent=cotangent,
            scales=scales,
        ),
        far(
            whole_hidden=shape((length, width)),
            whole_down=shape((length, width)),
            up=shape((width, room)),
            down_rows=shape((room, width)),
        )
        | near(
            result=shape((size, width)),
            feed_term=shape((1, width), F32),
            product=shape((length, room)),
            both_low=shape((length, both)),
        ),
        dict(
            gate_near=pltpu.VMEM((width, room), BF16),
            up_near=pltpu.VMEM((width, room), BF16),
            down_near=pltpu.VMEM((room, width), BF16),
            landed=pltpu.VMEM((length, width), BF16),
            pre=pltpu.VMEM((length, both), F32),
            part=pltpu.VMEM((length, width), BF16),
            landings=landing(size, width, True),
            landed_down=pltpu.VMEM((length, width), BF16),
            down_low=pltpu.VMEM((size, width), BF16),
            product_grad=pltpu.VMEM((length, room), F32),
        ),
        15 + 15 + 17 + 34,
        24,
    )


def hidden_back(both_low, gate, up, cotangent, attn_raw, scales, out_whole, whole_hidden, number):
    ranks, owners = lax.axis_size("ctx"), lax.axis_size("fsdp")
    size, width = attn_raw.shape
    length, both = both_low.shape
    room, share = both // 2, width // ranks
    gate_up_block = (width // owners, both)

    def body(r, copies, stores):
        group, owner = Group("ctx"), Group("fsdp")
        others = [lax.rem(group.me + step, ranks) for step in (2, 6, 4, 1, 3, 5, 7)]
        fetches = [
            stores.start(r.both_low, r.act),
            stores.start(r.gate, r.gate_up_near.at[:, pl.ds(0, room)]),
            stores.start(r.up, r.gate_up_near.at[:, pl.ds(room, room)]),
        ]
        rows_fetch = stores.start(r.whole_hidden, r.rows_near)
        out_fetch = stores.start(r.out_whole, r.out_near)
        meet([{"ctx": other} for other in others] + owner.peers())
        item = Sum(Rows(r.part, ranks), *r.landings)
        part, from_sibling, *places = r.gate_up_sum
        own = Sum(Chips(part, owners), *places, r.gate_up_share)
        owned = owner_sum(
            owner,
            copies,
            stores,
            [Made(r.rows_near, r.act, r.given, owners)],
            [own],
            [from_sibling],
        )
        for fetch in fetches:
            fetch.wait()
        rows_fetch.wait()
        main = ctx_sum(group, copies, r.act, r.gate_up_near, [item], 512, True)
        weave(main, owned)
        hidden_grad = r.cotangent[...].astype(F32) + item.total(group)
        r.hidden_grad[...] = hidden_grad
        unit, inverse = norm(r.attn_raw[...])
        r.attn_term[...] = jnp.sum(hidden_grad * unit, axis=0, keepdims=True)
        r.attn_low[...] = low(norm_back(hidden_grad, unit, inverse, r.scales[2:3, :]))
        out_fetch.wait()
        value = r.attn_low[...]
        mine = rows_at(group.me, size)
        crossing = []
        for i, other in enumerate(others):
            r.mixed_out[i] = low(back_dot(value, r.out_near[rows_at(other, share), :]))
            crossing.append(
                copies.start(r.mixed_out.at[i], r.mixed_landed.at[mine], {"ctx": other})
            )
        r.mixed_landed[mine, :] = low(back_dot(value, r.out_near[rows_at(group.me, share), :]))
        finish(owned)
        arrived(crossing)
        r.mixed_grad[...] = r.mixed_landed[...]
        stores.drain()
        copies.drain()

    return launch(
        number,
        body,
        far(both_low=both_low, gate=gate, up=up, out_whole=out_whole, whole_hidden=whole_hidden)
        | near(cotangent=cotangent, attn_raw=attn_raw, scales=scales),
        near(
            hidden_grad=shape((size, width), F32),
            attn_term=shape((1, width), F32),
            attn_low=shape((size, width)),
            mixed_grad=shape((length, share)),
            gate_up_share=shape(gate_up_block),
        ),
        dict(
            act=pltpu.VMEM(both_low.shape, BF16),
            gate_up_near=pltpu.VMEM((width, both), BF16),
            out_near=pltpu.VMEM(out_whole.shape, BF16),
            part=pltpu.VMEM((length, width), BF16),
            landings=landing(size, width, True),
            rows_near=pltpu.VMEM((length, width), BF16),
            given=pltpu.VMEM((owners // 2, *gate_up_block), BF16),
            mixed_out=pltpu.VMEM((ranks - 1, size, share), BF16),
            mixed_landed=pltpu.VMEM((length, share), BF16),
            gate_up_sum=sum_scratch(*gate_up_block, owners),
        ),
        17 + 17 + ranks - 1,
        4 + 8,
    )


def attend_back(front, mixed_grad, cosine, sine, orders, gate_up_share, attn_low, number):
    ranks, owners = lax.axis_size("ctx"), lax.axis_size("fsdp")
    length, share = mixed_grad.shape
    lanes, chunk = 2 * HD, 256
    whole = (ranks * gate_up_share.shape[0], gate_up_share.shape[1])
    size, width = attn_low.shape
    out_block = (width // owners, width)

    def body(r, copies, stores):
        group, owner = Group("ctx"), Group("fsdp")
        others = [{"ctx": lax.rem(group.me + step, ranks)} for step in range(1, ranks)]
        meet(others + owner.peers())
        all_shares, stored = Rows(r.landed, ranks), Rows(r.whole, ranks)
        stream = ring_gather(group, copies, [(r.block, all_shares)], True)
        next(stream)
        stores.start(r.block, stored.block(group.me))
        part, from_sibling, *places = r.out_sum
        own = Sum(Chips(part, owners), *places, r.out_share)
        owned = owner_sum(
            owner,
            copies,
            stores,
            [Made(r.mixed_rows, r.attn_low, r.given, owners)],
            [own],
            [from_sibling],
        )
        next(owned)
        next(owned)
        r.key_turn[...] = jnp.zeros_like(r.key_turn)
        r.value_sum[...] = jnp.zeros_like(r.value_sum)

        r.grads[...] = low(dot(placing(r.query_pos), r.mixed_grad[...]))

        def advance():
            for index in next(stream, []):
                stores.start(all_shares.block(index), stored.block(index))
            next(owned, None)

        for pair in range(share // lanes):
            span = pl.ds(pair * lanes, lanes)
            key_turned = r.keys[:, span].astype(F32).T.astype(BF16)
            for start in range(0, length, chunk):
                rows = pl.ds(start, chunk)
                query, grad = r.queries[rows, span] * BF16(HD ** (-0.5)), r.grads[rows, span]
                nothing = jnp.zeros_like(query)
                outs = []
                for mask in heads_of(query):
                    query_head = jnp.where(mask, query, nothing)
                    grad_head = jnp.where(mask, grad, nothing)
                    pieces, over = soft(r.keys, span, query_head, start)
                    probs = [piece * over for _, piece in pieces]
                    prob_grads = [back_dot(r.values[at, span], grad_head) for at, _ in pieces]
                    delta = sum(
                        jnp.sum(prob * prob_grad, axis=0, keepdims=True)
                        for prob, prob_grad in zip(probs, prob_grads)
                    )
                    out = 0.0
                    for (at, _), prob, prob_grad in zip(pieces, probs, prob_grads):
                        score_low = low(prob * (prob_grad - delta))
                        r.value_sum[at, span] += dot(low(prob), grad_head)
                        r.key_turn[at, span] += dot(score_low, query_head)
                        out += dot(key_turned[:, at.start : at.start + at.size], score_low)
                    outs.append(out)
                query_rot = (pair_of(outs) * HD ** (-0.5)).T
                r.query_turn[rows, span] = query_rot * r.cosine[rows, :] + turned_back(
                    query_rot * r.sine[rows, :]
                )
                if start % (2 * chunk):
                    advance()
            key_rot = r.key_turn[:, span]
            r.key_turn[:, span] = key_rot * r.cosine[...] + turned_back(key_rot * r.sine[...])
        by_row = lax.broadcasted_iota(jnp.int32, (8, share), 0) < 4
        mine = rows_at(group.me, share)
        for i, (turn, unit) in enumerate(
            ((r.query_turn, r.query_unit), (r.key_turn, r.key_unit))
        ):
            product = turn[...] * unit[...]
            r.terms[pl.ds(i, 1), :] = jnp.sum(product, axis=0, keepdims=True)
            part = totals_by_row(
                jnp.where(by_row == (i == 0), 1.0, 0.0), product * r.scales[i : i + 1, mine]
            )
            r.sums[...] = part if i == 0 else r.sums[...] + part
        exchange = [copies.start(r.sums, r.sums_landed.at[i], to) for i, to in enumerate(others)]
        advance()
        arrived(exchange)
        totals = r.sums[...] + jnp.sum(r.sums_landed[...], axis=0)
        means = (totals * (1.0 / (ranks * share))).T
        for i, (turn, unit) in enumerate(
            ((r.query_turn, r.query_unit), (r.key_turn, r.key_unit))
        ):
            column = slice(4 * i, 4 * i + 1)
            r.placed_low[:, pl.ds(i * share, share)] = low(
                r.inverse[:, column]
                * (turn[...] * r.scales[i : i + 1, mine] - unit[...] * means[:, column])
            )
        r.placed_low[:, pl.ds(2 * share, share)] = low(r.value_sum[...])

        r.qkv_low[...] = low(dot(dealing(r.key_pos), r.placed_low[...]))
        for _ in range(10):
            advance()
        copies.drain()
        stores.drain()

    return launch(
        number,
        body,
        near(
            queries=front.queries,
            keys=front.keys,
            values=front.values,
            query_unit=front.query_unit,
            key_unit=front.key_unit,
            inverse=front.inverse,
            scales=front.scales,
            mixed_grad=mixed_grad,
            cosine=cosine,
            sine=sine,
            block=gate_up_share,
            mixed_rows=front.mixed_rows,
            attn_low=attn_low,
        )
        | near(**orders),
        near(
            qkv_low=shape((length, 3 * share)),
            terms=shape((2, share), F32),
            out_share=shape(out_block),
        )
        | far(whole=shape(whole)),
        dict(
            given=pltpu.VMEM((owners // 2, *out_block), BF16),
            grads=pltpu.VMEM((length, share), BF16),
            placed_low=pltpu.VMEM((length, 3 * share), BF16),
            query_turn=pltpu.VMEM((length, share), F32),
            key_turn=pltpu.VMEM((length, share), F32),
            value_sum=pltpu.VMEM((length, share), F32),
            sums=pltpu.VMEM((8, length), F32),
            sums_landed=pltpu.VMEM((ranks - 1, 8, length), F32),
            landed=pltpu.VMEM(whole, BF16),
            out_sum=sum_scratch(*out_block, owners),
        ),
        15 + 17 + ranks - 1,
        16,
    )


def input_back(qkv_low, qkv, hidden_grad, out_share, whole, strip_grad, number):
    ranks, owners = lax.axis_size("ctx"), lax.axis_size("fsdp")
    size, width = hidden_grad.shape
    length = qkv_low.shape[0]
    height = out_share.shape[0]
    qkv_block = (width // owners, qkv_low.shape[1])
    strip_block = (strip_grad.shape[0], width // owners)

    def body(r, copies, stores):
        group, owner = Group("ctx"), Group("fsdp")
        fetches = [
            stores.start(r.qkv_low, r.act),
            stores.start(r.qkv, r.qkv_near),
            stores.start(r.out_share, r.out_part),
            stores.start(r.whole, r.rows_near),
        ]
        meet(group.peers() + owner.peers())
        item = Sum(Rows(r.part, ranks), *r.landings)
        out_item = Sum(Strips(r.out_part, ranks), *r.out_landings)
        sums = [
            Sum(Chips(scratch[0], owners), *scratch[2:], out)
            for scratch, out in ((r.strip_sum, r.strip_share), (r.qkv_sum, r.qkv_share))
        ]
        owned = owner_sum(
            owner,
            copies,
            stores,
            [Strips(r.strip_grad, owners), Made(r.rows_near, r.act, r.given, owners)],
            sums,
            [r.strip_sum[1], r.qkv_sum[1]],
        )
        for fetch in fetches:
            fetch.wait()
        weave(ctx_sum(group, copies, r.act, r.qkv_near, [item, out_item], 512, True), owned)
        r.input_grad[...] = r.hidden_grad[...] + item.total(group)
        r.out_mine[...] = low(out_item.total(group))
        finish(owned)
        copies.drain()

    return launch(
        number,
        body,
        far(
            qkv_low=qkv_low, qkv=qkv, out_share=out_share, whole=whole, strip_grad=strip_grad
        )
        | near(hidden_grad=hidden_grad),
        near(
            input_grad=shape((size, width), F32),
            out_mine=shape((height, width // ranks)),
            qkv_share=shape(qkv_block),
            strip_share=shape(strip_block),
        ),
        dict(
            act=pltpu.VMEM(qkv_low.shape, BF16),
            qkv_near=pltpu.VMEM(qkv.shape, BF16),
            part=pltpu.VMEM((length, width), BF16),
            landings=landing(size, width, True),
            rows_near=pltpu.VMEM((length, width), BF16),
            given=pltpu.VMEM((owners // 2, *qkv_block), BF16),
            out_part=pltpu.VMEM(out_share.shape, BF16),
            out_landings=landing(height, width // ranks, True),
            qkv_sum=sum_scratch(*qkv_block, owners),
            strip_sum=sum_scratch(*strip_block, owners),
        ),
        34 + 34,
        4 + 16,
    )


def spread(parts, number):
    ranks, count = lax.axis_size("ctx"), len(parts)
    wholes = [(ranks * part.shape[0], part.shape[1]) for part in parts]
    names = [f"part_{i}" for i in range(count)]

    def body(r, copies, stores):
        group = Group("ctx")
        meet(group.peers())
        mine = [getattr(r, name) for name in names]
        stored = [Rows(getattr(r, "whole_" + name), ranks) for name in names]
        landed = [Rows(ref, ranks) for ref in r.landed]
        own = True
        for indexes in ring_gather(group, copies, list(zip(mine, landed)), True):
            for index in indexes:
                for block, all_blocks, to in zip(mine, landed, stored):
                    stores.start(block if own else all_blocks.block(index), to.block(index))
                own = False
        copies.drain()
        stores.drain()

    outs = launch(
        number,
        body,
        near(**dict(zip(names, parts))),
        far(**{"whole_" + name: shape(dims) for name, dims in zip(names, wholes)}),
        dict(landed=[pltpu.VMEM(dims, BF16) for dims in wholes]),
        15 * count,
        8 * count,
    )
    return [getattr(outs, "whole_" + name) for name in names]


def unfold_kernel(units, shares, gate, up):
    size, room = gate.shape[0], shares.shape[1] // 2
    tail = units // 128 * 128
    for i, out in enumerate((gate, up)):
        span = pl.ds(i * room, room)
        left = shares[pl.ds(0, size), span].astype(F32)
        right = pltpu.roll(shares[pl.ds(size, size), span].astype(F32), units - tail, 1)
        inside = lax.broadcasted_iota(jnp.int32, (size, 128), 1) < units - tail
        out[:, pl.ds(0, tail)] = left[:, :tail]
        out[:, pl.ds(tail, 128)] = jnp.where(inside, left[:, tail : tail + 128], right[:, :128])
        out[:, pl.ds(tail + 128, tail)] = right[:, 128 : tail + 128]


def unfold(shares, units):
    ranks = lax.axis_size("ctx")
    size = shares.shape[0] // ranks
    return pl.pallas_call(
        functools.partial(unfold_kernel, units),
        grid=(ranks // 2,),
        in_specs=[pl.BlockSpec((2 * size, shares.shape[1]), lambda i: (i, 0))],
        out_specs=[pl.BlockSpec((size, 2 * units), lambda i: (0, i))] * 2,
        out_shape=[shape((size, ranks * units), F32)] * 2,
        compiler_params=pltpu.CompilerParams(vmem_limit_bytes=ROOM),
    )(shares)


def widen_kernel(qkv, out, down, query_out, key_out, value_out, out_out, down_out):
    share = out.shape[1]
    for half in range(2):
        at = pl.ds(half * share, share)
        rows = pl.ds(half * query_out.shape[0], query_out.shape[0])
        for i, ref in enumerate((query_out, key_out, value_out)):
            ref[:, at] = qkv[rows, pl.ds(i * share, share)].astype(F32)
        out_out[:, at] = out[rows, :].astype(F32)
        size = down_out.shape[0]
        down_out[:, at] = down[pl.ds(half * size, size), :].astype(F32)


def widen(qkv, out, down):
    ranks = lax.axis_size("ctx")
    share = out.shape[1]
    heights = [part.shape[0] // ranks for part in (qkv, qkv, qkv, out, down)]
    return pl.pallas_call(
        widen_kernel,
        grid=(ranks // 2,),
        in_specs=[
            pl.BlockSpec((part.shape[0] // ranks * 2, part.shape[1]), lambda i: (i, 0))
            for part in (qkv, out, down)
        ],
        out_specs=[pl.BlockSpec((height, 2 * share), lambda i: (0, i)) for height in heights],
        out_shape=[shape((height, ranks * share), F32) for height in heights],
        compiler_params=pltpu.CompilerParams(vmem_limit_bytes=ROOM),
    )(qkv, out, down)


def body(
    layer_input,
    cotangent,
    query_weight,
    key_weight,
    value_weight,
    out_weight,
    gate_weight,
    up_weight,
    down_weight,
    query_gain,
    key_gain,
    attention_gain,
    feed_gain,
    pair_table,
):
    row_count = layer_input.shape[1]
    block_len = row_count // 2
    rank = lax.axis_index("ctx")
    owner = lax.axis_index("fsdp")
    ranks = lax.axis_size("ctx")
    owners = lax.axis_size("fsdp")
    width = query_weight.shape[1]
    share = width // ranks
    strip = width // owners
    units = gate_weight.shape[1] // ranks
    room = -(-units // 256) * 256
    blocks = pair_table.reshape(-1)
    positions = (
        blocks[:, None] * block_len + jnp.arange(block_len, dtype=jnp.int32)[None, :]
    ).reshape(-1)
    orders = dict(key_pos=positions[:, None], query_pos=positions[None, :])
    cosine, sine = angles(2 * ranks * block_len)

    def cut(weight, size):
        return lax.dynamic_slice_in_dim(weight, rank * size, size, axis=1)

    def wide(weight):
        return jnp.pad(cut(weight, units), ((0, 0), (0, room - units)))

    inputs = layer_input[0]
    qkv_mine = jnp.concatenate(
        [cut(w, share) for w in (query_weight, key_weight, value_weight)], axis=1
    )
    gains_mine = jnp.pad(
        jnp.stack([query_gain, key_gain, attention_gain, feed_gain]), ((0, 28), (0, 0))
    )
    flat = lambda c, f: c * owners + f
    odd = lax.rem(owner, 2)
    routes = [
        [
            (flat(c, 2 * d + j), flat(d, 2 * c + (j ^ k)))
            for c in range(ranks)
            for d in range(ranks)
            for j in range(2)
        ]
        for k in range(2)
    ]
    axes = ("ctx", "fsdp")
    pieces = []
    for k, route in enumerate(routes):
        target = 2 * rank + (odd ^ k)
        strips = lax.dynamic_slice_in_dim(down_weight, target * strip, strip, axis=1)
        pieces.append(lax.ppermute(strips, axes, route))

    def in_order(pair):
        return jnp.where(odd == 0, pair[0], pair[1]), jnp.where(odd == 0, pair[1], pair[0])

    low_piece, high_piece = in_order(pieces)
    strips = jnp.concatenate(
        [low_piece, high_piece, jnp.zeros((room - units, strip), BF16)], axis=0
    )

    front = attend(
        inputs, qkv_mine, gains_mine, out_weight, wide(gate_weight), cosine, sine, orders, 1
    )
    fed = feed(
        front.hidden,
        front.hidden_low,
        front.gate,
        wide(up_weight),
        strips,
        cotangent[0],
        front.scales,
        2,
    )
    inner = hidden_back(
        fed.both_low,
        front.gate,
        fed.up,
        cotangent[0],
        front.attn_raw,
        front.scales,
        front.out_whole,
        fed.whole_hidden,
        3,
    )
    outer = attend_back(
        front, inner.mixed_grad, cosine, sine, orders, inner.gate_up_share, inner.attn_low, 4
    )

    def placed(term):
        return lax.dynamic_update_slice_in_dim(
            jnp.zeros((width,), F32), term, rank * share, axis=0
        )

    gain_terms = jnp.stack(
        [placed(outer.terms[0]), placed(outer.terms[1]), inner.attn_term[0], fed.feed_term[0]]
    )
    strip_grads = low(
        outer_sum(fed.product, fed.whole_down)
        + jnp.pad(gain_terms, ((units, room - units - gain_terms.shape[0]), (0, 0)))
    )
    last = input_back(
        outer.qkv_low, front.qkv, inner.hidden_grad, outer.out_share, front.whole, strip_grads, 5
    )
    down_size = down_weight.shape[0]
    by_owner = [last.strip_share[j * down_size : (j + 1) * down_size] for j in range(2)]
    gains_share = last.strip_share[units : units + 32]
    by_route = in_order(by_owner)
    returned = [
        lax.ppermute(piece, axes, [(b, a) for a, b in route])
        for piece, route in zip(by_route, routes)
    ]
    down_share = jnp.concatenate(in_order(returned), axis=1)

    qkv_all, out_all, down_all, gains_all = spread(
        [last.qkv_share, last.out_mine, down_share, gains_share], 6
    )

    gate_share, up_share = unfold(outer.whole, units)
    query_share, key_share, value_share, out_share, down_share = widen(qkv_all, out_all, down_all)
    mine = jnp.sum(gains_all.reshape(ranks, -1, strip)[:, :4].astype(F32), axis=0)
    return (
        fed.result[None],
        last.input_grad[None],
        query_share,
        key_share,
        value_share,
        out_share,
        gate_share,
        up_share,
        down_share,
        mine[0],
        mine[1],
        mine[2],
        mine[3],
    )


def solution(mesh):
    weights = (P("fsdp", None),) * 7
    gains = (P("fsdp"),) * 4
    tokens = P("fsdp", "ctx", None)
    in_specs = (tokens, tokens, *weights, *gains, P())
    out_specs = (tokens, tokens, *weights, *gains)
    return jax.shard_map(body, mesh=mesh, in_specs=in_specs, out_specs=out_specs, check_vma=False)
```
